256 devices in a mesh: section: 16 (over z_lo, y, core), expert: 16 (over x, z_hi).
Axes of the slice: x: 4, y: 4, z: 8 (z_hi: 4, z_lo: 2; z = z_hi * 2 + z_lo), core: 2. Of those that a mesh axis runs over, the one named last changes fastest.
Arguments:
- hidden: bfloat16 [2048, 2048], P(('section', 'expert')), may hold values from -6 to 6
- routes: int32 [2048, 2], P(('section', 'expert')), may hold values from 0 to 15, all different within a row; in each aligned block of 8 rows (0 to 7, 8 to 15, ...) at most 2 rows name the same one
- gates: float32 [2048, 2], P(('section', 'expert')), may hold values from 0.2 to 1
- targets: int32 [2048], replicated, may hold values from 0 to 163839
- target_lengths: int32 [16], replicated, may hold values from 32 to 128
- moe_gain: float32 [2048], replicated, may hold values from 0.5 to 1.5
- fc_in: bfloat16 [16, 2048, 8192], P('expert', None, 'section'), may hold values from -0.125 to 0.125
- fc_out: bfloat16 [16, 8192, 2048], P('expert', 'section'), may hold values from -0.0625 to 0.0625
- final_gain: float32 [2048], replicated, may hold values from 0.5 to 1.5
- head_weight: bfloat16 [2048, 163840], P(None, ('section', 'expert')), may hold values from -6 to 6
Outputs:
- log_probs: bfloat16 [2048, 163840], P(None, ('section', 'expert'))
- head_logits: bfloat16 [2048, 163840], P(None, ('section', 'expert'))
- token_loss: float32 [2048], replicated
The draws below stay inside these ranges and needn't reach their ends.
Inputs may be any that keep to these rules, and one draw needn't show every extreme that they name: `routes`: within each aligned block of 8 rows (the rows of one device) no expert is named more than 2 times, and the two experts of a row differ.
All inputs are finite; a program needn't handle non-finite values.
Results may differ from the reference program's by a relative error of at most 0.019.
Values may be sent and summed in bfloat16 or wider, within the bound.
A program may use at most 128 MiB of HBM per device.

```python
import math
import jax
import jax.numpy as jnp
import numpy as np
from jax import lax

D = 2048
FF = 8192
TGT = 128
SENTS = 16
TOKENS = 2048
ROWS = 8
EXPERTS = 16
CAP = 2
VOCAB = 163840
N_SECTION = 16


def draw_target_lengths(key, part):
    key = jax.random.fold_in(key, 13)
    first_key, second_key = jax.random.split(key)
    values = jax.random.randint(first_key, (SENTS,), TGT // 4, TGT + 1)
    ordering = jax.random.permutation(second_key, SENTS)
    values = values.at[ordering[0]].set(TGT).at[ordering[1]].set(TGT // 4)
    return values.astype(jnp.int32)


def draw_head_weight(key, part):
    key = jax.random.fold_in(key, 7)
    first_key = jax.random.fold_in(key, 0)
    factor = 5.0 / math.sqrt(D)
    weight = jax.random.truncated_normal(first_key, -4.0, 4.0, (D, VOCAB), jnp.float32) * factor
    return weight.astype(jnp.bfloat16)


def plant(entries, stream_key, smallest, top_value):
    place = [jax.random.randint(jax.random.fold_in(stream_key, axis), (), 0, length) for axis, length in enumerate(entries.shape)]
    widest = entries.shape.index(max(entries.shape))
    neighbour = place[:widest] + [(place[widest] + 1) % entries.shape[widest]] + place[widest + 1:]
    return entries.at[tuple(place)].set(smallest).at[tuple(neighbour)].set(top_value)


def block_scale(own_key, extent, cuts, low, high):
    def one(dim, shards_of):
        steps = jax.random.uniform(jax.random.fold_in(jax.random.fold_in(own_key, 6), dim), (shards_of,), jnp.float32, low / len(cuts), high / len(cuts))
        return jnp.repeat(jnp.exp(steps), extent[dim] // shards_of).reshape((-1,) + (1,) * (len(extent) - dim - 1))

    gain = one(*cuts[0])
    for cut in cuts[1:]:
        gain = gain * one(*cut)
    return gain


def wide_ids(rng, dims, count, slope):
    weights = [min(1 << octave, count + 1 - (1 << octave)) * (1 << 20) // math.isqrt((1 << octave) ** slope) + 1 for octave in range((count + 1).bit_length()) if 1 << octave <= count]
    scale = 1 + sum(weights) // (1 << 30)
    grid = np.cumsum(np.array([max(1, weight // scale) for weight in weights]))
    pick = jax.random.randint(jax.random.fold_in(rng, 1), dims, 0, int(grid[len(weights) - 1]))
    start = jnp.left_shift(1, jnp.searchsorted(jnp.asarray(grid, jnp.int32), pick, side="right").astype(jnp.int32))
    rank = start - 1 + jax.random.randint(jax.random.fold_in(rng, 4), dims, 0, 1 << 30) % jnp.minimum(start, count + 1 - start)
    return jax.random.permutation(jax.random.fold_in(rng, 2), count)[rank].astype(jnp.int32)


def shared_out(stream_key, own, number, rows, amount, top, bound, skew):
    ranking = jax.random.permutation(stream_key, amount)
    packed, ordinary = shares(amount, rows * top, bound, skew, True), shares(amount, rows * top, bound, skew, False)
    places = jnp.arange(amount)

    def named(sizes, offset_by):
        used = int((sizes > 0).sum())
        fixed = max(1, used // 4)
        shifted = fixed + (places - fixed + offset_by * (used - fixed)) % max(1, amount - fixed)
        return jnp.zeros((amount,), jnp.int32).at[ranking[jnp.where(places < fixed, places, shifted)]].set(jnp.asarray(sizes, jnp.int32))

    sizes = jnp.where(number % 4 == 0, named(packed, number // 4), named(ordinary, number - number // 4 - 1))
    mixed = jax.random.permutation(jax.random.fold_in(own, 3), amount)
    donor, sink = mixed[0:amount // 2 * 2:2], mixed[1:amount // 2 * 2:2]
    slack = jnp.minimum(sizes[donor] - 1, bound - sizes[sink]) // 2
    slack = jnp.where((donor == ranking[0]) | (sink == ranking[0]) | (sizes[sink] == 0), 0, jnp.maximum(slack, 0))
    shifted = jax.random.randint(jax.random.fold_in(own, 4), (amount // 2,), 0, 1 << 20) % (slack + 1)
    sizes = sizes.at[donor].add(-shifted).at[sink].add(shifted)
    items = jnp.searchsorted(jnp.cumsum(sizes), jnp.arange(rows * top), side="right").astype(jnp.int32)
    grid = items.reshape(top, rows).T
    grid = grid[jax.random.permutation(jax.random.fold_in(own, 1), rows)]
    offset_by = jax.random.randint(jax.random.fold_in(own, 2), (rows, 1), 0, top)
    return jnp.take_along_axis(grid, (jnp.arange(top)[None, :] + offset_by) % top, axis=1)


def shares(number_of, total, reach, skew, full):
    portions = [(1 << 20) // math.isqrt(grade ** skew) + 1 for grade in range(1, number_of + 1)]
    largest = reach if full else min(reach, max(-(-total // number_of), total * portions[0] // sum(portions)))
    least = 1 if total - largest >= number_of - 1 else 0
    counts, spare = [largest] + [least] * (number_of - 1), total - largest - least * (number_of - 1)
    while spare > 0:
        free = [i for i in range(1, number_of) if counts[i] < largest] or [i for i in range(1, number_of) if counts[i] < reach]
        mass, budget = sum([portions[i] for i in free]), spare
        for i in free:
            more = min(reach - counts[i], max(1, budget * portions[i] // mass), spare)
            counts[i] = counts[i] + more
            spare = spare - more
    return np.array(counts)


def bell_draw(key, shape, scale, bound, cuts=(), kind=jnp.bfloat16):
    factor_of = block_scale(key, shape, cuts, -0.22, 0.18) if cuts else 1.0
    result = jax.random.normal(key, shape, jnp.float32) * scale * factor_of
    return jnp.minimum(jnp.maximum(result, -bound), bound).astype(kind)


def setup_inputs(seed: int = 0) -> dict:
    splits = jax.random.split(jax.random.key(seed), 11)
    hidden = bell_draw(splits[0], (TOKENS, D), 1.0, 6.0, ((0, 256),))
    routes_keys = jax.random.split(jax.random.fold_in(splits[1], 1), TOKENS // ROWS)
    routes_turns = jax.random.permutation(jax.random.fold_in(splits[1], 3), TOKENS // ROWS)
    routes = jax.vmap(lambda own, number: shared_out(jax.random.fold_in(splits[1], 2), own, number, ROWS, EXPERTS, 2, CAP, 2))(routes_keys, routes_turns).reshape((TOKENS, 2))
    gates = jnp.clip(0.2 + 0.8 * jax.random.uniform(splits[2], (TOKENS, 2), jnp.float32) ** block_scale(splits[2], (TOKENS, 2), ((0, 256),), -0.2, 0.2), 0.2, 1.0)
    targets = plant(wide_ids(splits[3], (TOKENS,), VOCAB, 2), jax.random.fold_in(splits[3], 3), 0, VOCAB - 1).astype(jnp.int32)
    target_lengths = draw_target_lengths(jax.random.fold_in(splits[10], 71), 0)
    moe_gain = jnp.clip(1.0 + 0.1 * jax.random.normal(splits[5], (D,), jnp.float32), 0.5, 1.5)
    fc_in = bell_draw(splits[6], (EXPERTS, D, FF), D ** -0.5, 0.125, ((0, 16), (2, 16)))
    fc_out = bell_draw(splits[7], (EXPERTS, FF, D), FF ** -0.5, 0.0625, ((0, 16), (1, 16)))
    final_gain = jnp.clip(1.0 + 0.1 * jax.random.normal(splits[8], (D,), jnp.float32), 0.5, 1.5)
    head_weight = draw_head_weight(jax.random.fold_in(splits[10], 71), 0)
    return {"hidden": hidden, "routes": routes, "gates": gates, "targets": targets, "target_lengths": target_lengths, "moe_gain": moe_gain, "fc_in": fc_in, "fc_out": fc_out, "final_gain": final_gain, "head_weight": head_weight}


def layer_norm(values, scales):
    average = lax.optimization_barrier(jnp.mean(values, axis=-1, keepdims=True))
    centered = values - average
    spread = lax.optimization_barrier(jnp.mean(centered * centered, axis=-1, keepdims=True))
    return centered * lax.rsqrt(spread + 1e-05) * scales

def expert_pass(inputs):
    arrived, weight_in, weight_out = inputs
    hidden_units = jnp.maximum(jnp.dot(arrived, weight_in, preferred_element_type=jnp.float32), 0.0).astype(jnp.bfloat16)
    row_count = hidden_units.shape[0]
    block_width = FF // N_SECTION
    split_units = hidden_units.reshape(row_count, N_SECTION, block_width).astype(jnp.float32)
    split_weight = weight_out.reshape(N_SECTION, block_width, D).astype(jnp.float32)
    partials = jnp.einsum('rsf,sfd->srd', split_units, split_weight)
    rounded = lax.optimization_barrier(partials.astype(jnp.bfloat16))
    return lax.optimization_barrier(jnp.sum(rounded.astype(jnp.float32), axis=0)).astype(jnp.bfloat16)

def reference(hidden, routes, gates, targets, target_lengths, moe_gain, fc_in, fc_out, final_gain, head_weight):
    residual = hidden.astype(jnp.float32)
    normed = layer_norm(residual, moe_gain).astype(jnp.bfloat16)
    experts = fc_in.shape[0]
    blocks = TOKENS // ROWS
    block_routes = routes.reshape(blocks, 2 * ROWS).astype(jnp.int32)
    labels = jnp.arange(experts, dtype=jnp.int32)
    matches = (block_routes[:, :, None] == labels[None, None, :]).astype(jnp.int32)
    earlier = jnp.cumsum(matches, axis=1) - matches
    slot_index = lax.optimization_barrier(jnp.sum(earlier * matches, axis=2))
    block_ids = jnp.arange(blocks, dtype=jnp.int32)[:, None]
    placement = (block_routes * (blocks * CAP) + block_ids * CAP + slot_index).reshape(-1).astype(jnp.int32)
    copies = jnp.repeat(normed, 2, axis=0)
    buffers = jnp.zeros((experts * blocks * CAP, D), jnp.bfloat16).at[placement].set(copies)
    outputs = lax.map(expert_pass, (buffers.reshape(experts, blocks * CAP, D), fc_in, fc_out))
    results = outputs.reshape(experts * blocks * CAP, D)[placement].astype(jnp.float32).reshape(TOKENS, 2, D)
    mixed = residual + gates[:, 0:1] * results[:, 0] + gates[:, 1:2] * results[:, 1]
    final = layer_norm(mixed, final_gain).astype(jnp.bfloat16)
    logits = jnp.dot(final, head_weight, preferred_element_type=jnp.float32)
    head_logits = logits.astype(jnp.bfloat16)
    highest = lax.optimization_barrier(jnp.max(logits, axis=1))
    totals = lax.optimization_barrier(jnp.sum(jnp.exp(logits - highest[:, None]), axis=1))
    log_norm = highest + jnp.log(totals)
    log_probs = (logits - log_norm[:, None]).astype(jnp.bfloat16)
    picked = jnp.take_along_axis(logits, targets.astype(jnp.int32)[:, None], axis=1)[:, 0]
    positions = jnp.arange(TOKENS, dtype=jnp.int32)
    lengths = jnp.repeat(target_lengths.astype(jnp.int32), TGT)
    token_loss = jnp.where(positions % TGT < lengths, log_norm - picked, jnp.zeros_like(picked))
    return (log_probs, head_logits, token_loss)
```

```python
import jax
import jax.numpy as jnp
from jax import lax
from jax.experimental import pallas as pl
from jax.experimental.pallas import tpu as pltpu
from jax.sharding import PartitionSpec as P

TGT = 128
MESH = pl.DeviceIdType.MESH
HALF = 1024
PIECES = 8


def layer_norm(values, scales):
    average = jnp.mean(values, axis=-1, keepdims=True)
    centered = values - average
    spread = jnp.mean(centered * centered, axis=-1, keepdims=True)
    return centered * lax.rsqrt(spread + 1e-05) * scales


class Place:
    def __init__(self):
        self.s = lax.axis_index("section")
        self.e = lax.axis_index("expert")
        self.core = lax.rem(self.s, 2)
        self.y = lax.rem(lax.div(self.s, 2), 4)
        self.zl = lax.div(self.s, 8)
        self.x = lax.div(self.e, 4)
        self.zh = lax.rem(self.e, 4)
        self.z = self.zh * 2 + self.zl
        self.sibling = (self.s + 1 - 2 * self.core, self.e)

    def at(self, axis):
        return {"x": self.x, "y": self.y, "z": self.z}[axis]

    def beside(self, axis, step):
        x, y, z = self.x, self.y, self.z
        if axis == "x":
            x = lax.rem(x + step + 4, 4)
        elif axis == "y":
            y = lax.rem(y + step + 4, 4)
        else:
            z = lax.rem(z + step + 8, 8)
        return ((lax.rem(z, 2) * 4 + y) * 2 + self.core, x * 4 + lax.div(z, 2))


def remote(src, dst, send, recv, to):
    return pltpu.make_async_remote_copy(
        src_ref=src, dst_ref=dst, send_sem=send, recv_sem=recv, device_id=to, device_id_type=MESH
    )


ORDERS = ((("x", 4), ("y", 4), ("z", 8)), (("z", 8), ("x", 4), ("y", 4)))


def view(g, core, phase, where, pos, part):
    lanes = slice(None) if part is None else pl.ds(part * (HALF // 2), HALF // 2)
    if core == 0:
        if phase == 0:
            return g.at[0, where.zl, where.y, pos, where.zh, :, lanes]
        if phase == 1:
            return g.at[0, where.zl, pos, :, where.zh, :, lanes]
        return g.at[0, lax.rem(pos, 2), :, :, lax.div(pos, 2), :, lanes]
    if phase == 0:
        return g.at[1, lax.rem(pos, 2), where.y, where.x, lax.div(pos, 2), :, lanes]
    if phase == 1:
        return g.at[1, :, where.y, pos, :, :, lanes]
    return g.at[1, :, pos, :, :, :, lanes]


def arrivals(g, core, where):
    for phase, (axis, n) in enumerate(ORDERS[core]):
        me = where.at(axis)
        for step in range(1, n // 2 + 1):
            last = step == n // 2
            parts = (0, 1) if last else (None, None)
            sends = (
                view(g, core, phase, where, lax.rem(me - step + 1 + n, n), parts[0]),
                view(g, core, phase, where, lax.rem(me + step - 1, n), parts[1]),
            )
            lands = (
                view(g, core, phase, where, lax.rem(me - step + n, n), parts[0]),
                view(g, core, phase, where, lax.rem(me + step, n), parts[1]),
            )
            yield axis, sends, lands


def gather(core, where, g, ring_send, ring_recv, pair_send, pair_recv):
    own = g.at[core, where.zl, where.y, where.x, where.zh]
    shared = [(own, remote(own, own, pair_send.at[0], pair_recv.at[0], where.sibling))]
    shared[0][1].start()
    sent = []
    k = 0
    for axis, sends, lands in arrivals(g, core, where):
        for side in (0, 1):
            to = where.beside(axis, 1 - 2 * side)
            copy = remote(sends[side], sends[side], ring_send.at[k + side], ring_recv.at[k + side], to)
            copy.start()
            sent.append(copy)
        for side in (0, 1):
            landed = lands[side]
            remote(
                landed, landed, ring_send.at[k + side], ring_recv.at[k + side], where.beside(axis, 2 * side - 1)
            ).wait_recv()
            copy = remote(landed, landed, pair_send.at[1 + k + side], pair_recv.at[1 + k + side], where.sibling)
            copy.start()
            shared.append((landed, copy))
        k += 2
    other = g.at[1 - core, where.zl, where.y, where.x, where.zh]
    remote(other, other, pair_send.at[0], pair_recv.at[0], where.sibling).wait_recv()
    k = 1
    for _, _, lands in arrivals(g, 1 - core, where):
        for side in (0, 1):
            landed = lands[side]
            remote(landed, landed, pair_send.at[k], pair_recv.at[k], where.sibling).wait_recv()
            k += 1
    for copy in sent:
        copy.wait_send()
    for _, copy in shared:
        copy.wait_send()


def exchange(n, me, to, src, dst, send, recv):
    def each(i, _):
        other = lax.rem(me + i, n)
        remote(src(other), dst.at[me], send.at[i], recv.at[i], to(other)).start()
        return 0

    lax.fori_loop(1, n, each, 0)

    def done(i, _):
        origin = lax.rem(me - i + n, n)
        copy = remote(src(origin), dst.at[origin], send.at[i], recv.at[i], to(origin))
        copy.wait_recv()
        copy.wait_send()
        return 0

    lax.fori_loop(1, n, done, 0)


def merge(stats):
    high = stats[:, 0:1, :]
    top = jnp.max(high, axis=0)
    total = jnp.sum(stats[:, 1:2, :] * jnp.exp(high - top[None]), axis=0)
    return top, total, jnp.sum(stats[:, 2:3, :], axis=0)


def rows8(first, second, third):
    row = lax.broadcasted_iota(jnp.int32, (8, 128), 0)
    zero = jnp.zeros((8, 128), jnp.float32)
    out = jnp.where(row == 0, first, zero)
    out = jnp.where(row == 1, second, out)
    return jnp.where(row == 2, third, out)


def head_kernel(
    final_ref, targets_ref, weight_hbm, logits_hbm, norms_ref,
    g, weight, logits, halves, stats, by_group, by_section, merged, solved,
    weight_sem, out_sem, swap_send, swap_recv, ring_send, ring_recv, pair_send, pair_recv,
    one_send, one_recv, two_send, two_recv, three_send, three_recv,
):
    where = Place()
    barrier = pltpu.get_barrier_semaphore()
    load = pltpu.make_async_copy(weight_hbm, weight, weight_sem)
    load.start()

    def greet(i, _):
        pl.semaphore_signal(
            barrier, inc=1, device_id=(lax.rem(where.s + i, 16), where.e), device_id_type=MESH
        )
        pl.semaphore_signal(
            barrier, inc=1, device_id=(where.s, lax.rem(where.e + i, 16)), device_id_type=MESH
        )
        return 0

    lax.fori_loop(1, 16, greet, 0)
    for step in (1, -1):
        pl.semaphore_signal(barrier, inc=1, device_id=where.beside("z", step), device_id_type=MESH)
    pl.semaphore_wait(barrier, 32)

    for core in (0, 1):

        @pl.when(where.core == core)
        def _():
            away = final_ref.at[:, pl.ds((1 - core) * HALF, HALF)]
            swap = remote(away, halves, swap_send, swap_recv, where.sibling)
            swap.start()
            swap.wait()
            mine = final_ref[:, core * HALF : (core + 1) * HALF]
            both = (mine, halves[...]) if core == 0 else (halves[...], mine)
            g[core, where.zl, where.y, where.x, where.zh] = jnp.concatenate(both, axis=0).astype(jnp.bfloat16)
            gather(core, where, g, ring_send, ring_recv, pair_send, pair_recv)

    load.wait()
    columns = weight.shape[1]
    offset = (where.s * 16 + where.e) * columns
    lane = lax.broadcasted_iota(jnp.int32, (128, 128), 1)

    def chunk(i, _):
        zl, y = lax.div(i, 4), lax.rem(i, 4)
        low = g[0, zl, y].reshape(256, HALF)
        high = g[1, zl, y].reshape(256, HALF)
        found = jnp.dot(low, weight[0:HALF], preferred_element_type=jnp.float32)
        found = found + jnp.dot(high, weight[HALF:], preferred_element_type=jnp.float32)
        found = found.reshape(16, 2, 8, columns)
        for core in (0, 1):
            group = i * 2 + core
            part = found[:, core].reshape(128, columns)
            logits[pl.ds(group * 128, 128), :] = part
            top = jnp.max(part, axis=1, keepdims=True)
            total = jnp.sum(jnp.exp(part - top), axis=1, keepdims=True)
            wanted = jnp.transpose(jnp.broadcast_to(targets_ref[pl.ds(group, 1), :], (128, 128)))
            picked = jnp.zeros((128, 128), jnp.float32)
            for tile in range(columns // 128):
                ids = (lane + (offset + tile * 128)).astype(jnp.float32)
                picked = picked + jnp.where(ids == wanted, part[:, tile * 128 : (tile + 1) * 128], 0.0)
            picked = jnp.sum(picked, axis=1, keepdims=True)
            table = jnp.where(lane == 0, top, jnp.where(lane == 1, total, jnp.where(lane == 2, picked, 0.0)))
            stats[group] = jnp.transpose(table)[0:8]
        pltpu.make_async_copy(
            logits.at[pl.ds(i * 256, 256)], logits_hbm.at[pl.ds(i * 256, 256)], out_sem.at[i]
        ).start()
        return 0

    lax.fori_loop(0, PIECES, chunk, 0)

    to_expert = lambda other: (where.s, other)
    to_section = lambda other: (other, where.e)
    by_group[where.e] = stats[where.e]
    exchange(16, where.e, to_expert, lambda other: stats.at[other], by_group, one_send, one_recv)
    merged[...] = rows8(*merge(by_group[...]))
    by_section[where.s] = merged[...]
    exchange(16, where.s, to_section, lambda other: merged, by_section, two_send, two_recv)
    top, total, picked = merge(by_section[...])
    log_norm = top + jnp.log(total)
    solved[...] = rows8(log_norm, log_norm - picked, jnp.zeros_like(picked))
    norms_ref[where.e] = solved[...]
    exchange(16, where.e, to_expert, lambda other: solved, norms_ref, three_send, three_recv)

    def stored(i, _):
        pltpu.make_async_copy(
            logits.at[pl.ds(i * 256, 256)], logits_hbm.at[pl.ds(i * 256, 256)], out_sem.at[i]
        ).wait()
        return 0

    lax.fori_loop(0, PIECES, stored, 0)


def head(final, targets, weight):
    features, columns = weight.shape
    tokens = targets.size
    dma = pltpu.SemaphoreType.DMA
    return pl.pallas_call(
        head_kernel,
        name="head",
        out_shape=(
            jax.ShapeDtypeStruct((tokens, columns), jnp.float32),
            jax.ShapeDtypeStruct((16, 8, 128), jnp.float32),
        ),
        in_specs=[
            pl.BlockSpec(memory_space=pltpu.VMEM),
            pl.BlockSpec(memory_space=pltpu.VMEM),
            pl.BlockSpec(memory_space=pl.ANY),
        ],
        out_specs=(pl.BlockSpec(memory_space=pl.ANY), pl.BlockSpec(memory_space=pltpu.VMEM)),
        scratch_shapes=[
            pltpu.VMEM((2, 2, 4, 4, 4, 16, HALF), jnp.bfloat16),
            pltpu.VMEM((features, columns), jnp.bfloat16),
            pltpu.VMEM((tokens, columns), jnp.float32),
            pltpu.VMEM((8, HALF), jnp.float32),
            pltpu.VMEM((16, 8, 128), jnp.float32),
            pltpu.VMEM((16, 8, 128), jnp.float32),
            pltpu.VMEM((16, 8, 128), jnp.float32),
            pltpu.VMEM((8, 128), jnp.float32),
            pltpu.VMEM((8, 128), jnp.float32),
            dma, dma((PIECES,)), dma, dma,
            dma((16,)), dma((16,)), dma((17,)), dma((17,)),
            dma((16,)), dma((16,)), dma((16,)), dma((16,)), dma((16,)), dma((16,)),
        ],
        compiler_params=pltpu.CompilerParams(
            collective_id=1, has_side_effects=True, vmem_limit_bytes=48 * 1024 * 1024
        ),
    )(final, targets, weight)


def finish_kernel(logits_ref, norms_ref, lengths_ref, probs_ref, head_ref, loss_ref):
    values = logits_ref[...]
    head_ref[...] = values.astype(jnp.bfloat16)
    shift = jnp.transpose(jnp.broadcast_to(norms_ref[0, 0:1, :], (128, 128)))
    for tile in range(values.shape[1] // 128):
        lanes = slice(tile * 128, (tile + 1) * 128)
        probs_ref[:, lanes] = (values[:, lanes] - shift).astype(jnp.bfloat16)

    position = lax.broadcasted_iota(jnp.int32, (1, 128), 1)
    group = pl.program_id(0)
    loss_ref[pl.ds(group, 1), :] = jnp.where(position < lengths_ref[group], norms_ref[0, 1:2, :], 0.0)


def finish(logits, norms, lengths):
    tokens, columns = logits.shape
    groups = tokens // TGT
    rows = pl.BlockSpec((TGT, columns), lambda i: (i, 0))
    return pl.pallas_call(
        finish_kernel,
        name="finish",
        grid=(groups,),
        out_shape=(
            jax.ShapeDtypeStruct((tokens, columns), jnp.bfloat16),
            jax.ShapeDtypeStruct((tokens, columns), jnp.bfloat16),
            jax.ShapeDtypeStruct((groups, TGT), jnp.float32),
        ),
        in_specs=[
            rows,
            pl.BlockSpec((1, 8, 128), lambda i: (i, 0, 0)),
            pl.BlockSpec(memory_space=pltpu.SMEM),
        ],
        out_specs=(rows, rows, pl.BlockSpec((groups, TGT), lambda i: (0, 0))),
    )(logits, norms, lengths)


def on_device(
    hidden, routes, gates, targets, target_lengths, moe_gain, fc_in, fc_out, final_gain, head_weight
):
    token_rows = hidden.shape[0]
    features = hidden.shape[1]
    groups = lax.axis_size("expert")
    capacity = max(2, (3 * token_rows + groups - 1) // groups)
    residual = hidden.astype(jnp.float32)
    normed = layer_norm(residual, moe_gain).astype(jnp.bfloat16)
    flat_routes = routes.reshape(-1)
    labels = jnp.arange(groups, dtype=jnp.int32)
    matches = (flat_routes[:, None] == labels[None, :]).astype(jnp.int32)
    earlier = jnp.cumsum(matches, axis=0) - matches
    slot_index = jnp.sum(earlier * matches, axis=1)
    placement = flat_routes * capacity + slot_index
    copies = jnp.repeat(normed, 2, axis=0)
    outgoing = jnp.zeros((groups * capacity, features), jnp.bfloat16).at[placement].set(copies)
    outgoing = outgoing.reshape(groups, capacity, features)
    weight_in = fc_in[0]
    weight_out = fc_out[0]
    block_rows = lax.all_gather(
        lax.all_to_all(outgoing, "expert", split_axis=0, concat_axis=0, tiled=True),
        "section",
        axis=0,
        tiled=True,
    )
    sources = block_rows.shape[0]
    slot_count = block_rows.shape[1]
    flattened = block_rows.reshape(sources * slot_count, features)
    hidden_units = jnp.maximum(
        jnp.dot(flattened, weight_in, preferred_element_type=jnp.float32), 0.0
    ).astype(jnp.bfloat16)
    partial_value = jnp.dot(hidden_units, weight_out, preferred_element_type=jnp.float32)
    partials = partial_value.reshape(sources, slot_count, features)
    summed = lax.psum_scatter(
        partials.astype(jnp.bfloat16), "section", scatter_dimension=0, tiled=True
    )
    returned_rows = lax.all_to_all(summed, "expert", split_axis=0, concat_axis=0, tiled=True)
    results = returned_rows.reshape(groups * capacity, features)[placement]
    results = results.astype(jnp.float32).reshape(token_rows, 2, features)
    mixed = residual + gates[:, 0:1] * results[:, 0] + gates[:, 1:2] * results[:, 1]
    final = layer_norm(mixed, final_gain).astype(jnp.bfloat16)
    wanted = targets.astype(jnp.float32).reshape(-1, TGT)
    logits, norms = head(final.astype(jnp.float32), wanted, head_weight)
    log_probs, head_logits, loss = finish(logits, norms, target_lengths)
    return (log_probs, head_logits, loss.reshape(-1))


def solution(mesh):
    return jax.shard_map(
        on_device,
        mesh=mesh,
        in_specs=(
            P(("section", "expert"), None),
            P(("section", "expert"), None),
            P(("section", "expert"), None),
            P(),
            P(),
            P(),
            P("expert", None, "section"),
            P("expert", "section", None),
            P(),
            P(None, ("section", "expert")),
        ),
        out_specs=(P(None, ("section", "expert")), P(None, ("section", "expert")), P()),
        check_vma=False,
    )
```

```python
import jax
import jax.numpy as jnp
from jax import lax
from jax.experimental import pallas as pl
from jax.experimental.pallas import tpu as pltpu
from jax.sharding import PartitionSpec as P

TGT = 128
MESH = pl.DeviceIdType.MESH
HALF = 1024
PIECES = 8
QUARTERS = 4


class Place:
    def __init__(self):
        self.s = lax.axis_index("section")
        self.e = lax.axis_index("expert")
        self.core = lax.rem(self.s, 2)
        self.y = lax.rem(lax.div(self.s, 2), 4)
        self.zl = lax.div(self.s, 8)
        self.x = lax.div(self.e, 4)
        self.zh = lax.rem(self.e, 4)
        self.z = self.zh * 2 + self.zl
        self.sibling = (self.s + 1 - 2 * self.core, self.e)

    def at(self, axis):
        return {"x": self.x, "y": self.y, "z": self.z}[axis]

    def beside(self, axis, step):
        x, y, z = self.x, self.y, self.z
        if axis == "x":
            x = lax.rem(x + step + 4, 4)
        elif axis == "y":
            y = lax.rem(y + step + 4, 4)
        else:
            z = lax.rem(z + step + 8, 8)
        return ((lax.rem(z, 2) * 4 + y) * 2 + self.core, x * 4 + lax.div(z, 2))


def remote(src, dst, send, recv, to):
    return pltpu.make_async_remote_copy(
        src_ref=src, dst_ref=dst, send_sem=send, recv_sem=recv, device_id=to, device_id_type=MESH
    )


ORDERS = ((("x", 4), ("y", 4), ("z", 8)), (("z", 8), ("x", 4), ("y", 4)))


def view(g, core, phase, where, pos, part):
    lanes = slice(None) if part is None else pl.ds(part * (HALF // 2), HALF // 2)
    if core == 0:
        if phase == 0:
            return g.at[0, where.zl, where.y, pos, where.zh, :, lanes]
        if phase == 1:
            return g.at[0, where.zl, pos, :, where.zh, :, lanes]
        return g.at[0, lax.rem(pos, 2), :, :, lax.div(pos, 2), :, lanes]
    if phase == 0:
        return g.at[1, lax.rem(pos, 2), where.y, where.x, lax.div(pos, 2), :, lanes]
    if phase == 1:
        return g.at[1, :, where.y, pos, :, :, lanes]
    return g.at[1, :, pos, :, :, :, lanes]


def arrivals(g, core, where):
    for phase, (axis, n) in enumerate(ORDERS[core]):
        me = where.at(axis)
        for step in range(1, n // 2 + 1):
            last = step == n // 2
            parts = (0, 1) if last else (None, None)
            sends = (
                view(g, core, phase, where, lax.rem(me - step + 1 + n, n), parts[0]),
                view(g, core, phase, where, lax.rem(me + step - 1, n), parts[1]),
            )
            lands = (
                view(g, core, phase, where, lax.rem(me - step + n, n), parts[0]),
                view(g, core, phase, where, lax.rem(me + step, n), parts[1]),
            )
            yield axis, sends, lands


def gather(core, where, g, ring_send, ring_recv, pair_send, pair_recv):
    own = g.at[core, where.zl, where.y, where.x, where.zh]
    shared = [(own, remote(own, own, pair_send.at[0], pair_recv.at[0], where.sibling))]
    shared[0][1].start()
    sent = []
    k = 0
    for axis, sends, lands in arrivals(g, core, where):
        for side in (0, 1):
            to = where.beside(axis, 1 - 2 * side)
            copy = remote(sends[side], sends[side], ring_send.at[k + side], ring_recv.at[k + side], to)
            copy.start()
            sent.append(copy)
        for side in (0, 1):
            landed = lands[side]
            remote(
                landed, landed, ring_send.at[k + side], ring_recv.at[k + side], where.beside(axis, 2 * side - 1)
            ).wait_recv()
            copy = remote(landed, landed, pair_send.at[1 + k + side], pair_recv.at[1 + k + side], where.sibling)
            copy.start()
            shared.append((landed, copy))
        k += 2
    other = g.at[1 - core, where.zl, where.y, where.x, where.zh]
    remote(other, other, pair_send.at[0], pair_recv.at[0], where.sibling).wait_recv()
    k = 1
    for _, _, lands in arrivals(g, 1 - core, where):
        for side in (0, 1):
            landed = lands[side]
            remote(landed, landed, pair_send.at[k], pair_recv.at[k], where.sibling).wait_recv()
            k += 1
    for copy in sent:
        copy.wait_send()
    for _, copy in shared:
        copy.wait_send()


def exchange(n, me, to, src, dst, send, recv):
    def each(i, _):
        other = lax.rem(me + i, n)
        remote(src(other), dst.at[me], send.at[i], recv.at[i], to(other)).start()
        return 0

    lax.fori_loop(1, n, each, 0)

    def done(i, _):
        origin = lax.rem(me - i + n, n)
        copy = remote(src(origin), dst.at[origin], send.at[i], recv.at[i], to(origin))
        copy.wait_recv()
        copy.wait_send()
        return 0

    lax.fori_loop(1, n, done, 0)


def merge(stats):
    high = stats[:, 0:1, :]
    top = jnp.max(high, axis=0)
    total = jnp.sum(stats[:, 1:2, :] * jnp.exp(high - top[None]), axis=0)
    return top, total, jnp.sum(stats[:, 2:3, :], axis=0)


def rows8(first, second, third):
    row = lax.broadcasted_iota(jnp.int32, (8, 128), 0)
    zero = jnp.zeros((8, 128), jnp.float32)
    out = jnp.where(row == 0, first, zero)
    out = jnp.where(row == 1, second, out)
    return jnp.where(row == 2, third, out)


def one_hot(table, tokens):
    shape = (tokens, 256)
    column = lax.broadcasted_iota(jnp.int32, shape, 1)
    token = lax.broadcasted_iota(jnp.int32, shape, 0)
    expert = lax.div(column, 16).astype(jnp.float32)
    slot = lax.rem(lax.div(column, 4), 2).astype(jnp.float32)
    same = lax.rem(lax.div(column, 8), 2) == lax.div(token, 8)
    piece = lax.rem(column, 4)
    hits = [jnp.where(table[:, k : k + 1] == expert, 1.0, 0.0) for k in (0, 1)]
    later = lax.broadcasted_iota(jnp.int32, (tokens, tokens), 0)
    sooner = lax.broadcasted_iota(jnp.int32, (tokens, tokens), 1)
    before = jnp.where((sooner < later) & (lax.div(sooner, 8) == lax.div(later, 8)), 1.0, 0.0)
    earlier = jnp.dot(
        before.astype(jnp.bfloat16), (hits[0] + hits[1]).astype(jnp.bfloat16), preferred_element_type=jnp.float32
    )
    placed = [jnp.where(same & (earlier == slot), hit, 0.0) for hit in hits]
    return [
        jnp.concatenate([jnp.where(piece == j, one, 0.0) for j in range(QUARTERS)], axis=0) for one in placed
    ]


def stack(values):
    return jnp.concatenate([values[:, j * 256 : (j + 1) * 256] for j in range(QUARTERS)], axis=0)


def experts(
    where, hidden_ref, routes_ref, gates_ref, gain_ref, final_gain_ref, weight_in, weight_out, loads, g,
    pack, outgoing, incoming, rows, units, away, sent_half, near, summed, parts, returning, returned, spread,
    pack_send, pack_recv, go_send, go_recv, row_send, row_recv, rowp_send, rowp_recv, half_send, half_recv,
    sum_send, sum_recv, back_send, back_recv, ln_send, ln_recv,
):
    core, m = where.core, where.y * 2 + where.zl
    mine = pl.ds(pl.multiple_of(core * HALF, HALF), HALF)
    theirs = pl.ds(pl.multiple_of((1 - core) * HALF, HALF), HALF)
    to_expert = lambda other: (where.s, other)
    to_chip = lambda other: ((lax.rem(other, 2) * 4 + lax.div(other, 2)) * 2 + core, where.e)
    features = 2 * HALF

    lane = lax.broadcasted_iota(jnp.int32, (8, 128), 1)
    routes = routes_ref[...].astype(jnp.float32)
    gates = gates_ref[...]
    table = jnp.where(lane == 0, routes[:, 0:1], jnp.where(lane == 1, routes[:, 1:2], 0.0))
    table = jnp.where(lane == 2, gates[:, 0:1], jnp.where(lane == 3, gates[:, 1:2], table))
    pack[core, :, 0:features] = hidden_ref[...].astype(jnp.float32)
    pack[core, :, features:] = table
    swap = remote(pack.at[core], pack.at[core], pack_send, pack_recv, where.sibling)
    swap.start()
    swap.wait()

    tokens = 16
    whole = pack[:, :, 0:features].reshape(tokens, features)
    table = pack[:, :, features:].reshape(tokens, 128)
    average = jnp.mean(whole, axis=-1, keepdims=True)
    centered = whole - average
    spread_of = jnp.mean(centered * centered, axis=-1, keepdims=True)
    residual = pack[:, :, mine].reshape(tokens, HALF)
    normed = ((residual - average) * lax.rsqrt(spread_of + 1e-05) * gain_ref[:, mine]).astype(jnp.bfloat16)
    chosen = one_hot(table, tokens)
    place = jnp.transpose(chosen[0] + chosen[1]).astype(jnp.bfloat16)
    slots = jnp.dot(place, stack(normed), preferred_element_type=jnp.float32).astype(jnp.bfloat16)
    outgoing[...] = slots.reshape(16, 16, 256)
    incoming[where.e] = outgoing[where.e]
    exchange(16, where.e, to_expert, lambda other: outgoing.at[other], incoming, go_send, go_recv)

    down = lax.broadcasted_iota(jnp.int32, (256, 256), 0)
    across = lax.broadcasted_iota(jnp.int32, (256, 256), 1)
    split = jnp.where(across == 4 * lax.rem(down, 64) + lax.div(down, 64), 1.0, 0.0).astype(jnp.bfloat16)
    join = jnp.where(down == 4 * lax.rem(across, 64) + lax.div(across, 64), 1.0, 0.0).astype(jnp.bfloat16)
    arrived = jnp.dot(split, incoming[...].reshape(256, 256), preferred_element_type=jnp.float32)
    for j in range(QUARTERS):
        rows[core, m, :, j * 256 : (j + 1) * 256] = arrived[j * 64 : (j + 1) * 64].astype(jnp.bfloat16)

    own = rows.at[core, m]
    pair = lambda i, block: remote(block, block, rowp_send.at[i], rowp_recv.at[i], where.sibling)
    pair(0, own).start()

    def send_rows(i, _):
        remote(own, own, row_send.at[i], row_recv.at[i], to_chip(lax.rem(m + i, 8))).start()
        return 0

    def take_rows(i, _):
        origin = lax.rem(m - i + 8, 8)
        block = rows.at[core, origin]
        remote(block, block, row_send.at[i], row_recv.at[i], to_chip(origin)).wait_recv()
        pair(i, block).start()
        return 0

    def take_pair(i, _):
        pair(i, rows.at[1 - core, lax.rem(m - i + 8, 8)]).wait_recv()
        return 0

    def rows_left(i, _):
        remote(own, own, row_send.at[i], row_recv.at[i], to_chip(lax.rem(m + i, 8))).wait_send()
        return 0

    def pairs_left(i, _):
        pair(i, own).wait_send()
        return 0

    lax.fori_loop(1, 8, send_rows, 0)
    lax.fori_loop(1, 8, take_rows, 0)
    lax.fori_loop(0, 8, take_pair, 0)

    loads[0].wait()
    loads[1].wait()

    def first(i, _):
        low = rows[0, pl.ds(i * 4, 4)].reshape(256, HALF)
        high = rows[1, pl.ds(i * 4, 4)].reshape(256, HALF)
        found = jnp.dot(low, weight_in[0:HALF], preferred_element_type=jnp.float32)
        found = found + jnp.dot(high, weight_in[HALF:], preferred_element_type=jnp.float32)
        units[pl.ds(i * 2, 2)] = jnp.maximum(found, 0.0).astype(jnp.bfloat16).reshape(2, 128, -1)
        return 0

    lax.fori_loop(0, 2, first, 0)

    def half(i, other):
        return remote(away.at[other], sent_half.at[other], half_send.at[i], half_recv.at[i], where.sibling)

    def second(i, _):
        other = lax.rem(where.y + 1 + i, 4)
        some = units[other]
        away[other] = jnp.dot(some, weight_out[:, theirs], preferred_element_type=jnp.float32).astype(jnp.bfloat16)
        half(i, other).start()
        near[other] = jnp.dot(some, weight_out[:, mine], preferred_element_type=jnp.float32)
        return 0

    lax.fori_loop(0, 4, second, 0)

    def part(block, origin):
        return remote(summed.at[block], parts.at[origin], sum_send.at[block], sum_recv.at[origin], to_chip(block))

    def add(i, _):
        other = lax.rem(where.y + 1 + i, 4)
        half(i, other).wait_recv()
        total = (near[other] + sent_half[other].astype(jnp.float32)).astype(jnp.bfloat16)
        summed[pl.ds(other * 2, 2)] = total.reshape(2, 64, HALF)
        for side in (0, 1):
            block = other * 2 + side

            @pl.when(block != m)
            def _():
                part(block, m).start()

        return 0

    lax.fori_loop(0, 4, add, 0)
    parts[m] = summed[m]

    def take_part(i, _):
        origin = lax.rem(m - i + 8, 8)
        remote(summed.at[origin], parts.at[origin], sum_send.at[origin], sum_recv.at[origin], to_chip(origin)).wait_recv()
        return 0

    lax.fori_loop(1, 8, take_part, 0)
    total = parts[0].astype(jnp.float32)
    for i in range(1, 8):
        total = total + parts[i].astype(jnp.float32)
    results = jnp.dot(join, stack(total.astype(jnp.bfloat16)), preferred_element_type=jnp.float32)
    returning[...] = results.astype(jnp.bfloat16).reshape(16, 16, 256)
    returned[where.e] = returning[where.e]
    exchange(16, where.e, to_expert, lambda other: returning.at[other], returned, back_send, back_recv)

    back = returned[...].reshape(256, 256)
    mixed = [residual[:, j * 256 : (j + 1) * 256] for j in range(QUARTERS)]
    for k in (0, 1):
        found = jnp.dot(chosen[k].astype(jnp.bfloat16), back, preferred_element_type=jnp.float32)
        gate = table[:, 2 + k : 3 + k]
        mixed = [old + gate * found[j * tokens : (j + 1) * tokens] for j, old in enumerate(mixed)]
    mixed = jnp.concatenate(mixed, axis=1)
    center = jnp.mean(mixed, axis=-1, keepdims=True)
    squares = jnp.sum((mixed - center) * (mixed - center), axis=-1, keepdims=True)
    lane = lax.broadcasted_iota(jnp.int32, (tokens, 128), 1)
    spread[core] = jnp.where(lane == 0, center, jnp.where(lane == 1, squares, 0.0))
    swap = remote(spread.at[core], spread.at[core], ln_send, ln_recv, where.sibling)
    swap.start()
    swap.wait()
    centers = [spread[i, :, 0:1] for i in (0, 1)]
    average = 0.5 * (centers[0] + centers[1])
    apart = centers[0] - centers[1]
    variance = (spread[0, :, 1:2] + spread[1, :, 1:2] + apart * apart * (0.5 * HALF)) / features
    final = (mixed - average) * lax.rsqrt(variance + 1e-05) * final_gain_ref[:, mine]
    g[core, where.zl, where.y, where.x, where.zh] = final.astype(jnp.bfloat16)

    lax.fori_loop(1, 8, rows_left, 0)
    lax.fori_loop(0, 8, pairs_left, 0)

    def halves_left(i, _):
        half(i, lax.rem(where.y + 1 + i, 4)).wait_send()
        return 0

    lax.fori_loop(0, 4, halves_left, 0)

    def parts_left(i, _):
        part(lax.rem(m + i, 8), m).wait_send()
        return 0

    lax.fori_loop(1, 8, parts_left, 0)


def layer_kernel(
    hidden_ref, routes_ref, gates_ref, gain_ref, final_gain_ref, targets_ref, in_hbm, out_hbm, weight_hbm,
    logits_hbm, norms_ref,
    g, weight, logits, stats, by_group, by_section, merged, solved,
    weight_sem, out_sem, ring_send, ring_recv, pair_send, pair_recv,
    one_send, one_recv, two_send, two_recv, three_send, three_recv,
    weight_in, weight_out, weight_sems, *scratch,
):
    where = Place()
    barrier = pltpu.get_barrier_semaphore()
    load = pltpu.make_async_copy(weight_hbm, weight, weight_sem)
    loads = [
        pltpu.make_async_copy(in_hbm.at[0], weight_in, weight_sems.at[0]),
        pltpu.make_async_copy(out_hbm.at[0], weight_out, weight_sems.at[1]),
    ]
    for one in loads:
        one.start()
    load.start()

    def greet(i, _):
        pl.semaphore_signal(
            barrier, inc=1, device_id=(lax.rem(where.s + i, 16), where.e), device_id_type=MESH
        )
        pl.semaphore_signal(
            barrier, inc=1, device_id=(where.s, lax.rem(where.e + i, 16)), device_id_type=MESH
        )
        return 0

    lax.fori_loop(1, 16, greet, 0)
    for step in (1, -1):
        pl.semaphore_signal(barrier, inc=1, device_id=where.beside("z", step), device_id_type=MESH)
    pl.semaphore_wait(barrier, 32)

    experts(
        where, hidden_ref, routes_ref, gates_ref, gain_ref, final_gain_ref, weight_in, weight_out, loads, g, *scratch
    )
    for core in (0, 1):

        @pl.when(where.core == core)
        def _():
            gather(core, where, g, ring_send, ring_recv, pair_send, pair_recv)

    load.wait()
    columns = weight.shape[1]
    offset = (where.s * 16 + where.e) * columns
    lane = lax.broadcasted_iota(jnp.int32, (128, 128), 1)

    def chunk(i, _):
        zl, y = lax.div(i, 4), lax.rem(i, 4)
        low = g[0, zl, y].reshape(256, HALF)
        high = g[1, zl, y].reshape(256, HALF)
        found = jnp.dot(low, weight[0:HALF], preferred_element_type=jnp.float32)
        found = found + jnp.dot(high, weight[HALF:], preferred_element_type=jnp.float32)
        found = found.reshape(16, 2, 8, columns)
        for core in (0, 1):
            group = i * 2 + core
            part = found[:, core].reshape(128, columns)
            logits[pl.ds(group * 128, 128), :] = part
            top = jnp.max(part, axis=1, keepdims=True)
            total = jnp.sum(jnp.exp(part - top), axis=1, keepdims=True)
            wanted = jnp.transpose(jnp.broadcast_to(targets_ref[pl.ds(group, 1), :], (128, 128)))
            picked = jnp.zeros((128, 128), jnp.float32)
            for tile in range(columns // 128):
                ids = (lane + (offset + tile * 128)).astype(jnp.float32)
                picked = picked + jnp.where(ids == wanted, part[:, tile * 128 : (tile + 1) * 128], 0.0)
            picked = jnp.sum(picked, axis=1, keepdims=True)
            table = jnp.where(lane == 0, top, jnp.where(lane == 1, total, jnp.where(lane == 2, picked, 0.0)))
            stats[group] = jnp.transpose(table)[0:8]
        pltpu.make_async_copy(
            logits.at[pl.ds(i * 256, 256)], logits_hbm.at[pl.ds(i * 256, 256)], out_sem.at[i]
        ).start()
        return 0

    lax.fori_loop(0, PIECES, chunk, 0)

    to_expert = lambda other: (where.s, other)
    to_section = lambda other: (other, where.e)
    by_group[where.e] = stats[where.e]
    exchange(16, where.e, to_expert, lambda other: stats.at[other], by_group, one_send, one_recv)
    merged[...] = rows8(*merge(by_group[...]))
    by_section[where.s] = merged[...]
    exchange(16, where.s, to_section, lambda other: merged, by_section, two_send, two_recv)
    top, total, picked = merge(by_section[...])
    log_norm = top + jnp.log(total)
    solved[...] = rows8(log_norm, log_norm - picked, jnp.zeros_like(picked))
    norms_ref[where.e] = solved[...]
    exchange(16, where.e, to_expert, lambda other: solved, norms_ref, three_send, three_recv)

    def stored(i, _):
        pltpu.make_async_copy(
            logits.at[pl.ds(i * 256, 256)], logits_hbm.at[pl.ds(i * 256, 256)], out_sem.at[i]
        ).wait()
        return 0

    lax.fori_loop(0, PIECES, stored, 0)


def layer(hidden, routes, gates, gain, final_gain, targets, weight_in, weight_out, weight):
    features, columns = weight.shape
    tokens = targets.size
    inner = weight_in.shape[2]
    dma = pltpu.SemaphoreType.DMA
    bf16, f32 = jnp.bfloat16, jnp.float32
    vmem, hbm = pl.BlockSpec(memory_space=pltpu.VMEM), pl.BlockSpec(memory_space=pl.ANY)
    return pl.pallas_call(
        layer_kernel,
        name="layer",
        out_shape=(
            jax.ShapeDtypeStruct((tokens, columns), f32),
            jax.ShapeDtypeStruct((16, 8, 128), f32),
        ),
        in_specs=[vmem] * 6 + [hbm] * 3,
        out_specs=(hbm, vmem),
        scratch_shapes=[
            pltpu.VMEM((2, 2, 4, 4, 4, 16, HALF), bf16),
            pltpu.VMEM((features, columns), bf16),
            pltpu.VMEM((tokens, columns), f32),
            pltpu.VMEM((16, 8, 128), f32),
            pltpu.VMEM((16, 8, 128), f32),
            pltpu.VMEM((16, 8, 128), f32),
            pltpu.VMEM((8, 128), f32),
            pltpu.VMEM((8, 128), f32),
            dma, dma((PIECES,)),
            dma((16,)), dma((16,)), dma((17,)), dma((17,)),
            dma((16,)), dma((16,)), dma((16,)), dma((16,)), dma((16,)), dma((16,)),
            pltpu.VMEM((features, inner), bf16),
            pltpu.VMEM((inner, features), bf16),
            dma((2,)),
            pltpu.VMEM((2, 8, features + 128), f32),
            pltpu.VMEM((16, 16, 256), bf16),
            pltpu.VMEM((16, 16, 256), bf16),
            pltpu.VMEM((2, 8, 64, HALF), bf16),
            pltpu.VMEM((4, 128, inner), bf16),
            pltpu.VMEM((4, 128, HALF), bf16),
            pltpu.VMEM((4, 128, HALF), bf16),
            pltpu.VMEM((4, 128, HALF), f32),
            pltpu.VMEM((8, 64, HALF), bf16),
            pltpu.VMEM((8, 64, HALF), bf16),
            pltpu.VMEM((16, 16, 256), bf16),
            pltpu.VMEM((16, 16, 256), bf16),
            pltpu.VMEM((2, 16, 128), f32),
            dma, dma, dma((16,)), dma((16,)), dma((8,)), dma((8,)), dma((8,)), dma((8,)),
            dma((4,)), dma((4,)), dma((8,)), dma((8,)), dma((16,)), dma((16,)), dma, dma,
        ],
        compiler_params=pltpu.CompilerParams(
            collective_id=1, has_side_effects=True, vmem_limit_bytes=56 * 1024 * 1024
        ),
    )(hidden, routes, gates, gain, final_gain, targets, weight_in, weight_out, weight)


def finish_kernel(logits_ref, norms_ref, lengths_ref, probs_ref, head_ref, loss_ref):
    values = logits_ref[...]
    head_ref[...] = values.astype(jnp.bfloat16)
    shift = jnp.transpose(jnp.broadcast_to(norms_ref[0, 0:1, :], (128, 128)))
    for tile in range(values.shape[1] // 128):
        lanes = slice(tile * 128, (tile + 1) * 128)
        probs_ref[:, lanes] = (values[:, lanes] - shift).astype(jnp.bfloat16)

    position = lax.broadcasted_iota(jnp.int32, (1, 128), 1)
    group = pl.program_id(0)
    loss_ref[pl.ds(group, 1), :] = jnp.where(position < lengths_ref[group], norms_ref[0, 1:2, :], 0.0)


def finish(logits, norms, lengths):
    tokens, columns = logits.shape
    groups = tokens // TGT
    rows = pl.BlockSpec((TGT, columns), lambda i: (i, 0))
    return pl.pallas_call(
        finish_kernel,
        name="finish",
        grid=(groups,),
        out_shape=(
            jax.ShapeDtypeStruct((tokens, columns), jnp.bfloat16),
            jax.ShapeDtypeStruct((tokens, columns), jnp.bfloat16),
            jax.ShapeDtypeStruct((groups, TGT), jnp.float32),
        ),
        in_specs=[
            rows,
            pl.BlockSpec((1, 8, 128), lambda i: (i, 0, 0)),
            pl.BlockSpec(memory_space=pltpu.SMEM),
        ],
        out_specs=(rows, rows, pl.BlockSpec((groups, TGT), lambda i: (0, 0))),
    )(logits, norms, lengths)


def on_device(
    hidden, routes, gates, targets, target_lengths, moe_gain, fc_in, fc_out, final_gain, head_weight
):
    wanted = targets.astype(jnp.float32).reshape(-1, TGT)
    logits, norms = layer(
        hidden, routes, gates, moe_gain[None], final_gain[None], wanted, fc_in, fc_out, head_weight
    )
    log_probs, head_logits, loss = finish(logits, norms, target_lengths)
    return (log_probs, head_logits, loss.reshape(-1))


def solution(mesh):
    return jax.shard_map(
        on_device,
        mesh=mesh,
        in_specs=(
            P(("section", "expert"), None),
            P(("section", "expert"), None),
            P(("section", "expert"), None),
            P(),
            P(),
            P(),
            P("expert", None, "section"),
            P("expert", "section", None),
            P(),
            P(None, ("section", "expert")),
        ),
        out_specs=(P(None, ("section", "expert")), P(None, ("section", "expert")), P()),
        check_vma=False,
    )
```

```python
import jax
import jax.numpy as jnp
from jax import lax
from jax.experimental import pallas as pl
from jax.experimental.pallas import tpu as pltpu
from jax.sharding import PartitionSpec as P

TGT = 128
MESH = pl.DeviceIdType.MESH
HALF = 1024
PIECES = 8
QUARTERS = 4
FINISH = 4


class Place:
    def __init__(self):
        self.s = lax.axis_index("section")
        self.e = lax.axis_index("expert")
        self.core = lax.rem(self.s, 2)
        self.y = lax.rem(lax.div(self.s, 2), 4)
        self.zl = lax.div(self.s, 8)
        self.x = lax.div(self.e, 4)
        self.zh = lax.rem(self.e, 4)
        self.z = self.zh * 2 + self.zl
        self.sibling = (self.s + 1 - 2 * self.core, self.e)

    def at(self, axis):
        return {"x": self.x, "y": self.y, "z": self.z}[axis]

    def beside(self, axis, step):
        x, y, z = self.x, self.y, self.z
        if axis == "x":
            x = lax.rem(x + step + 4, 4)
        elif axis == "y":
            y = lax.rem(y + step + 4, 4)
        else:
            z = lax.rem(z + step + 8, 8)
        return ((lax.rem(z, 2) * 4 + y) * 2 + self.core, x * 4 + lax.div(z, 2))


def remote(src, dst, send, recv, to):
    return pltpu.make_async_remote_copy(
        src_ref=src, dst_ref=dst, send_sem=send, recv_sem=recv, device_id=to, device_id_type=MESH
    )


class Wires:
    def __init__(self, send, recv):
        self.send, self.recv, self.sent = send, recv, []

    def push(self, src, dst, to):
        k = len(self.sent)
        copy = remote(src, dst, self.send.at[k], self.recv.at[k], to)
        copy.start()
        self.sent.append(copy)
        return k

    def pull(self, k, landed, origin):
        remote(landed, landed, self.send.at[k], self.recv.at[k], origin).wait_recv()

    def drain(self):
        for copy in self.sent:
            copy.wait_send()


class Shared:
    def __init__(self, where, wires):
        self.where, self.wires, self.blocks = where, wires, []

    def push(self, block):
        mine = block(self.where.core)
        self.blocks.append((self.wires.push(mine, mine, self.where.sibling), block))

    def pull(self):
        for k, block in self.blocks:
            self.wires.pull(k, block(1 - self.where.core), self.where.sibling)


def straight(where, wires, axis, n, block):
    me = where.at(axis)
    mine = block(where.core, me)
    numbers = [wires.push(mine, mine, where.beside(axis, i)) for i in range(1, n)]
    yield
    for i, k in enumerate(numbers, 1):
        wires.pull(k, block(where.core, lax.rem(me - i + n, n)), where.beside(axis, -i))


def ring(where, wires, axis, n, block, shared=None):
    me = where.at(axis)
    for step in range(1, n // 2 + 1):
        numbers = []
        for side, sign in ((0, 1), (1, -1)):
            part = side if step == n // 2 else None
            mine = block(where.core, lax.rem(me - sign * (step - 1) + n, n), part)
            numbers.append(wires.push(mine, mine, where.beside(axis, sign)))
        yield
        for side, sign in ((0, 1), (1, -1)):
            part = side if step == n // 2 else None
            pos = lax.rem(me - sign * step + n, n)
            wires.pull(numbers[side], block(where.core, pos, part), where.beside(axis, -sign))
            if shared is not None:
                shared.push(lambda core, pos=pos, part=part: block(core, pos, part))


def together(*chains):
    chains = list(chains)
    while chains:
        chains = [chain for chain in chains if next(chain, chain) is not chain]


def some(part, size):
    return slice(None) if part is None else pl.ds(part * size, size)


def gather(where, g, ring_send, ring_recv, pair_send, pair_recv):
    wires, shared = Wires(ring_send, ring_recv), Shared(where, Wires(pair_send, pair_recv))
    x, y, zl, zh = where.x, where.y, where.zl, where.zh
    one, two, three, both = pl.ds(0, 384), pl.ds(384, 384), pl.ds(768, 256), pl.ds(384, 640)

    def plane(core, pos, part=None):
        return g.at[core, lax.rem(pos, 2), some(part, 2), :, lax.div(pos, 2), :, one]

    def along_x(core, pos, part=None):
        return g.at[core, some(part, 1), :, pos, :, :, two]

    def along_y(core, pos, part=None):
        return g.at[core, some(part, 1), pos, :, :, :, three]

    def z_last():
        yield from straight(where, wires, "x", 4, lambda core, pos: g.at[core, zl, y, pos, zh, :, one])
        yield from straight(where, wires, "y", 4, lambda core, pos: g.at[core, zl, pos, :, zh, :, one])
        shared.push(lambda core: plane(core, where.z))
        yield from ring(where, wires, "z", 8, plane, shared)

    def z_first():
        return straight(
            where, wires, "z", 8, lambda core, pos: g.at[core, lax.rem(pos, 2), y, x, lax.div(pos, 2), :, both]
        )

    def x_last():
        yield from ring(
            where, wires, "y", 4, lambda core, pos, part: g.at[core, some(part, 1), pos, x, :, :, two]
        )
        shared.push(lambda core: along_x(core, x))
        yield from ring(where, wires, "x", 4, along_x, shared)

    def y_last():
        yield from ring(
            where, wires, "x", 4, lambda core, pos, part: g.at[core, some(part, 1), y, pos, :, :, three]
        )
        shared.push(lambda core: along_y(core, y))
        yield from ring(where, wires, "y", 4, along_y, shared)

    def z_split():
        yield from z_first()
        chains = [x_last(), y_last()]
        while chains:
            chains = [chain for chain in chains if next(chain, chain) is not chain]
            yield

    together(z_last(), z_split())
    shared.pull()
    wires.drain()
    shared.wires.drain()


def spread_rows(where, rows, ring_send, ring_recv, pair_send, pair_recv):
    wires, shared = Wires(ring_send, ring_recv), Shared(where, Wires(pair_send, pair_recv))
    y, zl = where.y, where.zl
    low, high = pl.ds(0, HALF // 2), pl.ds(HALF // 2, HALF // 2)
    facing = ((((1 - zl) * 4 + y) * 2 + where.core), where.e)

    def swap(block):
        mine = block(where.core, zl)
        k = wires.push(mine, mine, facing)
        yield
        wires.pull(k, block(where.core, 1 - zl), facing)

    def z_last():
        block = lambda core, side: rows.at[core, :, side, :, low]
        yield from ring(
            where, wires, "y", 4, lambda core, pos, part: rows.at[core, pos, zl, some(part, 32), low]
        )
        shared.push(lambda core: block(core, zl))
        yield from swap(block)
        shared.push(lambda core: block(core, 1 - zl))

    def y_last():
        block = lambda core, pos, part=None: rows.at[core, pos, some(part, 1), :, high]
        yield from swap(lambda core, side: rows.at[core, y, side, :, high])
        shared.push(lambda core: block(core, y))
        yield from ring(where, wires, "y", 4, block, shared)

    together(z_last(), y_last())
    shared.pull()
    return wires, shared.wires


def exchange(n, me, to, src, dst, send, recv):
    def each(i, _):
        other = lax.rem(me + i, n)
        remote(src(other), dst.at[me], send.at[i], recv.at[i], to(other)).start()
        return 0

    lax.fori_loop(1, n, each, 0)

    def done(i, _):
        origin = lax.rem(me - i + n, n)
        copy = remote(src(origin), dst.at[origin], send.at[i], recv.at[i], to(origin))
        copy.wait_recv()
        copy.wait_send()
        return 0

    lax.fori_loop(1, n, done, 0)


def merge(stats):
    high = stats[:, 0:1, :]
    top = jnp.max(high, axis=0)
    total = jnp.sum(stats[:, 1:2, :] * jnp.exp(high - top[None]), axis=0)
    return top, total, jnp.sum(stats[:, 2:3, :], axis=0)


def rows8(first, second, third):
    row = lax.broadcasted_iota(jnp.int32, (8, 128), 0)
    zero = jnp.zeros((8, 128), jnp.float32)
    out = jnp.where(row == 0, first, zero)
    out = jnp.where(row == 1, second, out)
    return jnp.where(row == 2, third, out)


def one_hot(table, tokens):
    shape = (tokens, 256)
    column = lax.broadcasted_iota(jnp.int32, shape, 1)
    token = lax.broadcasted_iota(jnp.int32, shape, 0)
    expert = lax.div(column, 16).astype(jnp.float32)
    slot = lax.rem(lax.div(column, 4), 2).astype(jnp.float32)
    same = lax.rem(lax.div(column, 8), 2) == lax.div(token, 8)
    piece = lax.rem(column, 4)
    hits = [jnp.where(table[:, k : k + 1] == expert, 1.0, 0.0) for k in (0, 1)]
    later = lax.broadcasted_iota(jnp.int32, (tokens, tokens), 0)
    sooner = lax.broadcasted_iota(jnp.int32, (tokens, tokens), 1)
    before = jnp.where((sooner < later) & (lax.div(sooner, 8) == lax.div(later, 8)), 1.0, 0.0)
    earlier = jnp.dot(
        before.astype(jnp.bfloat16), (hits[0] + hits[1]).astype(jnp.bfloat16), preferred_element_type=jnp.float32
    )
    placed = [jnp.where(same & (earlier == slot), hit, 0.0) for hit in hits]
    return [
        jnp.concatenate([jnp.where(piece == j, one, 0.0) for j in range(QUARTERS)], axis=0) for one in placed
    ]


def stack(values):
    return jnp.concatenate([values[:, j * 256 : (j + 1) * 256] for j in range(QUARTERS)], axis=0)


def experts(
    where, hidden_ref, routes_ref, gates_ref, gain_ref, final_gain_ref, weight_in, weight_out, loads, g,
    pack, outgoing, incoming, rows, units, away, sent_half, near, summed, parts, returning, returned, spread,
    pack_send, pack_recv, go_send, go_recv, row_send, row_recv, rowp_send, rowp_recv, half_send, half_recv,
    sum_send, sum_recv, back_send, back_recv, ln_send, ln_recv,
):
    core, m = where.core, where.y * 2 + where.zl
    mine = pl.ds(pl.multiple_of(core * HALF, HALF), HALF)
    theirs = pl.ds(pl.multiple_of((1 - core) * HALF, HALF), HALF)
    to_expert = lambda other: (where.s, other)
    to_chip = lambda other: ((lax.rem(other, 2) * 4 + lax.div(other, 2)) * 2 + core, where.e)
    features = 2 * HALF

    lane = lax.broadcasted_iota(jnp.int32, (8, 128), 1)
    same = lax.broadcasted_iota(jnp.int32, (8, 8), 0) == lax.broadcasted_iota(jnp.int32, (8, 8), 1)
    table = jnp.zeros((8, 128), jnp.float32)
    for place, (source, k) in enumerate(((routes_ref, 0), (routes_ref, 1), (gates_ref, 0), (gates_ref, 1))):
        row = source[k : k + 1, :].astype(jnp.float32)
        column = jnp.sum(jnp.where(same, row, 0.0), axis=1, keepdims=True)
        table = jnp.where(lane == place, column, table)
    pack[core, :, 0:features] = hidden_ref[...].astype(jnp.float32)
    pack[core, :, features:] = table
    swap = remote(pack.at[core], pack.at[core], pack_send, pack_recv, where.sibling)
    swap.start()
    swap.wait()

    tokens = 16
    whole = pack[:, :, 0:features].reshape(tokens, features)
    table = pack[:, :, features:].reshape(tokens, 128)
    average = jnp.mean(whole, axis=-1, keepdims=True)
    centered = whole - average
    spread_of = jnp.mean(centered * centered, axis=-1, keepdims=True)
    residual = pack[:, :, mine].reshape(tokens, HALF)
    normed = ((residual - average) * lax.rsqrt(spread_of + 1e-05) * gain_ref[:, mine]).astype(jnp.bfloat16)
    chosen = one_hot(table, tokens)
    place = jnp.transpose(chosen[0] + chosen[1]).astype(jnp.bfloat16)
    slots = jnp.dot(place, stack(normed), preferred_element_type=jnp.float32).astype(jnp.bfloat16)
    outgoing[...] = slots.reshape(16, 16, 256)
    incoming[where.e] = outgoing[where.e]
    exchange(16, where.e, to_expert, lambda other: outgoing.at[other], incoming, go_send, go_recv)

    down = lax.broadcasted_iota(jnp.int32, (256, 256), 0)
    across = lax.broadcasted_iota(jnp.int32, (256, 256), 1)
    split = jnp.where(across == 4 * lax.rem(down, 64) + lax.div(down, 64), 1.0, 0.0).astype(jnp.bfloat16)
    join = jnp.where(down == 4 * lax.rem(across, 64) + lax.div(across, 64), 1.0, 0.0).astype(jnp.bfloat16)
    arrived = jnp.dot(split, incoming[...].reshape(256, 256), preferred_element_type=jnp.float32)
    for j in range(QUARTERS):
        rows[core, where.y, where.zl, :, j * 256 : (j + 1) * 256] = arrived[j * 64 : (j + 1) * 64].astype(jnp.bfloat16)

    wires, pairs = spread_rows(where, rows, row_send, row_recv, rowp_send, rowp_recv)
    loads[0].wait()
    loads[1].wait()

    def first(i, _):
        low = rows[0, pl.ds(i * 2, 2)].reshape(256, HALF)
        high = rows[1, pl.ds(i * 2, 2)].reshape(256, HALF)
        found = jnp.dot(low, weight_in[0:HALF], preferred_element_type=jnp.float32)
        found = found + jnp.dot(high, weight_in[HALF:], preferred_element_type=jnp.float32)
        units[pl.ds(i * 2, 2)] = jnp.maximum(found, 0.0).astype(jnp.bfloat16).reshape(2, 128, -1)
        return 0

    lax.fori_loop(0, 2, first, 0)

    def half(i, other):
        return remote(away.at[other], sent_half.at[other], half_send.at[i], half_recv.at[i], where.sibling)

    def second(i, _):
        other = lax.rem(where.y + 1 + i, 4)
        some = units[other]
        away[other] = jnp.dot(some, weight_out[:, theirs], preferred_element_type=jnp.float32).astype(jnp.bfloat16)
        half(i, other).start()
        near[other] = jnp.dot(some, weight_out[:, mine], preferred_element_type=jnp.float32)
        return 0

    lax.fori_loop(0, 4, second, 0)

    def part(block, origin):
        return remote(summed.at[block], parts.at[origin], sum_send.at[block], sum_recv.at[origin], to_chip(block))

    def add(i, _):
        other = lax.rem(where.y + 1 + i, 4)
        half(i, other).wait_recv()
        total = (near[other] + sent_half[other].astype(jnp.float32)).astype(jnp.bfloat16)
        summed[pl.ds(other * 2, 2)] = total.reshape(2, 64, HALF)
        for side in (0, 1):
            block = other * 2 + side

            @pl.when(block != m)
            def _():
                part(block, m).start()

        return 0

    lax.fori_loop(0, 4, add, 0)
    parts[m] = summed[m]

    def take_part(i, _):
        origin = lax.rem(m - i + 8, 8)
        remote(summed.at[origin], parts.at[origin], sum_send.at[origin], sum_recv.at[origin], to_chip(origin)).wait_recv()
        return 0

    lax.fori_loop(1, 8, take_part, 0)
    total = parts[0].astype(jnp.float32)
    for i in range(1, 8):
        total = total + parts[i].astype(jnp.float32)
    results = jnp.dot(join, stack(total.astype(jnp.bfloat16)), preferred_element_type=jnp.float32)
    returning[...] = results.astype(jnp.bfloat16).reshape(16, 16, 256)
    returned[where.e] = returning[where.e]
    exchange(16, where.e, to_expert, lambda other: returning.at[other], returned, back_send, back_recv)

    back = returned[...].reshape(256, 256)
    mixed = [residual[:, j * 256 : (j + 1) * 256] for j in range(QUARTERS)]
    for k in (0, 1):
        found = jnp.dot(chosen[k].astype(jnp.bfloat16), back, preferred_element_type=jnp.float32)
        gate = table[:, 2 + k : 3 + k]
        mixed = [old + gate * found[j * tokens : (j + 1) * tokens] for j, old in enumerate(mixed)]
    mixed = jnp.concatenate(mixed, axis=1)
    center = jnp.mean(mixed, axis=-1, keepdims=True)
    squares = jnp.sum((mixed - center) * (mixed - center), axis=-1, keepdims=True)
    lane = lax.broadcasted_iota(jnp.int32, (tokens, 128), 1)
    spread[core] = jnp.where(lane == 0, center, jnp.where(lane == 1, squares, 0.0))
    swap = remote(spread.at[core], spread.at[core], ln_send, ln_recv, where.sibling)
    swap.start()
    swap.wait()
    centers = [spread[i, :, 0:1] for i in (0, 1)]
    average = 0.5 * (centers[0] + centers[1])
    apart = centers[0] - centers[1]
    variance = (spread[0, :, 1:2] + spread[1, :, 1:2] + apart * apart * (0.5 * HALF)) / features
    final = (mixed - average) * lax.rsqrt(variance + 1e-05) * final_gain_ref[:, mine]
    g[core, where.zl, where.y, where.x, where.zh] = final.astype(jnp.bfloat16)

    wires.drain()
    pairs.drain()

    def halves_left(i, _):
        half(i, lax.rem(where.y + 1 + i, 4)).wait_send()
        return 0

    lax.fori_loop(0, 4, halves_left, 0)

    def parts_left(i, _):
        part(lax.rem(m + i, 8), m).wait_send()
        return 0

    lax.fori_loop(1, 8, parts_left, 0)


def layer_kernel(
    hidden_ref, routes_ref, gates_ref, gain_ref, final_gain_ref, targets_ref, in_hbm, out_hbm, weight_hbm,
    logits_hbm, norms_ref,
    g, weight, logits, stats, by_group, by_section, merged, solved,
    weight_sem, out_sem, ring_send, ring_recv, pair_send, pair_recv,
    one_send, one_recv, two_send, two_recv, three_send, three_recv,
    weight_in, weight_out, weight_sems, *scratch,
):
    where = Place()
    barrier = pltpu.get_barrier_semaphore()
    load = pltpu.make_async_copy(weight_hbm, weight, weight_sem)
    loads = [
        pltpu.make_async_copy(in_hbm.at[0], weight_in, weight_sems.at[0]),
        pltpu.make_async_copy(out_hbm.at[0], weight_out, weight_sems.at[1]),
    ]
    for one in loads:
        one.start()
    load.start()

    def greet(i, _):
        pl.semaphore_signal(
            barrier, inc=1, device_id=(lax.rem(where.s + i, 16), where.e), device_id_type=MESH
        )
        pl.semaphore_signal(
            barrier, inc=1, device_id=(where.s, lax.rem(where.e + i, 16)), device_id_type=MESH
        )
        return 0

    lax.fori_loop(1, 16, greet, 0)
    for step in (1, -1):
        pl.semaphore_signal(barrier, inc=1, device_id=where.beside("z", step), device_id_type=MESH)
    pl.semaphore_wait(barrier, 32)

    experts(
        where, hidden_ref, routes_ref, gates_ref, gain_ref, final_gain_ref, weight_in, weight_out, loads, g, *scratch
    )
    gather(where, g, ring_send, ring_recv, pair_send, pair_recv)
    load.wait()
    columns = weight.shape[1]
    offset = (where.s * 16 + where.e) * columns
    lane = lax.broadcasted_iota(jnp.int32, (128, 128), 1)

    def chunk(i, _):
        zl, y = lax.div(i, 4), lax.rem(i, 4)
        low = g[0, zl, y].reshape(256, HALF)
        high = g[1, zl, y].reshape(256, HALF)
        found = jnp.dot(low, weight[0:HALF], preferred_element_type=jnp.float32)
        found = found + jnp.dot(high, weight[HALF:], preferred_element_type=jnp.float32)
        found = found.reshape(16, 2, 8, columns)
        for core in (0, 1):
            group = i * 2 + core
            part = found[:, core].reshape(128, columns)
            logits[pl.ds(group * 128, 128), :] = part
            top = jnp.max(part, axis=1, keepdims=True)
            total = jnp.sum(jnp.exp(part - top), axis=1, keepdims=True)
            wanted = jnp.transpose(jnp.broadcast_to(targets_ref[pl.ds(group, 1), :].astype(jnp.float32), (128, 128)))
            picked = jnp.zeros((128, 128), jnp.float32)
            for tile in range(columns // 128):
                ids = (lane + (offset + tile * 128)).astype(jnp.float32)
                picked = picked + jnp.where(ids == wanted, part[:, tile * 128 : (tile + 1) * 128], 0.0)
            picked = jnp.sum(picked, axis=1, keepdims=True)
            table = jnp.where(lane == 0, top, jnp.where(lane == 1, total, jnp.where(lane == 2, picked, 0.0)))
            stats[group] = jnp.transpose(table)[0:8]
        pltpu.make_async_copy(
            logits.at[pl.ds(i * 256, 256)], logits_hbm.at[pl.ds(i * 256, 256)], out_sem.at[i]
        ).start()
        return 0

    lax.fori_loop(0, PIECES, chunk, 0)

    to_expert = lambda other: (where.s, other)
    to_section = lambda other: (other, where.e)
    by_group[where.e] = stats[where.e]
    exchange(16, where.e, to_expert, lambda other: stats.at[other], by_group, one_send, one_recv)
    merged[...] = rows8(*merge(by_group[...]))
    by_section[where.s] = merged[...]
    exchange(16, where.s, to_section, lambda other: merged, by_section, two_send, two_recv)
    top, total, picked = merge(by_section[...])
    log_norm = top + jnp.log(total)
    solved[...] = rows8(log_norm, log_norm - picked, jnp.zeros_like(picked))
    norms_ref[where.e] = solved[...]
    exchange(16, where.e, to_expert, lambda other: solved, norms_ref, three_send, three_recv)

    def stored(i, _):
        pltpu.make_async_copy(
            logits.at[pl.ds(i * 256, 256)], logits_hbm.at[pl.ds(i * 256, 256)], out_sem.at[i]
        ).wait()
        return 0

    lax.fori_loop(0, PIECES, stored, 0)


def layer(hidden, routes, gates, gain, final_gain, targets, weight_in, weight_out, weight):
    features, columns = weight.shape
    tokens = targets.size
    inner = weight_in.shape[2]
    dma = pltpu.SemaphoreType.DMA
    bf16, f32 = jnp.bfloat16, jnp.float32
    vmem, hbm = pl.BlockSpec(memory_space=pltpu.VMEM), pl.BlockSpec(memory_space=pl.ANY)
    return pl.pallas_call(
        layer_kernel,
        name="layer",
        out_shape=(
            jax.ShapeDtypeStruct((tokens, columns), f32),
            jax.ShapeDtypeStruct((16, 8, 128), f32),
        ),
        in_specs=[vmem] * 6 + [hbm] * 3,
        out_specs=(hbm, vmem),
        scratch_shapes=[
            pltpu.VMEM((2, 2, 4, 4, 4, 16, HALF), bf16),
            pltpu.VMEM((features, columns), bf16),
            pltpu.VMEM((tokens, columns), f32),
            pltpu.VMEM((16, 8, 128), f32),
            pltpu.VMEM((16, 8, 128), f32),
            pltpu.VMEM((16, 8, 128), f32),
            pltpu.VMEM((8, 128), f32),
            pltpu.VMEM((8, 128), f32),
            dma, dma((PIECES,)),
            dma((37,)), dma((37,)), dma((19,)), dma((19,)),
            dma((16,)), dma((16,)), dma((16,)), dma((16,)), dma((16,)), dma((16,)),
            pltpu.VMEM((features, inner), bf16),
            pltpu.VMEM((inner, features), bf16),
            dma((2,)),
            pltpu.VMEM((2, 8, features + 128), f32),
            pltpu.VMEM((16, 16, 256), bf16),
            pltpu.VMEM((16, 16, 256), bf16),
            pltpu.VMEM((2, 4, 2, 64, HALF), bf16),
            pltpu.VMEM((4, 128, inner), bf16),
            pltpu.VMEM((4, 128, HALF), bf16),
            pltpu.VMEM((4, 128, HALF), bf16),
            pltpu.VMEM((4, 128, HALF), f32),
            pltpu.VMEM((8, 64, HALF), bf16),
            pltpu.VMEM((8, 64, HALF), bf16),
            pltpu.VMEM((16, 16, 256), bf16),
            pltpu.VMEM((16, 16, 256), bf16),
            pltpu.VMEM((2, 16, 128), f32),
            dma, dma, dma((16,)), dma((16,)), dma((10,)), dma((10,)), dma((7,)), dma((7,)),
            dma((4,)), dma((4,)), dma((8,)), dma((8,)), dma((16,)), dma((16,)), dma, dma,
        ],
        compiler_params=pltpu.CompilerParams(
            collective_id=1, has_side_effects=True, vmem_limit_bytes=56 * 1024 * 1024
        ),
    )(hidden, routes, gates, gain, final_gain, targets, weight_in, weight_out, weight)


def finish_kernel(logits_ref, norms_ref, lengths_ref, probs_ref, head_ref, loss_ref):
    step = pl.program_id(0)
    position = lax.broadcasted_iota(jnp.int32, (1, TGT), 1)
    for i in range(FINISH):
        rows = slice(i * TGT, (i + 1) * TGT)
        shift = jnp.transpose(jnp.broadcast_to(norms_ref[i, 0:1, :], (TGT, TGT)))
        for tile in range(logits_ref.shape[1] // TGT):
            lanes = slice(tile * TGT, (tile + 1) * TGT)
            values = logits_ref[rows, lanes]
            head_ref[rows, lanes] = values.astype(jnp.bfloat16)
            probs_ref[rows, lanes] = (values - shift).astype(jnp.bfloat16)
        group = step * FINISH + i
        loss_ref[pl.ds(group, 1), :] = jnp.where(position < lengths_ref[group], norms_ref[i, 1:2, :], 0.0)


def finish(logits, norms, lengths):
    tokens, columns = logits.shape
    groups = tokens // TGT
    rows = pl.BlockSpec((FINISH * TGT, columns), lambda i: (i, 0))
    return pl.pallas_call(
        finish_kernel,
        name="finish",
        grid=(groups // FINISH,),
        out_shape=(
            jax.ShapeDtypeStruct((tokens, columns), jnp.bfloat16),
            jax.ShapeDtypeStruct((tokens, columns), jnp.bfloat16),
            jax.ShapeDtypeStruct((groups, TGT), jnp.float32),
        ),
        in_specs=[
            rows,
            pl.BlockSpec((FINISH, 8, 128), lambda i: (i, 0, 0)),
            pl.BlockSpec(memory_space=pltpu.SMEM),
        ],
        out_specs=(rows, rows, pl.BlockSpec((groups, TGT), lambda i: (0, 0))),
    )(logits, norms, lengths)


def on_device(
    hidden, routes, gates, targets, target_lengths, moe_gain, fc_in, fc_out, final_gain, head_weight
):
    wanted = targets.reshape(-1, TGT)
    logits, norms = layer(
        hidden, routes.T, gates.T, moe_gain[None], final_gain[None], wanted, fc_in, fc_out, head_weight
    )
    log_probs, head_logits, loss = finish(logits, norms, target_lengths)
    return (log_probs, head_logits, loss.reshape(-1))


def solution(mesh):
    return jax.shard_map(
        on_device,
        mesh=mesh,
        in_specs=(
            P(("section", "expert"), None),
            P(("section", "expert"), None),
            P(("section", "expert"), None),
            P(),
            P(),
            P(),
            P("expert", None, "section"),
            P("expert", "section", None),
            P(),
            P(None, ("section", "expert")),
        ),
        out_specs=(P(None, ("section", "expert")), P(None, ("section", "expert")), P()),
        check_vma=False,
    )
```

```python
import jax
import jax.numpy as jnp
from jax import lax
from jax.experimental import pallas as pl
from jax.experimental.pallas import tpu as pltpu
from jax.sharding import PartitionSpec as P

TGT = 128
MESH = pl.DeviceIdType.MESH
HALF = 1024
PIECES = 8
QUARTERS = 4


class Place:
    def __init__(self):
        self.s = lax.axis_index("section")
        self.e = lax.axis_index("expert")
        self.core = lax.rem(self.s, 2)
        self.y = lax.rem(lax.div(self.s, 2), 4)
        self.zl = lax.div(self.s, 8)
        self.x = lax.div(self.e, 4)
        self.zh = lax.rem(self.e, 4)
        self.z = self.zh * 2 + self.zl
        self.sibling = (self.s + 1 - 2 * self.core, self.e)

    def at(self, axis):
        return {"x": self.x, "y": self.y, "z": self.z}[axis]

    def beside(self, axis, step):
        x, y, z = self.x, self.y, self.z
        if axis == "x":
            x = lax.rem(x + step + 4, 4)
        elif axis == "y":
            y = lax.rem(y + step + 4, 4)
        else:
            z = lax.rem(z + step + 8, 8)
        return ((lax.rem(z, 2) * 4 + y) * 2 + self.core, x * 4 + lax.div(z, 2))


def remote(src, dst, send, recv, to):
    return pltpu.make_async_remote_copy(
        src_ref=src, dst_ref=dst, send_sem=send, recv_sem=recv, device_id=to, device_id_type=MESH
    )


class Wires:
    def __init__(self, send, recv):
        self.send, self.recv, self.sent = send, recv, []

    def push(self, src, dst, to):
        k = len(self.sent)
        copy = remote(src, dst, self.send.at[k], self.recv.at[k], to)
        copy.start()
        self.sent.append(copy)
        return k

    def pull(self, k, landed, origin):
        remote(landed, landed, self.send.at[k], self.recv.at[k], origin).wait_recv()

    def drain(self):
        for copy in self.sent:
            copy.wait_send()


class Shared:
    def __init__(self, where, wires):
        self.where, self.wires, self.blocks = where, wires, []

    def push(self, block):
        mine = block(self.where.core)
        self.blocks.append((self.wires.push(mine, mine, self.where.sibling), block))

    def pull(self):
        for k, block in self.blocks:
            self.wires.pull(k, block(1 - self.where.core), self.where.sibling)
        self.blocks = []


def straight(where, wires, axis, n, block):
    me = where.at(axis)
    mine = block(where.core, me)
    numbers = [wires.push(mine, mine, where.beside(axis, i)) for i in range(1, n)]
    yield
    for i, k in enumerate(numbers, 1):
        wires.pull(k, block(where.core, lax.rem(me - i + n, n)), where.beside(axis, -i))


def ring(where, wires, axis, n, block, shared=None):
    me = where.at(axis)
    for step in range(1, n // 2 + 1):
        numbers = []
        for side, sign in ((0, 1), (1, -1)):
            part = side if step == n // 2 else None
            mine = block(where.core, lax.rem(me - sign * (step - 1) + n, n), part)
            numbers.append(wires.push(mine, mine, where.beside(axis, sign)))
        yield
        for side, sign in ((0, 1), (1, -1)):
            part = side if step == n // 2 else None
            pos = lax.rem(me - sign * step + n, n)
            wires.pull(numbers[side], block(where.core, pos, part), where.beside(axis, -sign))
            if shared is not None:
                shared.push(lambda core, pos=pos, part=part: block(core, pos, part))


def together(*chains):
    chains = list(chains)
    while chains:
        chains = [chain for chain in chains if next(chain, chain) is not chain]


def some(part, size):
    return slice(None) if part is None else pl.ds(part * size, size)


def planes(where, wires, block, shared):
    me = where.z
    numbers = []
    mine = block(where.core, me)
    for step in (1, -1, 2, -2):
        numbers.append((wires.push(mine, mine, where.beside("z", step)), step))
    yield
    for k, step in numbers:
        pos = lax.rem(me - step + 8, 8)
        wires.pull(k, block(where.core, pos), where.beside("z", -step))
        shared.push(lambda core, pos=pos: block(core, pos))
    numbers = []
    for side, sign in ((0, 1), (1, -1)):
        pos = lax.rem(me - 2 * sign + 8, 8)
        for step, part in ((sign, None), (2 * sign, side)):
            mine = block(where.core, pos, part)
            numbers.append((wires.push(mine, mine, where.beside("z", step)), step, sign, part))
    yield
    for k, step, sign, part in numbers:
        pos = lax.rem(me - step - 2 * sign + 8, 8)
        wires.pull(k, block(where.core, pos, part), where.beside("z", -step))
        shared.push(lambda core, pos=pos, part=part: block(core, pos, part))


def gather(where, g, weight, logits, ring_send, ring_recv, pair_send, pair_recv):
    wires, shared = Wires(ring_send, ring_recv), Shared(where, Wires(pair_send, pair_recv))
    x, y, zl, zh = where.x, where.y, where.zl, where.zh
    one, two, three, rest = (0, 256), (256, 384), (640, 384), (256, 768)

    def z_last(half):
        def block(core, pos, part=None):
            return g.at[
                core, lax.rem(pos, 2), pl.ds(2 * half, 2), some(part, 2), lax.div(pos, 2), :, pl.ds(*one)
            ]

        shared.push(lambda core: block(core, where.z))
        yield from planes(where, wires, block, shared)

    def x_last(half):
        def block(core, pos, part=None):
            return g.at[core, half, some(part, 2), pos, :, :, pl.ds(*two)]

        yield from straight(where, wires, "y", 4, lambda core, pos: g.at[core, half, pos, x, :, :, pl.ds(*two)])
        shared.push(lambda core: block(core, x))
        yield from ring(where, wires, "x", 4, block, shared)

    def y_last(half):
        def block(core, pos, part=None):
            return g.at[core, half, pos, some(part, 2), :, :, pl.ds(*three)]

        yield from straight(where, wires, "x", 4, lambda core, pos: g.at[core, half, y, pos, :, :, pl.ds(*three)])
        shared.push(lambda core: block(core, y))
        yield from ring(where, wires, "y", 4, block, shared)

    def multiply(at, lanes):
        start, width = lanes
        total = logits[at]
        shape = total.shape
        total = total.reshape(256, shape[-1])
        for core in (0, 1):
            rows = g[(core, *at, slice(None), pl.ds(start, width))].reshape(256, width)
            columns = weight[core * HALF + start : core * HALF + start + width]
            total = total + jnp.dot(rows, columns, preferred_element_type=jnp.float32)
        logits[at] = total.reshape(shape)

    def over_planes(count, step):
        def body(i, _):
            pos = lax.rem(where.z + step(i), 8)
            multiply((lax.rem(pos, 2), slice(None), slice(None), lax.div(pos, 2)), one)
            return 0

        lax.fori_loop(0, count, body, 0)

    def over_slabs(count, step):
        def body(i, _):
            side, ahead = lax.rem(i, 2), step(lax.div(i, 2))
            multiply((side, slice(None), lax.rem(x + ahead, 4), slice(None)), two)
            multiply((side, lax.rem(y + ahead, 4), slice(None), slice(None)), three)
            return 0

        lax.fori_loop(0, 2 * count, body, 0)

    def advance(chains):
        for chain in chains:
            next(chain, None)

    by_x = straight(where, wires, "x", 4, lambda core, pos: g.at[core, zl, y, pos, zh, :, pl.ds(*one)])
    by_y = straight(where, wires, "y", 4, lambda core, pos: g.at[core, zl, pos, :, zh, :, pl.ds(*one)])
    by_z = straight(
        where, wires, "z", 8, lambda core, pos: g.at[core, lax.rem(pos, 2), y, x, lax.div(pos, 2), :, pl.ds(*rest)]
    )
    early, late = [x_last(0), y_last(0)], [x_last(1), y_last(1)]
    advance([by_x, by_z])
    logits[...] = jnp.zeros_like(logits)
    advance([by_x, by_y, by_z] + early + late)
    advance([by_y])
    early, late = [z_last(0)] + early, [z_last(1)] + late
    advance(early + late)
    shared.pull()
    over_planes(1, lambda i: 0)
    over_slabs(1, lambda i: 0)
    advance(early + late)
    shared.pull()
    over_planes(4, lambda i: i + 1 + 3 * lax.div(i, 2))
    over_slabs(2, lambda i: 2 * i + 1)
    advance(early + late)
    shared.pull()
    over_planes(3, lambda i: i + 3)
    over_slabs(1, lambda i: 2)
    wires.drain()
    shared.wires.drain()


def spread_rows(where, rows, ring_send, ring_recv, pair_send, pair_recv):
    wires, shared = Wires(ring_send, ring_recv), Shared(where, Wires(pair_send, pair_recv))
    y, zl = where.y, where.zl
    low, high = pl.ds(0, HALF // 2), pl.ds(HALF // 2, HALF // 2)
    facing = ((((1 - zl) * 4 + y) * 2 + where.core), where.e)

    def swap(block):
        mine = block(where.core, zl)
        k = wires.push(mine, mine, facing)
        yield
        wires.pull(k, block(where.core, 1 - zl), facing)

    def z_last():
        block = lambda core, side: rows.at[core, :, side, :, low]
        yield from ring(
            where, wires, "y", 4, lambda core, pos, part: rows.at[core, pos, zl, some(part, 32), low]
        )
        shared.push(lambda core: block(core, zl))
        yield from swap(block)
        shared.push(lambda core: block(core, 1 - zl))

    def y_last():
        block = lambda core, pos, part=None: rows.at[core, pos, some(part, 1), :, high]
        yield from swap(lambda core, side: rows.at[core, y, side, :, high])
        shared.push(lambda core: block(core, y))
        yield from ring(where, wires, "y", 4, block, shared)

    together(z_last(), y_last())
    shared.pull()
    return wires, shared.wires


def exchange(n, me, to, src, dst, send, recv):
    def each(i, _):
        other = lax.rem(me + i, n)
        remote(src(other), dst.at[me], send.at[i], recv.at[i], to(other)).start()
        return 0

    lax.fori_loop(1, n, each, 0)

    def done(i, _):
        origin = lax.rem(me - i + n, n)
        copy = remote(src(origin), dst.at[origin], send.at[i], recv.at[i], to(origin))
        copy.wait_recv()
        copy.wait_send()
        return 0

    lax.fori_loop(1, n, done, 0)


def merge(stats):
    high = stats[:, 0:1, :]
    top = jnp.max(high, axis=0)
    total = jnp.sum(stats[:, 1:2, :] * jnp.exp(high - top[None]), axis=0)
    return top, total, jnp.sum(stats[:, 2:3, :], axis=0)


def rows8(first, second, third):
    row = lax.broadcasted_iota(jnp.int32, (8, 128), 0)
    zero = jnp.zeros((8, 128), jnp.float32)
    out = jnp.where(row == 0, first, zero)
    out = jnp.where(row == 1, second, out)
    return jnp.where(row == 2, third, out)


def one_hot(table, tokens):
    shape = (tokens, 256)
    column = lax.broadcasted_iota(jnp.int32, shape, 1)
    token = lax.broadcasted_iota(jnp.int32, shape, 0)
    expert = lax.div(column, 16).astype(jnp.float32)
    slot = lax.rem(lax.div(column, 4), 2).astype(jnp.float32)
    same = lax.rem(lax.div(column, 8), 2) == lax.div(token, 8)
    piece = lax.rem(column, 4)
    hits = [jnp.where(table[:, k : k + 1] == expert, 1.0, 0.0) for k in (0, 1)]
    later = lax.broadcasted_iota(jnp.int32, (tokens, tokens), 0)
    sooner = lax.broadcasted_iota(jnp.int32, (tokens, tokens), 1)
    before = jnp.where((sooner < later) & (lax.div(sooner, 8) == lax.div(later, 8)), 1.0, 0.0)
    earlier = jnp.dot(
        before.astype(jnp.bfloat16), (hits[0] + hits[1]).astype(jnp.bfloat16), preferred_element_type=jnp.float32
    )
    placed = [jnp.where(same & (earlier == slot), hit, 0.0) for hit in hits]
    return [
        jnp.concatenate([jnp.where(piece == j, one, 0.0) for j in range(QUARTERS)], axis=0) for one in placed
    ]


def stack(values):
    return jnp.concatenate([values[:, j * 256 : (j + 1) * 256] for j in range(QUARTERS)], axis=0)


def experts(
    where, barrier, small, late, hidden_ref, routes_ref, gates_ref, gain_ref, final_gain_ref, weight_in, weight_out, loads, g,
    local, outbox, pack, outgoing, incoming, rows, units, away, sent_half, near, summed, parts, returning, returned, spread,
    pack_send, pack_recv, go_send, go_recv, row_send, row_recv, rowp_send, rowp_recv, half_send, half_recv,
    sum_send, sum_recv, back_send, back_recv, ln_send, ln_recv,
):
    core, m = where.core, where.y * 2 + where.zl
    mine = pl.ds(pl.multiple_of(core * HALF, HALF), HALF)
    theirs = pl.ds(pl.multiple_of((1 - core) * HALF, HALF), HALF)
    to_expert = lambda other: (where.s, other)
    to_chip = lambda other: ((lax.rem(other, 2) * 4 + lax.div(other, 2)) * 2 + core, where.e)
    features = 2 * HALF

    for one in small:
        one.wait()
    lane = lax.broadcasted_iota(jnp.int32, (8, 128), 1)
    same = lax.broadcasted_iota(jnp.int32, (8, 8), 0) == lax.broadcasted_iota(jnp.int32, (8, 8), 1)
    table = jnp.zeros((8, 128), jnp.float32)
    for place, (source, k) in enumerate(((routes_ref, 0), (routes_ref, 1), (gates_ref, 0), (gates_ref, 1))):
        row = source[k : k + 1, :].astype(jnp.float32)
        column = jnp.sum(jnp.where(same, row, 0.0), axis=1, keepdims=True)
        table = jnp.where(lane == place, column, table)
    whole = hidden_ref[...].astype(jnp.float32)
    average = jnp.mean(whole, axis=-1, keepdims=True)
    centered = whole - average
    spread_of = jnp.mean(centered * centered, axis=-1, keepdims=True)
    normed = centered * lax.rsqrt(spread_of + 1e-05) * gain_ref[...]
    local[0] = normed.astype(jnp.bfloat16).astype(jnp.float32)
    local[1] = whole
    for box, half in ((outbox, theirs), (pack.at[core], mine)):
        box[:, 0:HALF] = local[0, :, half]
        box[:, HALF:features] = local[1, :, half]
        box[:, features:] = table
    pl.semaphore_wait(barrier, 32)
    swap = remote(outbox, pack.at[core], pack_send, pack_recv, where.sibling)
    swap.start()
    swap.wait()

    tokens = 16
    normed = pack[:, :, 0:HALF].reshape(tokens, HALF).astype(jnp.bfloat16)
    residual = pack[:, :, HALF:features].reshape(tokens, HALF)
    table = pack[:, :, features:].reshape(tokens, 128)
    chosen = one_hot(table, tokens)
    place = jnp.transpose(chosen[0] + chosen[1]).astype(jnp.bfloat16)
    slots = jnp.dot(place, stack(normed), preferred_element_type=jnp.float32).astype(jnp.bfloat16)
    outgoing[...] = slots.reshape(16, 16, 256)
    incoming[where.e] = outgoing[where.e]
    exchange(16, where.e, to_expert, lambda other: outgoing.at[other], incoming, go_send, go_recv)

    down = lax.broadcasted_iota(jnp.int32, (256, 256), 0)
    across = lax.broadcasted_iota(jnp.int32, (256, 256), 1)
    split = jnp.where(across == 4 * lax.rem(down, 64) + lax.div(down, 64), 1.0, 0.0).astype(jnp.bfloat16)
    join = jnp.where(down == 4 * lax.rem(across, 64) + lax.div(across, 64), 1.0, 0.0).astype(jnp.bfloat16)
    arrived = jnp.dot(split, incoming[...].reshape(256, 256), preferred_element_type=jnp.float32)
    for j in range(QUARTERS):
        rows[core, where.y, where.zl, :, j * 256 : (j + 1) * 256] = arrived[j * 64 : (j + 1) * 64].astype(jnp.bfloat16)

    wires, pairs = spread_rows(where, rows, row_send, row_recv, rowp_send, rowp_recv)
    loads[0].wait()
    loads[1].wait()

    def first(i, _):
        low = rows[0, pl.ds(i * 2, 2)].reshape(256, HALF)
        high = rows[1, pl.ds(i * 2, 2)].reshape(256, HALF)
        found = jnp.dot(low, weight_in[0:HALF], preferred_element_type=jnp.float32)
        found = found + jnp.dot(high, weight_in[HALF:], preferred_element_type=jnp.float32)
        units[pl.ds(i * 2, 2)] = jnp.maximum(found, 0.0).astype(jnp.bfloat16).reshape(2, 128, -1)
        return 0

    lax.fori_loop(0, 2, first, 0)

    def half(i, other):
        return remote(away.at[other], sent_half.at[other], half_send.at[i], half_recv.at[i], where.sibling)

    def second(i, _):
        other = lax.rem(where.y + 1 + i, 4)
        some = units[other]
        away[other] = jnp.dot(some, weight_out[:, theirs], preferred_element_type=jnp.float32).astype(jnp.bfloat16)
        half(i, other).start()
        near[other] = jnp.dot(some, weight_out[:, mine], preferred_element_type=jnp.float32)
        return 0

    lax.fori_loop(0, 4, second, 0)

    def part(block, origin):
        return remote(summed.at[block], parts.at[origin], sum_send.at[block], sum_recv.at[origin], to_chip(block))

    def add(i, _):
        other = lax.rem(where.y + 1 + i, 4)
        half(i, other).wait_recv()
        total = (near[other] + sent_half[other].astype(jnp.float32)).astype(jnp.bfloat16)
        summed[pl.ds(other * 2, 2)] = total.reshape(2, 64, HALF)
        for side in (0, 1):
            block = other * 2 + side

            @pl.when(block != m)
            def _():
                part(block, m).start()

        return 0

    lax.fori_loop(0, 4, add, 0)
    parts[m] = summed[m]

    def take_part(i, _):
        origin = lax.rem(m - i + 8, 8)
        remote(summed.at[origin], parts.at[origin], sum_send.at[origin], sum_recv.at[origin], to_chip(origin)).wait_recv()
        return 0

    lax.fori_loop(1, 8, take_part, 0)
    total = parts[0].astype(jnp.float32)
    for i in range(1, 8):
        total = total + parts[i].astype(jnp.float32)
    results = jnp.dot(join, stack(total.astype(jnp.bfloat16)), preferred_element_type=jnp.float32)
    returning[...] = results.astype(jnp.bfloat16).reshape(16, 16, 256)
    returned[where.e] = returning[where.e]
    exchange(16, where.e, to_expert, lambda other: returning.at[other], returned, back_send, back_recv)

    back = returned[...].reshape(256, 256)
    mixed = [residual[:, j * 256 : (j + 1) * 256] for j in range(QUARTERS)]
    for k in (0, 1):
        found = jnp.dot(chosen[k].astype(jnp.bfloat16), back, preferred_element_type=jnp.float32)
        gate = table[:, 2 + k : 3 + k]
        mixed = [old + gate * found[j * tokens : (j + 1) * tokens] for j, old in enumerate(mixed)]
    mixed = jnp.concatenate(mixed, axis=1)
    center = jnp.mean(mixed, axis=-1, keepdims=True)
    squares = jnp.sum((mixed - center) * (mixed - center), axis=-1, keepdims=True)
    lane = lax.broadcasted_iota(jnp.int32, (tokens, 128), 1)
    spread[core] = jnp.where(lane == 0, center, jnp.where(lane == 1, squares, 0.0))
    swap = remote(spread.at[core], spread.at[core], ln_send, ln_recv, where.sibling)
    swap.start()
    swap.wait()
    centers = [spread[i, :, 0:1] for i in (0, 1)]
    average = 0.5 * (centers[0] + centers[1])
    apart = centers[0] - centers[1]
    variance = (spread[0, :, 1:2] + spread[1, :, 1:2] + apart * apart * (0.5 * HALF)) / features
    late.wait()
    final = (mixed - average) * lax.rsqrt(variance + 1e-05) * final_gain_ref[:, mine]
    g[core, where.zl, where.y, where.x, where.zh] = final.astype(jnp.bfloat16)

    wires.drain()
    pairs.drain()

    def halves_left(i, _):
        half(i, lax.rem(where.y + 1 + i, 4)).wait_send()
        return 0

    lax.fori_loop(0, 4, halves_left, 0)

    def parts_left(i, _):
        part(lax.rem(m + i, 8), m).wait_send()
        return 0

    lax.fori_loop(1, 8, parts_left, 0)


def layer_kernel(
    hidden_hbm, routes_hbm, gates_hbm, gain_hbm, final_gain_hbm, targets_hbm, in_hbm, out_hbm, weight_hbm,
    kept, norms_ref,
    g, weight, logits, stats, by_group, by_section, merged, solved,
    weight_sem, ring_send, ring_recv, pair_send, pair_recv,
    one_send, one_recv, two_send, two_recv, three_send, three_recv,
    weight_in, weight_out, weight_sems, hidden_ref, routes_ref, gates_ref, gain_ref, final_gain_ref, targets_ref,
    small_sems, *scratch,
):
    where = Place()
    barrier = pltpu.get_barrier_semaphore()
    pairs = (
        (hidden_hbm, hidden_ref), (routes_hbm, routes_ref), (gates_hbm, gates_ref), (gain_hbm, gain_ref),
        (final_gain_hbm, final_gain_ref), (targets_hbm, targets_ref),
    )
    small = [pltpu.make_async_copy(a, b, small_sems.at[i]) for i, (a, b) in enumerate(pairs)]
    for one in small:
        one.start()
    load = pltpu.make_async_copy(weight_hbm, weight, weight_sem)
    loads = [
        pltpu.make_async_copy(in_hbm.at[0], weight_in, weight_sems.at[0]),
        pltpu.make_async_copy(out_hbm.at[0], weight_out, weight_sems.at[1]),
    ]
    for one in loads:
        one.start()
    load.start()

    def greet(i, _):
        pl.semaphore_signal(
            barrier, inc=1, device_id=(lax.rem(where.s + i, 16), where.e), device_id_type=MESH
        )
        pl.semaphore_signal(
            barrier, inc=1, device_id=(where.s, lax.rem(where.e + i, 16)), device_id_type=MESH
        )
        return 0

    lax.fori_loop(1, 16, greet, 0)
    for step in (1, -1):
        pl.semaphore_signal(barrier, inc=1, device_id=where.beside("z", step), device_id_type=MESH)

    experts(
        where, barrier, small[:4], small[4], hidden_ref, routes_ref, gates_ref, gain_ref, final_gain_ref, weight_in, weight_out,
        loads, g, *scratch
    )
    load.wait()
    small[5].wait()
    gather(where, g, weight, logits, ring_send, ring_recv, pair_send, pair_recv)

    columns = weight.shape[1]
    offset = (where.s * 16 + where.e) * columns
    lane = lax.broadcasted_iota(jnp.int32, (128, 128), 1)

    def chunk(i, _):
        zl, y = lax.div(i, 4), lax.rem(i, 4)
        for core in (0, 1):
            group = i * 2 + core
            part = logits[zl, y, :, :, core * 8 : (core + 1) * 8]
            kept[group] = part
            part = part.reshape(128, columns)
            top = jnp.max(part, axis=1, keepdims=True)
            total = jnp.sum(jnp.exp(part - top), axis=1, keepdims=True)
            wanted = jnp.transpose(
                jnp.broadcast_to(targets_ref[pl.ds(group, 1), :].astype(jnp.float32), (128, 128))
            )
            picked = jnp.zeros((128, 128), jnp.float32)
            for tile in range(columns // 128):
                ids = (lane + (offset + tile * 128)).astype(jnp.float32)
                picked = picked + jnp.where(ids == wanted, part[:, tile * 128 : (tile + 1) * 128], 0.0)
            picked = jnp.sum(picked, axis=1, keepdims=True)
            table = jnp.where(lane == 0, top, jnp.where(lane == 1, total, jnp.where(lane == 2, picked, 0.0)))
            stats[group] = jnp.transpose(table)[0:8]
        return 0

    lax.fori_loop(0, PIECES, chunk, 0)

    to_expert = lambda other: (where.s, other)
    to_section = lambda other: (other, where.e)
    by_group[where.s] = stats[where.s]
    exchange(16, where.s, to_section, lambda other: stats.at[other], by_group, one_send, one_recv)
    merged[...] = rows8(*merge(by_group[...]))
    by_section[where.e] = merged[...]
    exchange(16, where.e, to_expert, lambda other: merged, by_section, two_send, two_recv)
    top, total, picked = merge(by_section[...])
    log_norm = top + jnp.log(total)
    solved[...] = rows8(log_norm, log_norm - picked, jnp.zeros_like(picked))
    norms_ref[where.s] = solved[...]
    exchange(16, where.s, to_section, lambda other: solved, norms_ref, three_send, three_recv)


def layer(hidden, routes, gates, gain, final_gain, targets, weight_in, weight_out, weight):
    features, columns = weight.shape
    tokens = targets.size
    inner = weight_in.shape[2]
    dma = pltpu.SemaphoreType.DMA
    bf16, f32 = jnp.bfloat16, jnp.float32
    vmem = pl.BlockSpec(memory_space=pltpu.VMEM)
    operands = (hidden, routes, gates, gain, final_gain, targets, weight_in, weight_out, weight)
    return pl.pallas_call(
        layer_kernel,
        name="layer",
        out_shape=(
            pltpu.VMEM((16, 4, 4, 8, columns), f32),
            jax.ShapeDtypeStruct((16, 8, 128), f32),
        ),
        in_specs=[pl.BlockSpec(memory_space=pltpu.HBM)] * 9,
        out_specs=(vmem, vmem),
        scratch_shapes=[
            pltpu.VMEM((2, 2, 4, 4, 4, 16, HALF), bf16),
            pltpu.VMEM((features, columns), bf16),
            pltpu.VMEM((2, 4, 4, 4, 16, columns), f32),
            pltpu.VMEM((16, 8, 128), f32),
            pltpu.VMEM((16, 8, 128), f32),
            pltpu.VMEM((16, 8, 128), f32),
            pltpu.VMEM((8, 128), f32),
            pltpu.VMEM((8, 128), f32),
            dma,
            dma((57,)), dma((57,)), dma((38,)), dma((38,)),
            dma((16,)), dma((16,)), dma((16,)), dma((16,)), dma((16,)), dma((16,)),
            pltpu.VMEM((features, inner), bf16),
            pltpu.VMEM((inner, features), bf16),
            dma((2,)),
            pltpu.VMEM(hidden.shape, bf16),
            pltpu.VMEM(routes.shape, jnp.int32),
            pltpu.VMEM(gates.shape, f32),
            pltpu.VMEM(gain.shape, f32),
            pltpu.VMEM(final_gain.shape, f32),
            pltpu.VMEM(targets.shape, jnp.int32),
            dma((6,)),
            pltpu.VMEM((2, 8, features), f32),
            pltpu.VMEM((8, features + 128), f32),
            pltpu.VMEM((2, 8, features + 128), f32),
            pltpu.VMEM((16, 16, 256), bf16),
            pltpu.VMEM((16, 16, 256), bf16),
            pltpu.VMEM((2, 4, 2, 64, HALF), bf16),
            pltpu.VMEM((4, 128, inner), bf16),
            pltpu.VMEM((4, 128, HALF), bf16),
            pltpu.VMEM((4, 128, HALF), bf16),
            pltpu.VMEM((4, 128, HALF), f32),
            pltpu.VMEM((8, 64, HALF), bf16),
            pltpu.VMEM((8, 64, HALF), bf16),
            pltpu.VMEM((16, 16, 256), bf16),
            pltpu.VMEM((16, 16, 256), bf16),
            pltpu.VMEM((2, 16, 128), f32),
            dma, dma, dma((16,)), dma((16,)), dma((10,)), dma((10,)), dma((7,)), dma((7,)),
            dma((4,)), dma((4,)), dma((8,)), dma((8,)), dma((16,)), dma((16,)), dma, dma,
        ],
        compiler_params=pltpu.CompilerParams(
            collective_id=1, has_side_effects=True, vmem_limit_bytes=48 * 1024 * 1024
        ),
    )(*(pltpu.with_memory_space_constraint(one, pltpu.HBM) for one in operands))


def finish_kernel(logits_ref, norms_ref, lengths_ref, probs_hbm, head_hbm, loss_ref, probs, heads, probs_sem, head_sem):
    position = lax.broadcasted_iota(jnp.int32, (1, TGT), 1)
    groups, columns = logits_ref.shape[0], logits_ref.shape[-1]

    def copies(group):
        rows = pl.ds(group * TGT, TGT)
        return (
            pltpu.make_async_copy(probs.at[rows], probs_hbm.at[rows], probs_sem.at[group]),
            pltpu.make_async_copy(heads.at[rows], head_hbm.at[rows], head_sem.at[group]),
        )

    def each(group, _):
        rows = pl.ds(group * TGT, TGT)
        shift = jnp.transpose(jnp.broadcast_to(norms_ref[group, 0:1, :], (TGT, TGT)))
        for tile in range(columns // TGT):
            lanes = slice(tile * TGT, (tile + 1) * TGT)
            values = logits_ref[group, :, :, :, lanes].reshape(TGT, TGT)
            heads[rows, lanes] = values.astype(jnp.bfloat16)
            probs[rows, lanes] = (values - shift).astype(jnp.bfloat16)
        loss_ref[pl.ds(group, 1), :] = jnp.where(position < lengths_ref[group], norms_ref[group, 1:2, :], 0.0)
        for copy in copies(group):
            copy.start()
        return 0

    def done(group, _):
        for copy in copies(group):
            copy.wait()
        return 0

    lax.fori_loop(0, groups, each, 0)
    lax.fori_loop(0, groups, done, 0)


def finish(logits, norms, lengths):
    groups, columns = logits.shape[0], logits.shape[-1]
    tokens = groups * TGT
    vmem, hbm = pl.BlockSpec(memory_space=pltpu.VMEM), pl.BlockSpec(memory_space=pl.ANY)
    return pl.pallas_call(
        finish_kernel,
        name="finish",
        out_shape=(
            jax.ShapeDtypeStruct((tokens, columns), jnp.bfloat16),
            jax.ShapeDtypeStruct((tokens, columns), jnp.bfloat16),
            jax.ShapeDtypeStruct((groups, TGT), jnp.float32),
        ),
        in_specs=[vmem, vmem, pl.BlockSpec(memory_space=pltpu.SMEM)],
        out_specs=(hbm, hbm, vmem),
        scratch_shapes=[
            pltpu.VMEM((tokens, columns), jnp.bfloat16),
            pltpu.VMEM((tokens, columns), jnp.bfloat16),
            pltpu.SemaphoreType.DMA((groups,)),
            pltpu.SemaphoreType.DMA((groups,)),
        ],
        compiler_params=pltpu.CompilerParams(vmem_limit_bytes=24 * 1024 * 1024),
    )(pltpu.with_memory_space_constraint(logits, pltpu.VMEM), norms, lengths)


def on_device(
    hidden, routes, gates, targets, target_lengths, moe_gain, fc_in, fc_out, final_gain, head_weight
):
    wanted = targets.reshape(-1, TGT)
    logits, norms = layer(
        hidden, routes.T, gates.T, moe_gain[None], final_gain[None], wanted, fc_in, fc_out, head_weight
    )
    log_probs, head_logits, loss = finish(logits, norms, target_lengths)
    return (log_probs, head_logits, loss.reshape(-1))


def solution(mesh):
    return jax.shard_map(
        on_device,
        mesh=mesh,
        in_specs=(
            P(("section", "expert"), None),
            P(("section", "expert"), None),
            P(("section", "expert"), None),
            P(),
            P(),
            P(),
            P("expert", None, "section"),
            P("expert", "section", None),
            P(),
            P(None, ("section", "expert")),
        ),
        out_specs=(P(None, ("section", "expert")), P(None, ("section", "expert")), P()),
        check_vma=False,
    )
```

```python
import functools
import math

import jax
import jax.numpy as jnp
from jax import lax
from jax.experimental import pallas as pl
from jax.experimental.pallas import tpu as pltpu
from jax.sharding import PartitionSpec as P

TGT = 128
MESH = pl.DeviceIdType.MESH
HALF = 1024
PIECES = 8
QUARTERS = 4


class Place:
    def __init__(self):
        self.s = lax.axis_index("section")
        self.e = lax.axis_index("expert")
        self.core = lax.rem(self.s, 2)
        self.y = lax.rem(lax.div(self.s, 2), 4)
        self.zl = lax.div(self.s, 8)
        self.x = lax.div(self.e, 4)
        self.zh = lax.rem(self.e, 4)
        self.z = self.zh * 2 + self.zl
        self.sibling = (self.s + 1 - 2 * self.core, self.e)

    def at(self, axis):
        return {"x": self.x, "y": self.y, "z": self.z}[axis]

    def beside(self, axis, step):
        x, y, z = self.x, self.y, self.z
        if axis == "x":
            x = lax.rem(x + step + 4, 4)
        elif axis == "y":
            y = lax.rem(y + step + 4, 4)
        else:
            z = lax.rem(z + step + 8, 8)
        return ((lax.rem(z, 2) * 4 + y) * 2 + self.core, x * 4 + lax.div(z, 2))


def remote(src, dst, send, recv, to):
    return pltpu.make_async_remote_copy(
        src_ref=src, dst_ref=dst, send_sem=send, recv_sem=recv, device_id=to, device_id_type=MESH
    )


class Wires:
    def __init__(self, send, recv):
        self.send, self.recv, self.sent = send, recv, []

    def push(self, src, dst, to):
        k = len(self.sent)
        copy = remote(src, dst, self.send.at[k], self.recv.at[k], to)
        copy.start()
        self.sent.append(copy)
        return k

    def pull(self, k, landed, origin):
        remote(landed, landed, self.send.at[k], self.recv.at[k], origin).wait_recv()

    def drain(self):
        for copy in self.sent:
            copy.wait_send()


class Shared:
    def __init__(self, where, wires):
        self.where, self.wires, self.blocks = where, wires, []

    def push(self, block):
        mine = block(self.where.core)
        self.blocks.append((self.wires.push(mine, mine, self.where.sibling), block))

    def pull(self):
        for k, block in self.blocks:
            self.wires.pull(k, block(1 - self.where.core), self.where.sibling)
        self.blocks = []


def straight(where, wires, axis, n, block):
    me = where.at(axis)
    mine = block(where.core, me)
    numbers = [wires.push(mine, mine, where.beside(axis, i)) for i in range(1, n)]
    yield
    for i, k in enumerate(numbers, 1):
        wires.pull(k, block(where.core, lax.rem(me - i + n, n)), where.beside(axis, -i))


def ring(where, wires, axis, n, block, shared=None):
    me = where.at(axis)
    for step in range(1, n // 2 + 1):
        numbers = []
        for side, sign in ((0, 1), (1, -1)):
            part = side if step == n // 2 else None
            mine = block(where.core, lax.rem(me - sign * (step - 1) + n, n), part)
            numbers.append(wires.push(mine, mine, where.beside(axis, sign)))
        yield
        for side, sign in ((0, 1), (1, -1)):
            part = side if step == n // 2 else None
            pos = lax.rem(me - sign * step + n, n)
            wires.pull(numbers[side], block(where.core, pos, part), where.beside(axis, -sign))
            if shared is not None:
                shared.push(lambda core, pos=pos, part=part: block(core, pos, part))


def together(*chains):
    chains = list(chains)
    while chains:
        chains = [chain for chain in chains if next(chain, chain) is not chain]


def some(part, size):
    return slice(None) if part is None else pl.ds(part * size, size)


def planes(where, wires, block, shared):
    me = where.z
    numbers = []
    mine = block(where.core, me)
    for step in (1, -1, 2, -2):
        numbers.append((wires.push(mine, mine, where.beside("z", step)), step))
    yield
    for k, step in numbers:
        pos = lax.rem(me - step + 8, 8)
        wires.pull(k, block(where.core, pos), where.beside("z", -step))
        shared.push(lambda core, pos=pos: block(core, pos))
    numbers = []
    for side, sign in ((0, 1), (1, -1)):
        pos = lax.rem(me - 2 * sign + 8, 8)
        for step, part in ((sign, None), (2 * sign, side)):
            mine = block(where.core, pos, part)
            numbers.append((wires.push(mine, mine, where.beside("z", step)), step, sign, part))
    yield
    for k, step, sign, part in numbers:
        pos = lax.rem(me - step - 2 * sign + 8, 8)
        wires.pull(k, block(where.core, pos, part), where.beside("z", -step))
        shared.push(lambda core, pos=pos, part=part: block(core, pos, part))


def gather(where, g, weight, logits, meanwhile, ring_send, ring_recv, pair_send, pair_recv):
    wires, shared = Wires(ring_send, ring_recv), Shared(where, Wires(pair_send, pair_recv))
    x, y, zl, zh = where.x, where.y, where.zl, where.zh
    one, two, three, rest = (0, 256), (256, 384), (640, 384), (256, 768)

    def z_last(half):
        def block(core, pos, part=None):
            return g.at[
                core, lax.rem(pos, 2), pl.ds(2 * half, 2), some(part, 2), lax.div(pos, 2), :, pl.ds(*one)
            ]

        shared.push(lambda core: block(core, where.z))
        yield from planes(where, wires, block, shared)

    def x_last(half):
        def block(core, pos, part=None):
            return g.at[core, half, some(part, 2), pos, :, :, pl.ds(*two)]

        yield from straight(where, wires, "y", 4, lambda core, pos: g.at[core, half, pos, x, :, :, pl.ds(*two)])
        shared.push(lambda core: block(core, x))
        yield from ring(where, wires, "x", 4, block, shared)

    def y_last(half):
        def block(core, pos, part=None):
            return g.at[core, half, pos, some(part, 2), :, :, pl.ds(*three)]

        yield from straight(where, wires, "x", 4, lambda core, pos: g.at[core, half, y, pos, :, :, pl.ds(*three)])
        shared.push(lambda core: block(core, y))
        yield from ring(where, wires, "y", 4, block, shared)

    def multiply(at, lanes):
        start, width = lanes
        total = logits[at]
        shape = total.shape
        height = math.prod(shape[:-1])
        total = total.reshape(height, shape[-1])
        for core in (0, 1):
            rows = g[(core, *at, slice(None), pl.ds(start, width))].reshape(height, width)
            columns = weight[core * HALF + start : core * HALF + start + width]
            total = total + jnp.dot(rows, columns, preferred_element_type=jnp.float32)
        logits[at] = total.reshape(shape)

    def over_planes(count, step):
        def body(i, _):
            pos = lax.rem(where.z + step(i), 8)
            multiply((lax.rem(pos, 2), slice(None), slice(None), lax.div(pos, 2)), one)
            return 0

        lax.fori_loop(0, count, body, 0)

    def over_slabs(count, step):
        def body(i, _):
            multiply((slice(None), slice(None), lax.rem(x + step(i), 4), slice(None)), two)
            multiply((slice(None), lax.rem(y + step(i), 4), slice(None), slice(None)), three)
            return 0

        lax.fori_loop(0, count, body, 0)

    def advance(chains):
        for chain in chains:
            next(chain, None)

    by_x = straight(where, wires, "x", 4, lambda core, pos: g.at[core, zl, y, pos, zh, :, pl.ds(*one)])
    by_y = straight(where, wires, "y", 4, lambda core, pos: g.at[core, zl, pos, :, zh, :, pl.ds(*one)])
    by_z = straight(
        where, wires, "z", 8, lambda core, pos: g.at[core, lax.rem(pos, 2), y, x, lax.div(pos, 2), :, pl.ds(*rest)]
    )
    early, late = [x_last(0), y_last(0)], [x_last(1), y_last(1)]
    advance([by_x, by_z])
    logits[...] = jnp.zeros_like(logits)
    meanwhile()
    advance([by_x, by_y, by_z] + early + late)
    advance([by_y])
    early, late = [z_last(0)] + early, [z_last(1)] + late
    advance(early + late)
    shared.pull()
    over_planes(1, lambda i: 0)
    over_slabs(1, lambda i: 0)
    advance(early + late)
    shared.pull()
    over_planes(4, lambda i: i + 1 + 3 * lax.div(i, 2))
    over_slabs(2, lambda i: 2 * i + 1)
    advance(early + late)
    shared.pull()
    over_planes(3, lambda i: i + 3)
    over_slabs(1, lambda i: 2)
    wires.drain()
    shared.wires.drain()


def spread_rows(where, rows, ring_send, ring_recv, pair_send, pair_recv):
    wires, shared = Wires(ring_send, ring_recv), Shared(where, Wires(pair_send, pair_recv))
    y, zl = where.y, where.zl
    low, high = pl.ds(0, HALF // 2), pl.ds(HALF // 2, HALF // 2)
    facing = ((((1 - zl) * 4 + y) * 2 + where.core), where.e)

    def swap(block):
        mine = block(where.core, zl)
        k = wires.push(mine, mine, facing)
        yield
        wires.pull(k, block(where.core, 1 - zl), facing)

    def z_last():
        block = lambda core, side: rows.at[core, :, side, :, low]
        yield from ring(
            where, wires, "y", 4, lambda core, pos, part: rows.at[core, pos, zl, some(part, 32), low]
        )
        shared.push(lambda core: block(core, zl))
        yield from swap(block)
        shared.push(lambda core: block(core, 1 - zl))

    def y_last():
        block = lambda core, pos, part=None: rows.at[core, pos, some(part, 1), :, high]
        yield from swap(lambda core, side: rows.at[core, y, side, :, high])
        shared.push(lambda core: block(core, y))
        yield from ring(where, wires, "y", 4, block, shared)

    together(z_last(), y_last())
    shared.pull()
    return wires, shared.wires


def exchange(n, me, to, src, dst, send, recv, meanwhile=None):
    def each(i, _):
        other = lax.rem(me + i, n)
        remote(src(other), dst.at[me], send.at[i], recv.at[i], to(other)).start()
        return 0

    lax.fori_loop(1, n, each, 0)
    if meanwhile is not None:
        meanwhile()

    def done(i, _):
        origin = lax.rem(me - i + n, n)
        copy = remote(src(origin), dst.at[origin], send.at[i], recv.at[i], to(origin))
        copy.wait_recv()
        copy.wait_send()
        return 0

    lax.fori_loop(1, n, done, 0)


def merge(stats):
    high = stats[:, 0:1, :]
    top = jnp.max(high, axis=0)
    total = jnp.sum(stats[:, 1:2, :] * jnp.exp(high - top[None]), axis=0)
    return top, total, jnp.sum(stats[:, 2:3, :], axis=0)


def rows8(first, second, third):
    row = lax.broadcasted_iota(jnp.int32, (8, 128), 0)
    zero = jnp.zeros((8, 128), jnp.float32)
    out = jnp.where(row == 0, first, zero)
    out = jnp.where(row == 1, second, out)
    return jnp.where(row == 2, third, out)


def one_hot(table, tokens):
    shape = (tokens, 256)
    column = lax.broadcasted_iota(jnp.int32, shape, 1)
    token = lax.broadcasted_iota(jnp.int32, shape, 0)
    expert = lax.div(column, 16).astype(jnp.float32)
    slot = lax.rem(lax.div(column, 4), 2).astype(jnp.float32)
    same = lax.rem(lax.div(column, 8), 2) == lax.div(token, 8)
    piece = lax.rem(column, 4)
    hits = [jnp.where(table[:, k : k + 1] == expert, 1.0, 0.0) for k in (0, 1)]
    later = lax.broadcasted_iota(jnp.int32, (tokens, tokens), 0)
    sooner = lax.broadcasted_iota(jnp.int32, (tokens, tokens), 1)
    before = jnp.where((sooner < later) & (lax.div(sooner, 8) == lax.div(later, 8)), 1.0, 0.0)
    earlier = jnp.dot(
        before.astype(jnp.bfloat16), (hits[0] + hits[1]).astype(jnp.bfloat16), preferred_element_type=jnp.float32
    )
    placed = [jnp.where(same & (earlier == slot), hit, 0.0) for hit in hits]
    return [
        jnp.concatenate([jnp.where(piece == j, one, 0.0) for j in range(QUARTERS)], axis=0) for one in placed
    ]


def stack(values):
    return jnp.concatenate([values[:, j * 256 : (j + 1) * 256] for j in range(QUARTERS)], axis=0)


def experts(
    where, barrier, small, late, hidden_ref, routes_ref, gates_ref, gain_ref, final_gain_ref, weight_in, weight_out, loads, g,
    local, outbox, pack, outgoing, incoming, rows, units, away, sent_half, summed, parts, returning, returned, spread,
    pack_send, pack_recv, go_send, go_recv, row_send, row_recv, rowp_send, rowp_recv, half_send, half_recv,
    sum_send, sum_recv, back_send, back_recv, ln_send, ln_recv,
):
    core, m = where.core, where.y * 2 + where.zl
    mine = pl.ds(pl.multiple_of(core * HALF, HALF), HALF)
    theirs = pl.ds(pl.multiple_of((1 - core) * HALF, HALF), HALF)
    to_expert = lambda other: (where.s, other)
    to_chip = lambda other: ((lax.rem(other, 2) * 4 + lax.div(other, 2)) * 2 + core, where.e)
    features = 2 * HALF

    for one in small:
        one.wait()
    lane = lax.broadcasted_iota(jnp.int32, (8, 128), 1)
    same = lax.broadcasted_iota(jnp.int32, (8, 8), 0) == lax.broadcasted_iota(jnp.int32, (8, 8), 1)
    table = jnp.zeros((8, 128), jnp.float32)
    for place, (source, k) in enumerate(((routes_ref, 0), (routes_ref, 1), (gates_ref, 0), (gates_ref, 1))):
        row = source[k : k + 1, :].astype(jnp.float32)
        column = jnp.sum(jnp.where(same, row, 0.0), axis=1, keepdims=True)
        table = jnp.where(lane == place, column, table)
    whole = hidden_ref[...].astype(jnp.float32)
    average = jnp.mean(whole, axis=-1, keepdims=True)
    centered = whole - average
    spread_of = jnp.mean(centered * centered, axis=-1, keepdims=True)
    normed = centered * lax.rsqrt(spread_of + 1e-05) * gain_ref[...]
    local[0] = normed.astype(jnp.bfloat16).astype(jnp.float32)
    local[1] = whole
    for box, half in ((outbox, theirs), (pack.at[core], mine)):
        box[:, 0:HALF] = local[0, :, half]
        box[:, HALF:features] = local[1, :, half]
        box[:, features:] = table
    pl.semaphore_wait(barrier, 32)
    swap = remote(outbox, pack.at[core], pack_send, pack_recv, where.sibling)
    swap.start()
    swap.wait()

    tokens = 16
    normed = pack[:, :, 0:HALF].reshape(tokens, HALF).astype(jnp.bfloat16)
    residual = pack[:, :, HALF:features].reshape(tokens, HALF)
    table = pack[:, :, features:].reshape(tokens, 128)
    chosen = one_hot(table, tokens)
    place = jnp.transpose(chosen[0] + chosen[1]).astype(jnp.bfloat16)
    slots = jnp.dot(place, stack(normed), preferred_element_type=jnp.float32).astype(jnp.bfloat16)
    outgoing[...] = slots.reshape(16, 16, 256)
    incoming[where.e] = outgoing[where.e]
    exchange(16, where.e, to_expert, lambda other: outgoing.at[other], incoming, go_send, go_recv)

    down = lax.broadcasted_iota(jnp.int32, (256, 256), 0)
    across = lax.broadcasted_iota(jnp.int32, (256, 256), 1)
    split = jnp.where(across == 4 * lax.rem(down, 64) + lax.div(down, 64), 1.0, 0.0).astype(jnp.bfloat16)
    join = jnp.where(down == 4 * lax.rem(across, 64) + lax.div(across, 64), 1.0, 0.0).astype(jnp.bfloat16)
    arrived = jnp.dot(split, incoming[...].reshape(256, 256), preferred_element_type=jnp.float32)
    for j in range(QUARTERS):
        rows[core, where.y, where.zl, :, j * 256 : (j + 1) * 256] = arrived[j * 64 : (j + 1) * 64].astype(jnp.bfloat16)

    wires, pairs = spread_rows(where, rows, row_send, row_recv, rowp_send, rowp_recv)
    loads[0].wait()
    loads[1].wait()

    def first(i, _):
        low = rows[0, pl.ds(i * 2, 2)].reshape(256, HALF)
        high = rows[1, pl.ds(i * 2, 2)].reshape(256, HALF)
        found = jnp.dot(low, weight_in[0:HALF], preferred_element_type=jnp.float32)
        found = found + jnp.dot(high, weight_in[HALF:], preferred_element_type=jnp.float32)
        units[pl.ds(i * 2, 2)] = jnp.maximum(found, 0.0).astype(jnp.bfloat16).reshape(2, 128, -1)
        return 0

    lax.fori_loop(0, 2, first, 0)

    def half(i, other):
        return remote(away.at[other], sent_half.at[other], half_send.at[i], half_recv.at[i], where.sibling)

    def second(i, _):
        other = lax.rem(where.y + 1 + i, 4)
        found = jnp.dot(units[other], weight_out[:, theirs], preferred_element_type=jnp.float32)
        away[other] = found.astype(jnp.bfloat16)
        half(i, other).start()
        return 0

    lax.fori_loop(0, 4, second, 0)

    def part(block, origin):
        return remote(summed.at[block], parts.at[origin], sum_send.at[block], sum_recv.at[origin], to_chip(block))

    def add(i, _):
        other = lax.rem(where.y + 1 + i, 4)
        near = jnp.dot(units[other], weight_out[:, mine], preferred_element_type=jnp.float32)
        half(i, other).wait_recv()
        total = (near + sent_half[other].astype(jnp.float32)).astype(jnp.bfloat16)
        summed[pl.ds(other * 2, 2)] = total.reshape(2, 64, HALF)
        for side in (0, 1):
            block = other * 2 + side

            @pl.when(block != m)
            def _():
                part(block, m).start()

        return 0

    lax.fori_loop(0, 4, add, 0)
    parts[m] = summed[m]

    def take_part(i, _):
        origin = lax.rem(m - i + 8, 8)
        remote(summed.at[origin], parts.at[origin], sum_send.at[origin], sum_recv.at[origin], to_chip(origin)).wait_recv()
        return 0

    lax.fori_loop(1, 8, take_part, 0)
    total = parts[0].astype(jnp.float32)
    for i in range(1, 8):
        total = total + parts[i].astype(jnp.float32)
    results = jnp.dot(join, stack(total.astype(jnp.bfloat16)), preferred_element_type=jnp.float32)
    returning[...] = results.astype(jnp.bfloat16).reshape(16, 16, 256)
    returned[where.e] = returning[where.e]
    exchange(16, where.e, to_expert, lambda other: returning.at[other], returned, back_send, back_recv)

    back = returned[...].reshape(256, 256)
    mixed = [residual[:, j * 256 : (j + 1) * 256] for j in range(QUARTERS)]
    for k in (0, 1):
        found = jnp.dot(chosen[k].astype(jnp.bfloat16), back, preferred_element_type=jnp.float32)
        gate = table[:, 2 + k : 3 + k]
        mixed = [old + gate * found[j * tokens : (j + 1) * tokens] for j, old in enumerate(mixed)]
    mixed = jnp.concatenate(mixed, axis=1)
    center = jnp.mean(mixed, axis=-1, keepdims=True)
    squares = jnp.sum((mixed - center) * (mixed - center), axis=-1, keepdims=True)
    lane = lax.broadcasted_iota(jnp.int32, (tokens, 128), 1)
    spread[core] = jnp.where(lane == 0, center, jnp.where(lane == 1, squares, 0.0))
    swap = remote(spread.at[core], spread.at[core], ln_send, ln_recv, where.sibling)
    swap.start()
    swap.wait()
    centers = [spread[i, :, 0:1] for i in (0, 1)]
    average = 0.5 * (centers[0] + centers[1])
    apart = centers[0] - centers[1]
    variance = (spread[0, :, 1:2] + spread[1, :, 1:2] + apart * apart * (0.5 * HALF)) / features
    late.wait()
    final = (mixed - average) * lax.rsqrt(variance + 1e-05) * final_gain_ref[:, mine]
    g[core, where.zl, where.y, where.x, where.zh] = final.astype(jnp.bfloat16)

    wires.drain()
    pairs.drain()

    def halves_left(i, _):
        half(i, lax.rem(where.y + 1 + i, 4)).wait_send()
        return 0

    lax.fori_loop(0, 4, halves_left, 0)

    def parts_left(i, _):
        part(lax.rem(m + i, 8), m).wait_send()
        return 0

    lax.fori_loop(1, 8, parts_left, 0)


def layer_kernel(
    hidden_hbm, routes_hbm, gates_hbm, gain_hbm, final_gain_hbm, targets_hbm, in_hbm, out_hbm, weight_hbm,
    kept, heads, norms_ref,
    g, weight, logits, wanted, stats, by_group, by_section, merged, solved,
    weight_sem, ring_send, ring_recv, pair_send, pair_recv,
    one_send, one_recv, two_send, two_recv, three_send, three_recv,
    weight_in, weight_out, weight_sems, hidden_ref, routes_ref, gates_ref, gain_ref, final_gain_ref, targets_ref,
    small_sems, *scratch,
):
    where = Place()
    barrier = pltpu.get_barrier_semaphore()
    pairs = (
        (hidden_hbm, hidden_ref), (routes_hbm, routes_ref), (gates_hbm, gates_ref), (gain_hbm, gain_ref),
        (final_gain_hbm, final_gain_ref), (targets_hbm, targets_ref),
    )
    small = [pltpu.make_async_copy(a, b, small_sems.at[i]) for i, (a, b) in enumerate(pairs)]
    for one in small:
        one.start()
    load = pltpu.make_async_copy(weight_hbm, weight, weight_sem)
    loads = [
        pltpu.make_async_copy(in_hbm.at[0], weight_in, weight_sems.at[0]),
        pltpu.make_async_copy(out_hbm.at[0], weight_out, weight_sems.at[1]),
    ]
    for one in loads:
        one.start()
    load.start()

    def greet(i, _):
        pl.semaphore_signal(
            barrier, inc=1, device_id=(lax.rem(where.s + i, 16), where.e), device_id_type=MESH
        )
        pl.semaphore_signal(
            barrier, inc=1, device_id=(where.s, lax.rem(where.e + i, 16)), device_id_type=MESH
        )
        return 0

    lax.fori_loop(1, 16, greet, 0)
    for step in (1, -1):
        pl.semaphore_signal(barrier, inc=1, device_id=where.beside("z", step), device_id_type=MESH)

    experts(
        where, barrier, small[:4], small[4], hidden_ref, routes_ref, gates_ref, gain_ref, final_gain_ref, weight_in, weight_out,
        loads, g, *scratch
    )
    load.wait()
    small[5].wait()

    def spread_targets():
        def body(group, _):
            row = targets_ref[pl.ds(group, 1), :].astype(jnp.float32)
            wanted[group] = jnp.transpose(jnp.broadcast_to(row, (128, 128))).astype(jnp.int32)
            return 0

        lax.fori_loop(0, 2 * PIECES, body, 0)

    gather(where, g, weight, logits, spread_targets, ring_send, ring_recv, pair_send, pair_recv)

    columns = weight.shape[1]
    offset = (where.s * 16 + where.e) * columns
    lane = lax.broadcasted_iota(jnp.int32, (128, 128), 1)

    def chunk(i, _):
        zl, y = lax.div(i, 4), lax.rem(i, 4)
        for core in (0, 1):
            group = i * 2 + core
            part = logits[zl, y, :, :, core * 8 : (core + 1) * 8]
            kept[group] = part
            part = part.reshape(128, columns)
            tiles = [part[:, i : i + 128] for i in range(0, columns, 128)]
            top = functools.reduce(jnp.maximum, tiles)
            total = sum(jnp.exp(tile - top) for tile in tiles)
            picked = sum(
                jnp.where(wanted[group] == lane + (offset + i * 128), tile, 0.0) for i, tile in enumerate(tiles)
            )
            top = jnp.transpose(top)
            highest = jnp.max(top, axis=0, keepdims=True)
            total = jnp.sum(jnp.transpose(total) * jnp.exp(top - highest), axis=0, keepdims=True)
            picked = jnp.sum(jnp.transpose(picked), axis=0, keepdims=True)
            stats[group] = rows8(highest, total, picked)
        return 0

    lax.fori_loop(0, PIECES, chunk, 0)

    to_expert = lambda other: (where.s, other)
    to_section = lambda other: (other, where.e)
    by_group[where.s] = stats[where.s]

    def round_logits():
        def body(group, _):
            heads[pl.ds(group * 128, 128), :] = kept[group].reshape(128, columns).astype(jnp.bfloat16)
            return 0

        lax.fori_loop(0, 2 * PIECES, body, 0)

    exchange(16, where.s, to_section, lambda other: stats.at[other], by_group, one_send, one_recv, round_logits)
    merged[...] = rows8(*merge(by_group[...]))
    by_section[where.e] = merged[...]
    exchange(16, where.e, to_expert, lambda other: merged, by_section, two_send, two_recv)
    top, total, picked = merge(by_section[...])
    log_norm = top + jnp.log(total)
    solved[...] = rows8(log_norm, log_norm - picked, jnp.zeros_like(picked))
    norms_ref[where.s] = solved[...]
    exchange(16, where.s, to_section, lambda other: solved, norms_ref, three_send, three_recv)


def layer(hidden, routes, gates, gain, final_gain, targets, weight_in, weight_out, weight):
    features, columns = weight.shape
    tokens = targets.size
    inner = weight_in.shape[2]
    dma = pltpu.SemaphoreType.DMA
    bf16, f32 = jnp.bfloat16, jnp.float32
    vmem = pl.BlockSpec(memory_space=pltpu.VMEM)
    operands = (hidden, routes, gates, gain, final_gain, targets, weight_in, weight_out, weight)
    return pl.pallas_call(
        layer_kernel,
        name="layer",
        out_shape=(
            pltpu.VMEM((16, 4, 4, 8, columns), f32),
            pltpu.VMEM((tokens, columns), bf16),
            pltpu.VMEM((16, 8, 128), f32),
        ),
        in_specs=[pl.BlockSpec(memory_space=pltpu.HBM)] * 9,
        out_specs=(vmem, vmem, vmem),
        scratch_shapes=[
            pltpu.VMEM((2, 2, 4, 4, 4, 16, HALF), bf16),
            pltpu.VMEM((features, columns), bf16),
            pltpu.VMEM((2, 4, 4, 4, 16, columns), f32),
            pltpu.VMEM((16, 128, 128), jnp.int32),
            pltpu.VMEM((16, 8, 128), f32),
            pltpu.VMEM((16, 8, 128), f32),
            pltpu.VMEM((16, 8, 128), f32),
            pltpu.VMEM((8, 128), f32),
            pltpu.VMEM((8, 128), f32),
            dma,
            dma((57,)), dma((57,)), dma((38,)), dma((38,)),
            dma((16,)), dma((16,)), dma((16,)), dma((16,)), dma((16,)), dma((16,)),
            pltpu.VMEM((features, inner), bf16),
            pltpu.VMEM((inner, features), bf16),
            dma((2,)),
            pltpu.VMEM(hidden.shape, bf16),
            pltpu.VMEM(routes.shape, jnp.int32),
            pltpu.VMEM(gates.shape, f32),
            pltpu.VMEM(gain.shape, f32),
            pltpu.VMEM(final_gain.shape, f32),
            pltpu.VMEM(targets.shape, jnp.int32),
            dma((6,)),
            pltpu.VMEM((2, 8, features), f32),
            pltpu.VMEM((8, features + 128), f32),
            pltpu.VMEM((2, 8, features + 128), f32),
            pltpu.VMEM((16, 16, 256), bf16),
            pltpu.VMEM((16, 16, 256), bf16),
            pltpu.VMEM((2, 4, 2, 64, HALF), bf16),
            pltpu.VMEM((4, 128, inner), bf16),
            pltpu.VMEM((4, 128, HALF), bf16),
            pltpu.VMEM((4, 128, HALF), bf16),
            pltpu.VMEM((8, 64, HALF), bf16),
            pltpu.VMEM((8, 64, HALF), bf16),
            pltpu.VMEM((16, 16, 256), bf16),
            pltpu.VMEM((16, 16, 256), bf16),
            pltpu.VMEM((2, 16, 128), f32),
            dma, dma, dma((16,)), dma((16,)), dma((10,)), dma((10,)), dma((7,)), dma((7,)),
            dma((4,)), dma((4,)), dma((8,)), dma((8,)), dma((16,)), dma((16,)), dma, dma,
        ],
        compiler_params=pltpu.CompilerParams(
            collective_id=1, has_side_effects=True, vmem_limit_bytes=48 * 1024 * 1024
        ),
    )(*(pltpu.with_memory_space_constraint(one, pltpu.HBM) for one in operands))


def finish_kernel(logits_ref, heads_ref, norms_ref, lengths_ref, probs_hbm, head_hbm, loss_ref, probs, probs_sem, head_sem):
    position = lax.broadcasted_iota(jnp.int32, (1, TGT), 1)
    groups, columns = logits_ref.shape[0], logits_ref.shape[-1]
    rounded = pltpu.make_async_copy(heads_ref, head_hbm, head_sem)
    rounded.start()

    def copy(group):
        rows = pl.ds(group * TGT, TGT)
        return pltpu.make_async_copy(probs.at[rows], probs_hbm.at[rows], probs_sem.at[group])

    def each(group, _):
        rows = pl.ds(group * TGT, TGT)
        shift = jnp.transpose(jnp.broadcast_to(norms_ref[group, 0:1, :], (TGT, TGT)))
        for tile in range(columns // TGT):
            lanes = slice(tile * TGT, (tile + 1) * TGT)
            values = logits_ref[group, :, :, :, lanes].reshape(TGT, TGT)
            probs[rows, lanes] = (values - shift).astype(jnp.bfloat16)
        copy(group).start()
        loss_ref[pl.ds(group, 1), :] = jnp.where(position < lengths_ref[group], norms_ref[group, 1:2, :], 0.0)
        return 0

    def done(group, _):
        copy(group).wait()
        return 0

    lax.fori_loop(0, groups, each, 0)
    lax.fori_loop(0, groups, done, 0)
    rounded.wait()


def finish(logits, heads, norms, lengths):
    groups = logits.shape[0]
    vmem, hbm = pl.BlockSpec(memory_space=pltpu.VMEM), pl.BlockSpec(memory_space=pl.ANY)
    return pl.pallas_call(
        finish_kernel,
        name="finish",
        out_shape=(
            jax.ShapeDtypeStruct(heads.shape, jnp.bfloat16),
            jax.ShapeDtypeStruct(heads.shape, jnp.bfloat16),
            jax.ShapeDtypeStruct((groups, TGT), jnp.float32),
        ),
        in_specs=[vmem, vmem, vmem, pl.BlockSpec(memory_space=pltpu.SMEM)],
        out_specs=(hbm, hbm, vmem),
        scratch_shapes=[
            pltpu.VMEM(heads.shape, jnp.bfloat16),
            pltpu.SemaphoreType.DMA((groups,)),
            pltpu.SemaphoreType.DMA,
        ],
        compiler_params=pltpu.CompilerParams(vmem_limit_bytes=24 * 1024 * 1024),
    )(
        pltpu.with_memory_space_constraint(logits, pltpu.VMEM),
        pltpu.with_memory_space_constraint(heads, pltpu.VMEM),
        pltpu.with_memory_space_constraint(norms, pltpu.VMEM),
        lengths,
    )


def on_device(
    hidden, routes, gates, targets, target_lengths, moe_gain, fc_in, fc_out, final_gain, head_weight
):
    wanted = targets.reshape(-1, TGT)
    logits, heads, norms = layer(
        hidden, routes.T, gates.T, moe_gain[None], final_gain[None], wanted, fc_in, fc_out, head_weight
    )
    log_probs, head_logits, loss = finish(logits, heads, norms, target_lengths)
    return (log_probs, head_logits, loss.reshape(-1))


def solution(mesh):
    return jax.shard_map(
        on_device,
        mesh=mesh,
        in_specs=(
            P(("section", "expert"), None),
            P(("section", "expert"), None),
            P(("section", "expert"), None),
            P(),
            P(),
            P(),
            P("expert", None, "section"),
            P("expert", "section", None),
            P(),
            P(None, ("section", "expert")),
        ),
        out_specs=(P(None, ("section", "expert")), P(None, ("section", "expert")), P()),
        check_vma=False,
    )
```

```python
import functools
import math

import jax
import jax.numpy as jnp
from jax import lax
from jax.experimental import pallas as pl
from jax.experimental.pallas import tpu as pltpu
from jax.sharding import PartitionSpec as P

TGT = 128
MESH = pl.DeviceIdType.MESH
HALF = 1024
PIECES = 8
QUARTERS = 4


class Place:
    def __init__(self):
        self.s = lax.axis_index("section")
        self.e = lax.axis_index("expert")
        self.core = lax.rem(self.s, 2)
        self.y = lax.rem(lax.div(self.s, 2), 4)
        self.zl = lax.div(self.s, 8)
        self.x = lax.div(self.e, 4)
        self.zh = lax.rem(self.e, 4)
        self.z = self.zh * 2 + self.zl
        self.sibling = (self.s + 1 - 2 * self.core, self.e)

    def at(self, axis):
        return {"x": self.x, "y": self.y, "z": self.z}[axis]

    def beside(self, axis, step):
        x, y, z = self.x, self.y, self.z
        if axis == "x":
            x = lax.rem(x + step + 4, 4)
        elif axis == "y":
            y = lax.rem(y + step + 4, 4)
        else:
            z = lax.rem(z + step + 8, 8)
        return ((lax.rem(z, 2) * 4 + y) * 2 + self.core, x * 4 + lax.div(z, 2))


def remote(src, dst, send, recv, to):
    return pltpu.make_async_remote_copy(
        src_ref=src, dst_ref=dst, send_sem=send, recv_sem=recv, device_id=to, device_id_type=MESH
    )


class Wires:
    def __init__(self, send, recv):
        self.send, self.recv, self.sent = send, recv, []

    def push(self, src, dst, to):
        k = len(self.sent)
        copy = remote(src, dst, self.send.at[k], self.recv.at[k], to)
        copy.start()
        self.sent.append(copy)
        return k

    def pull(self, k, landed, origin):
        remote(landed, landed, self.send.at[k], self.recv.at[k], origin).wait_recv()

    def drain(self):
        for copy in self.sent:
            copy.wait_send()


class Shared:
    def __init__(self, where, wires):
        self.where, self.wires, self.blocks = where, wires, []

    def push(self, block):
        mine = block(self.where.core)
        self.blocks.append((self.wires.push(mine, mine, self.where.sibling), block))

    def pull(self):
        for k, block in self.blocks:
            self.wires.pull(k, block(1 - self.where.core), self.where.sibling)
        self.blocks = []


def straight(where, wires, axis, n, block):
    me = where.at(axis)
    mine = block(where.core, me)
    order = sorted(range(1, n), key=lambda i: -min(i, n - i))
    numbers = [wires.push(mine, mine, where.beside(axis, i)) for i in order]
    yield
    for i, k in zip(order, numbers):
        wires.pull(k, block(where.core, lax.rem(me - i + n, n)), where.beside(axis, -i))


def ring(where, wires, axis, n, block, shared=None):
    me = where.at(axis)
    for step in range(1, n // 2 + 1):
        numbers = []
        for side, sign in ((0, 1), (1, -1)):
            part = side if step == n // 2 else None
            mine = block(where.core, lax.rem(me - sign * (step - 1) + n, n), part)
            numbers.append(wires.push(mine, mine, where.beside(axis, sign)))
        yield
        for side, sign in ((0, 1), (1, -1)):
            part = side if step == n // 2 else None
            pos = lax.rem(me - sign * step + n, n)
            wires.pull(numbers[side], block(where.core, pos, part), where.beside(axis, -sign))
            if shared is not None:
                shared.push(lambda core, pos=pos, part=part: block(core, pos, part))


def together(*chains):
    chains = list(chains)
    while chains:
        chains = [chain for chain in chains if next(chain, chain) is not chain]


def some(part, size):
    return slice(None) if part is None else pl.ds(part * size, size)


def planes(where, wires, block, shared):
    me = where.z
    numbers = []
    mine = block(where.core, me)
    for step in (2, -2, 1, -1):
        numbers.append((wires.push(mine, mine, where.beside("z", step)), step))
    yield
    for k, step in numbers:
        pos = lax.rem(me - step + 8, 8)
        wires.pull(k, block(where.core, pos), where.beside("z", -step))
        shared.push(lambda core, pos=pos: block(core, pos))
    numbers = []
    for side, sign in ((0, 1), (1, -1)):
        pos = lax.rem(me - 2 * sign + 8, 8)
        for step, part in ((2 * sign, side), (sign, None)):
            mine = block(where.core, pos, part)
            numbers.append((wires.push(mine, mine, where.beside("z", step)), step, sign, part))
    yield
    for k, step, sign, part in numbers:
        pos = lax.rem(me - step - 2 * sign + 8, 8)
        wires.pull(k, block(where.core, pos, part), where.beside("z", -step))
        shared.push(lambda core, pos=pos, part=part: block(core, pos, part))


def gather(where, g, weight, logits, meanwhile, ring_send, ring_recv, pair_send, pair_recv):
    wires, shared = Wires(ring_send, ring_recv), Shared(where, Wires(pair_send, pair_recv))
    x, y, zl, zh = where.x, where.y, where.zl, where.zh
    one, two, three, rest = (0, 256), (256, 384), (640, 384), (256, 768)

    def z_last(half):
        def block(core, pos, part=None):
            return g.at[
                core, lax.rem(pos, 2), pl.ds(2 * half, 2), some(part, 2), lax.div(pos, 2), :, pl.ds(*one)
            ]

        shared.push(lambda core: block(core, where.z))
        yield from planes(where, wires, block, shared)

    def x_last(half):
        def block(core, pos, part=None):
            return g.at[core, half, some(part, 2), pos, :, :, pl.ds(*two)]

        yield from straight(where, wires, "y", 4, lambda core, pos: g.at[core, half, pos, x, :, :, pl.ds(*two)])
        shared.push(lambda core: block(core, x))
        yield from ring(where, wires, "x", 4, block, shared)

    def y_last(half):
        def block(core, pos, part=None):
            return g.at[core, half, pos, some(part, 2), :, :, pl.ds(*three)]

        yield from straight(where, wires, "x", 4, lambda core, pos: g.at[core, half, y, pos, :, :, pl.ds(*three)])
        shared.push(lambda core: block(core, y))
        yield from ring(where, wires, "y", 4, block, shared)

    def multiply(core, at, lanes):
        start, width = lanes
        total = logits[at]
        shape = total.shape
        height = math.prod(shape[:-1])
        total = total.reshape(height, shape[-1])
        rows = g[(core, *at, slice(None), pl.ds(start, width))].reshape(height, width)
        columns = weight[pl.ds(pl.multiple_of(core * HALF + start, 128), width), :]
        total = total + jnp.dot(rows, columns, preferred_element_type=jnp.float32)
        logits[at] = total.reshape(shape)

    def over_planes(core, count, step):
        def body(i, _):
            pos = lax.rem(where.z + step(i), 8)
            multiply(core, (lax.rem(pos, 2), slice(None), slice(None), lax.div(pos, 2)), one)
            return 0

        lax.fori_loop(0, count, body, 0)

    def over_slabs(core, count, step):
        def body(i, _):
            multiply(core, (slice(None), slice(None), lax.rem(x + step(i), 4), slice(None)), two)
            multiply(core, (slice(None), lax.rem(y + step(i), 4), slice(None), slice(None)), three)
            return 0

        lax.fori_loop(0, count, body, 0)

    def advance(chains):
        for chain in chains:
            next(chain, None)

    by_x = straight(where, wires, "x", 4, lambda core, pos: g.at[core, zl, y, pos, zh, :, pl.ds(*one)])
    by_y = straight(where, wires, "y", 4, lambda core, pos: g.at[core, zl, pos, :, zh, :, pl.ds(*one)])
    by_z = straight(
        where, wires, "z", 8, lambda core, pos: g.at[core, lax.rem(pos, 2), y, x, lax.div(pos, 2), :, pl.ds(*rest)]
    )
    early, late = [x_last(0), y_last(0)], [x_last(1), y_last(1)]
    advance([by_x, by_z])
    logits[...] = jnp.zeros_like(logits)
    meanwhile()
    advance([by_x, by_y, by_z] + early + late)
    advance([by_y])
    early, late = [z_last(0)] + early, [z_last(1)] + late
    rounds = (
        (1, lambda i: 0, 1, lambda i: 0),
        (4, lambda i: i + 1 + 3 * lax.div(i, 2), 2, lambda i: 2 * i + 1),
        (3, lambda i: i + 3, 1, lambda i: 2),
    )
    for planes_in, plane_step, slabs_in, slab_step in rounds:
        advance(early + late)
        for core in (where.core, 1 - where.core):
            if core is not where.core:
                shared.pull()
            over_planes(core, planes_in, plane_step)
            over_slabs(core, slabs_in, slab_step)
    wires.drain()
    shared.wires.drain()


def spread_rows(where, rows, ring_send, ring_recv, pair_send, pair_recv):
    wires, shared = Wires(ring_send, ring_recv), Shared(where, Wires(pair_send, pair_recv))
    y, zl = where.y, where.zl
    low, high = pl.ds(0, HALF // 2), pl.ds(HALF // 2, HALF // 2)
    facing = ((((1 - zl) * 4 + y) * 2 + where.core), where.e)

    def swap(block):
        mine = block(where.core, zl)
        k = wires.push(mine, mine, facing)
        yield
        wires.pull(k, block(where.core, 1 - zl), facing)

    def z_last():
        block = lambda core, side: rows.at[core, :, side, :, low]
        yield from ring(
            where, wires, "y", 4, lambda core, pos, part: rows.at[core, pos, zl, some(part, 32), low]
        )
        shared.push(lambda core: block(core, zl))
        yield from swap(block)
        shared.push(lambda core: block(core, 1 - zl))

    def y_last():
        block = lambda core, pos, part=None: rows.at[core, pos, some(part, 1), :, high]
        yield from swap(lambda core, side: rows.at[core, y, side, :, high])
        shared.push(lambda core: block(core, y))
        yield from ring(where, wires, "y", 4, block, shared)

    together(z_last(), y_last())
    shared.pull()
    return wires, shared.wires


def exchange(n, me, to, src, dst, send, recv, meanwhile=None):
    def each(i, _):
        other = lax.rem(me + i, n)
        remote(src(other), dst.at[me], send.at[i], recv.at[i], to(other)).start()
        return 0

    lax.fori_loop(1, n, each, 0)
    if meanwhile is not None:
        meanwhile()

    def done(i, _):
        origin = lax.rem(me - i + n, n)
        copy = remote(src(origin), dst.at[origin], send.at[i], recv.at[i], to(origin))
        copy.wait_recv()
        copy.wait_send()
        return 0

    lax.fori_loop(1, n, done, 0)


def merge(stats):
    high = stats[:, 0:1, :]
    top = jnp.max(high, axis=0)
    total = jnp.sum(stats[:, 1:2, :] * jnp.exp(high - top[None]), axis=0)
    return top, total, jnp.sum(stats[:, 2:3, :], axis=0)


def rows8(first, second, third):
    row = lax.broadcasted_iota(jnp.int32, (8, 128), 0)
    zero = jnp.zeros((8, 128), jnp.float32)
    out = jnp.where(row == 0, first, zero)
    out = jnp.where(row == 1, second, out)
    return jnp.where(row == 2, third, out)


def one_hot(table, tokens):
    shape = (tokens, 256)
    column = lax.broadcasted_iota(jnp.int32, shape, 1)
    token = lax.broadcasted_iota(jnp.int32, shape, 0)
    expert = lax.div(column, 16).astype(jnp.float32)
    slot = lax.rem(lax.div(column, 4), 2).astype(jnp.float32)
    same = lax.rem(lax.div(column, 8), 2) == lax.div(token, 8)
    piece = lax.rem(column, 4)
    hits = [jnp.where(table[:, k : k + 1] == expert, 1.0, 0.0) for k in (0, 1)]
    later = lax.broadcasted_iota(jnp.int32, (tokens, tokens), 0)
    sooner = lax.broadcasted_iota(jnp.int32, (tokens, tokens), 1)
    before = jnp.where((sooner < later) & (lax.div(sooner, 8) == lax.div(later, 8)), 1.0, 0.0)
    earlier = jnp.dot(
        before.astype(jnp.bfloat16), (hits[0] + hits[1]).astype(jnp.bfloat16), preferred_element_type=jnp.float32
    )
    placed = [jnp.where(same & (earlier == slot), hit, 0.0) for hit in hits]
    return [
        jnp.concatenate([jnp.where(piece == j, one, 0.0) for j in range(QUARTERS)], axis=0) for one in placed
    ]


def stack(values):
    return jnp.concatenate([values[:, j * 256 : (j + 1) * 256] for j in range(QUARTERS)], axis=0)


def experts(
    where, barrier, small, late, hidden_ref, routes_ref, gates_ref, gain_ref, final_gain_ref, weight_in, weight_out, loads, g,
    local, outbox, pack, outgoing, incoming, rows, units, away, sent_half, summed, parts, returning, returned, spread,
    pack_send, pack_recv, go_send, go_recv, row_send, row_recv, rowp_send, rowp_recv, half_send, half_recv,
    sum_send, sum_recv, back_send, back_recv, ln_send, ln_recv,
):
    core, m = where.core, where.y * 2 + where.zl
    mine = pl.ds(pl.multiple_of(core * HALF, HALF), HALF)
    theirs = pl.ds(pl.multiple_of((1 - core) * HALF, HALF), HALF)
    to_expert = lambda other: (where.s, other)
    to_chip = lambda other: ((lax.rem(other, 2) * 4 + lax.div(other, 2)) * 2 + core, where.e)
    features = 2 * HALF

    for one in small:
        one.wait()
    lane = lax.broadcasted_iota(jnp.int32, (8, 128), 1)
    same = lax.broadcasted_iota(jnp.int32, (8, 8), 0) == lax.broadcasted_iota(jnp.int32, (8, 8), 1)
    table = jnp.zeros((8, 128), jnp.float32)
    for place, (source, k) in enumerate(((routes_ref, 0), (routes_ref, 1), (gates_ref, 0), (gates_ref, 1))):
        row = source[k : k + 1, :].astype(jnp.float32)
        column = jnp.sum(jnp.where(same, row, 0.0), axis=1, keepdims=True)
        table = jnp.where(lane == place, column, table)
    whole = hidden_ref[...].astype(jnp.float32)
    average = jnp.mean(whole, axis=-1, keepdims=True)
    centered = whole - average
    spread_of = jnp.mean(centered * centered, axis=-1, keepdims=True)
    normed = centered * lax.rsqrt(spread_of + 1e-05) * gain_ref[...]
    local[0] = normed.astype(jnp.bfloat16).astype(jnp.float32)
    local[1] = whole
    for box, half in ((outbox, theirs), (pack.at[core], mine)):
        box[:, 0:HALF] = local[0, :, half]
        box[:, HALF:features] = local[1, :, half]
        box[:, features:] = table
    pl.semaphore_wait(barrier, 32)
    swap = remote(outbox, pack.at[core], pack_send, pack_recv, where.sibling)
    swap.start()
    swap.wait()

    tokens = 16
    normed = pack[:, :, 0:HALF].reshape(tokens, HALF).astype(jnp.bfloat16)
    residual = pack[:, :, HALF:features].reshape(tokens, HALF)
    table = pack[:, :, features:].reshape(tokens, 128)
    chosen = one_hot(table, tokens)
    place = jnp.transpose(chosen[0] + chosen[1]).astype(jnp.bfloat16)
    slots = jnp.dot(place, stack(normed), preferred_element_type=jnp.float32).astype(jnp.bfloat16)
    outgoing[...] = slots.reshape(16, 16, 256)
    incoming[where.e] = outgoing[where.e]
    exchange(16, where.e, to_expert, lambda other: outgoing.at[other], incoming, go_send, go_recv)

    down = lax.broadcasted_iota(jnp.int32, (256, 256), 0)
    across = lax.broadcasted_iota(jnp.int32, (256, 256), 1)
    split = jnp.where(across == 4 * lax.rem(down, 64) + lax.div(down, 64), 1.0, 0.0).astype(jnp.bfloat16)
    join = jnp.where(down == 4 * lax.rem(across, 64) + lax.div(across, 64), 1.0, 0.0).astype(jnp.bfloat16)
    arrived = jnp.dot(split, incoming[...].reshape(256, 256), preferred_element_type=jnp.float32)
    for j in range(QUARTERS):
        rows[core, where.y, where.zl, :, j * 256 : (j + 1) * 256] = arrived[j * 64 : (j + 1) * 64].astype(jnp.bfloat16)

    wires, pairs = spread_rows(where, rows, row_send, row_recv, rowp_send, rowp_recv)
    loads[0].wait()
    loads[1].wait()

    def first(i, _):
        low = rows[0, pl.ds(i * 2, 2)].reshape(256, HALF)
        high = rows[1, pl.ds(i * 2, 2)].reshape(256, HALF)
        found = jnp.dot(low, weight_in[0:HALF], preferred_element_type=jnp.float32)
        found = found + jnp.dot(high, weight_in[HALF:], preferred_element_type=jnp.float32)
        units[pl.ds(i * 2, 2)] = jnp.maximum(found, 0.0).astype(jnp.bfloat16).reshape(2, 128, -1)
        return 0

    lax.fori_loop(0, 2, first, 0)

    def half(i, other):
        return remote(away.at[other], sent_half.at[other], half_send.at[i], half_recv.at[i], where.sibling)

    def second(i, _):
        other = lax.rem(where.y + 1 + i, 4)
        found = jnp.dot(units[other], weight_out[:, theirs], preferred_element_type=jnp.float32)
        away[other] = found.astype(jnp.bfloat16)
        half(i, other).start()
        return 0

    lax.fori_loop(0, 4, second, 0)

    def part(block, origin):
        return remote(summed.at[block], parts.at[origin], sum_send.at[block], sum_recv.at[origin], to_chip(block))

    def add(i, _):
        other = lax.rem(where.y + 1 + i, 4)
        near = jnp.dot(units[other], weight_out[:, mine], preferred_element_type=jnp.float32)
        half(i, other).wait_recv()
        total = (near + sent_half[other].astype(jnp.float32)).astype(jnp.bfloat16)
        summed[pl.ds(other * 2, 2)] = total.reshape(2, 64, HALF)
        for side in (0, 1):
            block = other * 2 + side

            @pl.when(block != m)
            def _():
                part(block, m).start()

        return 0

    lax.fori_loop(0, 4, add, 0)
    parts[m] = summed[m]

    def take_part(i, _):
        origin = lax.rem(m - i + 8, 8)
        remote(summed.at[origin], parts.at[origin], sum_send.at[origin], sum_recv.at[origin], to_chip(origin)).wait_recv()
        return 0

    lax.fori_loop(1, 8, take_part, 0)
    total = parts[0].astype(jnp.float32)
    for i in range(1, 8):
        total = total + parts[i].astype(jnp.float32)
    results = jnp.dot(join, stack(total.astype(jnp.bfloat16)), preferred_element_type=jnp.float32)
    returning[...] = results.astype(jnp.bfloat16).reshape(16, 16, 256)
    returned[where.e] = returning[where.e]
    exchange(16, where.e, to_expert, lambda other: returning.at[other], returned, back_send, back_recv)

    back = returned[...].reshape(256, 256)
    mixed = [residual[:, j * 256 : (j + 1) * 256] for j in range(QUARTERS)]
    for k in (0, 1):
        found = jnp.dot(chosen[k].astype(jnp.bfloat16), back, preferred_element_type=jnp.float32)
        gate = table[:, 2 + k : 3 + k]
        mixed = [old + gate * found[j * tokens : (j + 1) * tokens] for j, old in enumerate(mixed)]
    mixed = jnp.concatenate(mixed, axis=1)
    center = jnp.mean(mixed, axis=-1, keepdims=True)
    squares = jnp.sum((mixed - center) * (mixed - center), axis=-1, keepdims=True)
    lane = lax.broadcasted_iota(jnp.int32, (tokens, 128), 1)
    spread[core] = jnp.where(lane == 0, center, jnp.where(lane == 1, squares, 0.0))
    swap = remote(spread.at[core], spread.at[core], ln_send, ln_recv, where.sibling)
    swap.start()
    swap.wait()
    centers = [spread[i, :, 0:1] for i in (0, 1)]
    average = 0.5 * (centers[0] + centers[1])
    apart = centers[0] - centers[1]
    variance = (spread[0, :, 1:2] + spread[1, :, 1:2] + apart * apart * (0.5 * HALF)) / features
    late.wait()
    final = (mixed - average) * lax.rsqrt(variance + 1e-05) * final_gain_ref[:, mine]
    g[core, where.zl, where.y, where.x, where.zh] = final.astype(jnp.bfloat16)

    wires.drain()
    pairs.drain()

    def halves_left(i, _):
        half(i, lax.rem(where.y + 1 + i, 4)).wait_send()
        return 0

    lax.fori_loop(0, 4, halves_left, 0)

    def parts_left(i, _):
        part(lax.rem(m + i, 8), m).wait_send()
        return 0

    lax.fori_loop(1, 8, parts_left, 0)


def layer_kernel(
    hidden_hbm, routes_hbm, gates_hbm, gain_hbm, final_gain_hbm, targets_hbm, in_hbm, out_hbm, weight_hbm,
    kept, heads, norms_ref,
    g, weight, logits, wanted, stats, by_group, by_section, merged, solved,
    weight_sem, ring_send, ring_recv, pair_send, pair_recv,
    one_send, one_recv, two_send, two_recv, three_send, three_recv,
    weight_in, weight_out, weight_sems, hidden_ref, routes_ref, gates_ref, gain_ref, final_gain_ref, targets_ref,
    small_sems, *scratch,
):
    where = Place()
    barrier = pltpu.get_barrier_semaphore()
    pairs = (
        (hidden_hbm, hidden_ref), (routes_hbm, routes_ref), (gates_hbm, gates_ref), (gain_hbm, gain_ref),
        (final_gain_hbm, final_gain_ref), (targets_hbm, targets_ref),
    )
    small = [pltpu.make_async_copy(a, b, small_sems.at[i]) for i, (a, b) in enumerate(pairs)]
    for one in small:
        one.start()
    load = pltpu.make_async_copy(weight_hbm, weight, weight_sem)
    loads = [
        pltpu.make_async_copy(in_hbm.at[0], weight_in, weight_sems.at[0]),
        pltpu.make_async_copy(out_hbm.at[0], weight_out, weight_sems.at[1]),
    ]
    for one in loads:
        one.start()
    load.start()

    def greet(i, _):
        pl.semaphore_signal(
            barrier, inc=1, device_id=(lax.rem(where.s + i, 16), where.e), device_id_type=MESH
        )
        pl.semaphore_signal(
            barrier, inc=1, device_id=(where.s, lax.rem(where.e + i, 16)), device_id_type=MESH
        )
        return 0

    lax.fori_loop(1, 16, greet, 0)
    for step in (1, -1):
        pl.semaphore_signal(barrier, inc=1, device_id=where.beside("z", step), device_id_type=MESH)

    experts(
        where, barrier, small[:4], small[4], hidden_ref, routes_ref, gates_ref, gain_ref, final_gain_ref, weight_in, weight_out,
        loads, g, *scratch
    )
    load.wait()
    small[5].wait()

    def spread_targets():
        def body(group, _):
            row = targets_ref[pl.ds(group, 1), :].astype(jnp.float32)
            wanted[group] = jnp.transpose(jnp.broadcast_to(row, (128, 128))).astype(jnp.int32)
            return 0

        lax.fori_loop(0, 2 * PIECES, body, 0)

    gather(where, g, weight, logits, spread_targets, ring_send, ring_recv, pair_send, pair_recv)

    columns = weight.shape[1]
    offset = (where.s * 16 + where.e) * columns
    lane = lax.broadcasted_iota(jnp.int32, (128, 128), 1)

    def chunk(i, _):
        zl, y = lax.div(i, 4), lax.rem(i, 4)
        for core in (0, 1):
            group = i * 2 + core
            part = logits[zl, y, :, :, core * 8 : (core + 1) * 8]
            kept[group] = part
            part = part.reshape(128, columns)
            tiles = [part[:, i : i + 128] for i in range(0, columns, 128)]
            top = functools.reduce(jnp.maximum, tiles)
            total = sum(jnp.exp(tile - top) for tile in tiles)
            picked = sum(
                jnp.where(wanted[group] == lane + (offset + i * 128), tile, 0.0) for i, tile in enumerate(tiles)
            )
            top = jnp.transpose(top)
            highest = jnp.max(top, axis=0, keepdims=True)
            total = jnp.sum(jnp.transpose(total) * jnp.exp(top - highest), axis=0, keepdims=True)
            picked = jnp.sum(jnp.transpose(picked), axis=0, keepdims=True)
            stats[group] = rows8(highest, total, picked)
        return 0

    lax.fori_loop(0, PIECES, chunk, 0)

    to_expert = lambda other: (where.s, other)
    to_section = lambda other: (other, where.e)
    by_group[where.s] = stats[where.s]

    def round_logits():
        def body(group, _):
            heads[pl.ds(group * 128, 128), :] = kept[group].reshape(128, columns).astype(jnp.bfloat16)
            return 0

        lax.fori_loop(0, 2 * PIECES, body, 0)

    exchange(16, where.s, to_section, lambda other: stats.at[other], by_group, one_send, one_recv, round_logits)
    merged[...] = rows8(*merge(by_group[...]))
    by_section[where.e] = merged[...]
    exchange(16, where.e, to_expert, lambda other: merged, by_section, two_send, two_recv)
    top, total, picked = merge(by_section[...])
    log_norm = top + jnp.log(total)
    solved[...] = rows8(log_norm, log_norm - picked, jnp.zeros_like(picked))
    norms_ref[where.s] = solved[...]
    exchange(16, where.s, to_section, lambda other: solved, norms_ref, three_send, three_recv)


def layer(hidden, routes, gates, gain, final_gain, targets, weight_in, weight_out, weight):
    features, columns = weight.shape
    tokens = targets.size
    inner = weight_in.shape[2]
    dma = pltpu.SemaphoreType.DMA
    bf16, f32 = jnp.bfloat16, jnp.float32
    vmem = pl.BlockSpec(memory_space=pltpu.VMEM)
    operands = (hidden, routes, gates, gain, final_gain, targets, weight_in, weight_out, weight)
    return pl.pallas_call(
        layer_kernel,
        name="layer",
        out_shape=(
            pltpu.VMEM((16, 4, 4, 8, columns), f32),
            pltpu.VMEM((tokens, columns), bf16),
            pltpu.VMEM((16, 8, 128), f32),
        ),
        in_specs=[pl.BlockSpec(memory_space=pltpu.HBM)] * 9,
        out_specs=(vmem, vmem, vmem),
        scratch_shapes=[
            pltpu.VMEM((2, 2, 4, 4, 4, 16, HALF), bf16),
            pltpu.VMEM((features, columns), bf16),
            pltpu.VMEM((2, 4, 4, 4, 16, columns), f32),
            pltpu.VMEM((16, 128, 128), jnp.int32),
            pltpu.VMEM((16, 8, 128), f32),
            pltpu.VMEM((16, 8, 128), f32),
            pltpu.VMEM((16, 8, 128), f32),
            pltpu.VMEM((8, 128), f32),
            pltpu.VMEM((8, 128), f32),
            dma,
            dma((57,)), dma((57,)), dma((38,)), dma((38,)),
            dma((16,)), dma((16,)), dma((16,)), dma((16,)), dma((16,)), dma((16,)),
            pltpu.VMEM((features, inner), bf16),
            pltpu.VMEM((inner, features), bf16),
            dma((2,)),
            pltpu.VMEM(hidden.shape, bf16),
            pltpu.VMEM(routes.shape, jnp.int32),
            pltpu.VMEM(gates.shape, f32),
            pltpu.VMEM(gain.shape, f32),
            pltpu.VMEM(final_gain.shape, f32),
            pltpu.VMEM(targets.shape, jnp.int32),
            dma((6,)),
            pltpu.VMEM((2, 8, features), f32),
            pltpu.VMEM((8, features + 128), f32),
            pltpu.VMEM((2, 8, features + 128), f32),
            pltpu.VMEM((16, 16, 256), bf16),
            pltpu.VMEM((16, 16, 256), bf16),
            pltpu.VMEM((2, 4, 2, 64, HALF), bf16),
            pltpu.VMEM((4, 128, inner), bf16),
            pltpu.VMEM((4, 128, HALF), bf16),
            pltpu.VMEM((4, 128, HALF), bf16),
            pltpu.VMEM((8, 64, HALF), bf16),
            pltpu.VMEM((8, 64, HALF), bf16),
            pltpu.VMEM((16, 16, 256), bf16),
            pltpu.VMEM((16, 16, 256), bf16),
            pltpu.VMEM((2, 16, 128), f32),
            dma, dma, dma((16,)), dma((16,)), dma((10,)), dma((10,)), dma((7,)), dma((7,)),
            dma((4,)), dma((4,)), dma((8,)), dma((8,)), dma((16,)), dma((16,)), dma, dma,
        ],
        compiler_params=pltpu.CompilerParams(
            collective_id=1, has_side_effects=True, vmem_limit_bytes=48 * 1024 * 1024
        ),
    )(*(pltpu.with_memory_space_constraint(one, pltpu.HBM) for one in operands))


def finish_kernel(logits_ref, heads_ref, norms_ref, lengths_ref, probs_hbm, head_hbm, loss_ref, probs, probs_sem, head_sem):
    position = lax.broadcasted_iota(jnp.int32, (1, TGT), 1)
    groups, columns = logits_ref.shape[0], logits_ref.shape[-1]
    rounded = pltpu.make_async_copy(heads_ref, head_hbm, head_sem)
    rounded.start()

    def copy(group):
        rows = pl.ds(group * TGT, TGT)
        return pltpu.make_async_copy(probs.at[rows], probs_hbm.at[rows], probs_sem.at[group])

    def each(group, _):
        rows = pl.ds(group * TGT, TGT)
        shift = jnp.transpose(jnp.broadcast_to(norms_ref[group, 0:1, :], (TGT, TGT)))
        for tile in range(columns // TGT):
            lanes = slice(tile * TGT, (tile + 1) * TGT)
            values = logits_ref[group, :, :, :, lanes].reshape(TGT, TGT)
            probs[rows, lanes] = (values - shift).astype(jnp.bfloat16)
        copy(group).start()
        loss_ref[pl.ds(group, 1), :] = jnp.where(position < lengths_ref[group], norms_ref[group, 1:2, :], 0.0)
        return 0

    def done(group, _):
        copy(group).wait()
        return 0

    lax.fori_loop(0, groups, each, 0)
    lax.fori_loop(0, groups, done, 0)
    rounded.wait()


def finish(logits, heads, norms, lengths):
    groups = logits.shape[0]
    vmem, hbm = pl.BlockSpec(memory_space=pltpu.VMEM), pl.BlockSpec(memory_space=pl.ANY)
    return pl.pallas_call(
        finish_kernel,
        name="finish",
        out_shape=(
            jax.ShapeDtypeStruct(heads.shape, jnp.bfloat16),
            jax.ShapeDtypeStruct(heads.shape, jnp.bfloat16),
            jax.ShapeDtypeStruct((groups, TGT), jnp.float32),
        ),
        in_specs=[vmem, vmem, vmem, pl.BlockSpec(memory_space=pltpu.SMEM)],
        out_specs=(hbm, hbm, vmem),
        scratch_shapes=[
            pltpu.VMEM(heads.shape, jnp.bfloat16),
            pltpu.SemaphoreType.DMA((groups,)),
            pltpu.SemaphoreType.DMA,
        ],
        compiler_params=pltpu.CompilerParams(vmem_limit_bytes=24 * 1024 * 1024),
    )(
        pltpu.with_memory_space_constraint(logits, pltpu.VMEM),
        pltpu.with_memory_space_constraint(heads, pltpu.VMEM),
        pltpu.with_memory_space_constraint(norms, pltpu.VMEM),
        lengths,
    )


def on_device(
    hidden, routes, gates, targets, target_lengths, moe_gain, fc_in, fc_out, final_gain, head_weight
):
    wanted = targets.reshape(-1, TGT)
    logits, heads, norms = layer(
        hidden, routes.T, gates.T, moe_gain[None], final_gain[None], wanted, fc_in, fc_out, head_weight
    )
    log_probs, head_logits, loss = finish(logits, heads, norms, target_lengths)
    return (log_probs, head_logits, loss.reshape(-1))


def solution(mesh):
    return jax.shard_map(
        on_device,
        mesh=mesh,
        in_specs=(
            P(("section", "expert"), None),
            P(("section", "expert"), None),
            P(("section", "expert"), None),
            P(),
            P(),
            P(),
            P("expert", None, "section"),
            P("expert", "section", None),
            P(),
            P(None, ("section", "expert")),
        ),
        out_specs=(P(None, ("section", "expert")), P(None, ("section", "expert")), P()),
        check_vma=False,
    )
```

```python
import functools
import math

import jax
import jax.numpy as jnp
from jax import lax
from jax.experimental import pallas as pl
from jax.experimental.pallas import tpu as pltpu
from jax.sharding import PartitionSpec as P

TGT = 128
MESH = pl.DeviceIdType.MESH
HALF = 1024
PIECES = 8
QUARTERS = 4


class Place:
    def __init__(self):
        self.s = lax.axis_index("section")
        self.e = lax.axis_index("expert")
        self.core = lax.rem(self.s, 2)
        self.y = lax.rem(lax.div(self.s, 2), 4)
        self.zl = lax.div(self.s, 8)
        self.x = lax.div(self.e, 4)
        self.zh = lax.rem(self.e, 4)
        self.z = self.zh * 2 + self.zl
        self.sibling = (self.s + 1 - 2 * self.core, self.e)

    def at(self, axis):
        return {"x": self.x, "y": self.y, "z": self.z}[axis]

    def beside(self, axis, step):
        x, y, z = self.x, self.y, self.z
        if axis == "x":
            x = lax.rem(x + step + 4, 4)
        elif axis == "y":
            y = lax.rem(y + step + 4, 4)
        else:
            z = lax.rem(z + step + 8, 8)
        return ((lax.rem(z, 2) * 4 + y) * 2 + self.core, x * 4 + lax.div(z, 2))


def remote(src, dst, send, recv, to):
    return pltpu.make_async_remote_copy(
        src_ref=src, dst_ref=dst, send_sem=send, recv_sem=recv, device_id=to, device_id_type=MESH
    )


class Wires:
    def __init__(self, send, recv):
        self.send, self.recv, self.sent = send, recv, []

    def push(self, src, dst, to):
        k = len(self.sent)
        copy = remote(src, dst, self.send.at[k], self.recv.at[k], to)
        copy.start()
        self.sent.append(copy)
        return k

    def pull(self, k, landed, origin):
        remote(landed, landed, self.send.at[k], self.recv.at[k], origin).wait_recv()

    def drain(self):
        for copy in self.sent:
            copy.wait_send()


class Shared:
    def __init__(self, where, wires):
        self.where, self.wires, self.blocks = where, wires, []

    def push(self, block):
        mine = block(self.where.core)
        self.blocks.append((self.wires.push(mine, mine, self.where.sibling), block))

    def pull(self):
        for k, block in self.blocks:
            self.wires.pull(k, block(1 - self.where.core), self.where.sibling)
        self.blocks = []


def straight(where, wires, axis, n, block):
    me = where.at(axis)
    mine = block(where.core, me)
    order = sorted(range(1, n), key=lambda i: -min(i, n - i))
    numbers = [wires.push(mine, mine, where.beside(axis, i)) for i in order]
    yield
    for i, k in zip(order, numbers):
        wires.pull(k, block(where.core, lax.rem(me - i + n, n)), where.beside(axis, -i))


def ring(where, wires, axis, n, block, shared=None):
    me = where.at(axis)
    for step in range(1, n // 2 + 1):
        numbers = []
        for side, sign in ((0, 1), (1, -1)):
            part = side if step == n // 2 else None
            mine = block(where.core, lax.rem(me - sign * (step - 1) + n, n), part)
            numbers.append(wires.push(mine, mine, where.beside(axis, sign)))
        yield
        for side, sign in ((0, 1), (1, -1)):
            part = side if step == n // 2 else None
            pos = lax.rem(me - sign * step + n, n)
            wires.pull(numbers[side], block(where.core, pos, part), where.beside(axis, -sign))
            if shared is not None:
                shared.push(lambda core, pos=pos, part=part: block(core, pos, part))


def together(*chains):
    chains = list(chains)
    while chains:
        chains = [chain for chain in chains if next(chain, chain) is not chain]


def some(part, size):
    return slice(None) if part is None else pl.ds(part * size, size)


def planes(where, wires, block, shared):
    me = where.z
    numbers = []
    mine = block(where.core, me)
    for step in (2, -2, 1, -1):
        numbers.append((wires.push(mine, mine, where.beside("z", step)), step))
    yield
    for k, step in numbers:
        pos = lax.rem(me - step + 8, 8)
        wires.pull(k, block(where.core, pos), where.beside("z", -step))
        shared.push(lambda core, pos=pos: block(core, pos))
    numbers = []
    for side, sign in ((0, 1), (1, -1)):
        pos = lax.rem(me - 2 * sign + 8, 8)
        for step, part in ((2 * sign, side), (sign, None)):
            mine = block(where.core, pos, part)
            numbers.append((wires.push(mine, mine, where.beside("z", step)), step, sign, part))
    yield
    for k, step, sign, part in numbers:
        pos = lax.rem(me - step - 2 * sign + 8, 8)
        wires.pull(k, block(where.core, pos, part), where.beside("z", -step))
        shared.push(lambda core, pos=pos, part=part: block(core, pos, part))


def gather(where, g, weight, logits, meanwhile, ring_send, ring_recv, pair_send, pair_recv):
    wires, shared = Wires(ring_send, ring_recv), Shared(where, Wires(pair_send, pair_recv))
    x, y, zl, zh = where.x, where.y, where.zl, where.zh
    one, two, three, rest = (0, 256), (256, 384), (640, 384), (256, 768)

    def z_last(half):
        def block(core, pos, part=None):
            return g.at[
                core, lax.rem(pos, 2), pl.ds(2 * half, 2), some(part, 2), lax.div(pos, 2), :, pl.ds(*one)
            ]

        shared.push(lambda core: block(core, where.z))
        yield from planes(where, wires, block, shared)

    def x_last(half):
        def block(core, pos, part=None):
            return g.at[core, half, some(part, 2), pos, :, :, pl.ds(*two)]

        yield from straight(where, wires, "y", 4, lambda core, pos: g.at[core, half, pos, x, :, :, pl.ds(*two)])
        shared.push(lambda core: block(core, x))
        yield from ring(where, wires, "x", 4, block, shared)

    def y_last(half):
        def block(core, pos, part=None):
            return g.at[core, half, pos, some(part, 2), :, :, pl.ds(*three)]

        yield from straight(where, wires, "x", 4, lambda core, pos: g.at[core, half, y, pos, :, :, pl.ds(*three)])
        shared.push(lambda core: block(core, y))
        yield from ring(where, wires, "y", 4, block, shared)

    def multiply(core, at, lanes):
        start, width = lanes
        total = logits[at]
        shape = total.shape
        height = math.prod(shape[:-1])
        total = total.reshape(height, shape[-1])
        rows = g[(core, *at, slice(None), pl.ds(start, width))].reshape(height, width)
        columns = weight[pl.ds(pl.multiple_of(core * HALF + start, 128), width), :]
        total = total + jnp.dot(rows, columns, preferred_element_type=jnp.float32)
        logits[at] = total.reshape(shape)

    def over_planes(core, count, step):
        def body(i, _):
            pos = lax.rem(where.z + step(i), 8)
            multiply(core, (lax.rem(pos, 2), slice(None), slice(None), lax.div(pos, 2)), one)
            return 0

        lax.fori_loop(0, count, body, 0)

    def over_slabs(core, count, step):
        def body(i, _):
            multiply(core, (slice(None), slice(None), lax.rem(x + step(i), 4), slice(None)), two)
            multiply(core, (slice(None), lax.rem(y + step(i), 4), slice(None), slice(None)), three)
            return 0

        lax.fori_loop(0, count, body, 0)

    def advance(chains):
        for chain in chains:
            next(chain, None)

    by_x = straight(where, wires, "x", 4, lambda core, pos: g.at[core, zl, y, pos, zh, :, pl.ds(*one)])
    by_y = straight(where, wires, "y", 4, lambda core, pos: g.at[core, zl, pos, :, zh, :, pl.ds(*one)])
    by_z = straight(
        where, wires, "z", 8, lambda core, pos: g.at[core, lax.rem(pos, 2), y, x, lax.div(pos, 2), :, pl.ds(*rest)]
    )
    early, late = [x_last(0), y_last(0)], [x_last(1), y_last(1)]
    advance([by_x, by_z])
    logits[...] = jnp.zeros_like(logits)
    meanwhile()
    advance([by_x, by_y, by_z] + early + late)
    advance([by_y])
    early, late = [z_last(0)] + early, [z_last(1)] + late
    rounds = (
        (1, lambda i: 0, 1, lambda i: 0),
        (4, lambda i: i + 1 + 3 * lax.div(i, 2), 2, lambda i: 2 * i + 1),
        (3, lambda i: i + 3, 1, lambda i: 2),
    )
    for planes_in, plane_step, slabs_in, slab_step in rounds:
        advance(early + late)
        for core in (where.core, 1 - where.core):
            if core is not where.core:
                shared.pull()
            over_planes(core, planes_in, plane_step)
            over_slabs(core, slabs_in, slab_step)
    wires.drain()
    shared.wires.drain()


def spread_rows(where, rows, ring_send, ring_recv, pair_send, pair_recv):
    wires, shared = Wires(ring_send, ring_recv), Shared(where, Wires(pair_send, pair_recv))
    y, zl = where.y, where.zl
    low, high = pl.ds(0, HALF // 2), pl.ds(HALF // 2, HALF // 2)
    facing = ((((1 - zl) * 4 + y) * 2 + where.core), where.e)

    def swap(block):
        mine = block(where.core, zl)
        k = wires.push(mine, mine, facing)
        yield
        wires.pull(k, block(where.core, 1 - zl), facing)

    def z_last():
        block = lambda core, side: rows.at[core, :, side, :, low]
        yield from ring(
            where, wires, "y", 4, lambda core, pos, part: rows.at[core, pos, zl, some(part, 32), low]
        )
        shared.push(lambda core: block(core, zl))
        yield from swap(block)
        shared.push(lambda core: block(core, 1 - zl))

    def y_last():
        block = lambda core, pos, part=None: rows.at[core, pos, some(part, 1), :, high]
        yield from swap(lambda core, side: rows.at[core, y, side, :, high])
        shared.push(lambda core: block(core, y))
        yield from ring(where, wires, "y", 4, block, shared)

    together(z_last(), y_last())
    return wires, shared


def exchange(n, me, to, src, dst, send, recv, meanwhile=None):
    def each(i, _):
        other = lax.rem(me + i, n)
        remote(src(other), dst.at[me], send.at[i], recv.at[i], to(other)).start()
        return 0

    lax.fori_loop(1, n, each, 0)
    if meanwhile is not None:
        meanwhile()

    def done(i, _):
        origin = lax.rem(me - i + n, n)
        copy = remote(src(origin), dst.at[origin], send.at[i], recv.at[i], to(origin))
        copy.wait_recv()
        copy.wait_send()
        return 0

    lax.fori_loop(1, n, done, 0)


def merge(stats):
    high = stats[:, 0:1, :]
    top = jnp.max(high, axis=0)
    total = jnp.sum(stats[:, 1:2, :] * jnp.exp(high - top[None]), axis=0)
    return top, total, jnp.sum(stats[:, 2:3, :], axis=0)


def rows8(first, second, third):
    row = lax.broadcasted_iota(jnp.int32, (8, 128), 0)
    zero = jnp.zeros((8, 128), jnp.float32)
    out = jnp.where(row == 0, first, zero)
    out = jnp.where(row == 1, second, out)
    return jnp.where(row == 2, third, out)


def one_hot(table, tokens):
    shape = (tokens, 256)
    column = lax.broadcasted_iota(jnp.int32, shape, 1)
    token = lax.broadcasted_iota(jnp.int32, shape, 0)
    expert = lax.div(column, 16).astype(jnp.float32)
    slot = lax.rem(lax.div(column, 4), 2).astype(jnp.float32)
    same = lax.rem(lax.div(column, 8), 2) == lax.div(token, 8)
    piece = lax.rem(column, 4)
    hits = [jnp.where(table[:, k : k + 1] == expert, 1.0, 0.0) for k in (0, 1)]
    later = lax.broadcasted_iota(jnp.int32, (tokens, tokens), 0)
    sooner = lax.broadcasted_iota(jnp.int32, (tokens, tokens), 1)
    before = jnp.where((sooner < later) & (lax.div(sooner, 8) == lax.div(later, 8)), 1.0, 0.0)
    earlier = jnp.dot(
        before.astype(jnp.bfloat16), (hits[0] + hits[1]).astype(jnp.bfloat16), preferred_element_type=jnp.float32
    )
    placed = [jnp.where(same & (earlier == slot), hit, 0.0) for hit in hits]
    return [
        jnp.concatenate([jnp.where(piece == j, one, 0.0) for j in range(QUARTERS)], axis=0) for one in placed
    ]


def stack(values):
    return jnp.concatenate([values[:, j * 256 : (j + 1) * 256] for j in range(QUARTERS)], axis=0)


def experts(
    where, barrier, small, late, hidden_ref, routes_ref, gates_ref, gain_ref, final_gain_ref, weight_in, weight_out, loads, g,
    local, outbox, begun, pack, outgoing, incoming, rows, units, away, sent_half, summed, parts, returning, returned, spread,
    pack_send, pack_recv, go_send, go_recv, row_send, row_recv, rowp_send, rowp_recv, half_send, half_recv,
    sum_send, sum_recv, back_send, back_recv, ln_send, ln_recv,
):
    core, m = where.core, where.y * 2 + where.zl
    mine = pl.ds(pl.multiple_of(core * HALF, HALF), HALF)
    theirs = pl.ds(pl.multiple_of((1 - core) * HALF, HALF), HALF)
    to_expert = lambda other: (where.s, other)
    to_chip = lambda other: ((lax.rem(other, 2) * 4 + lax.div(other, 2)) * 2 + core, where.e)
    features = 2 * HALF

    for one in small:
        one.wait()
    lane = lax.broadcasted_iota(jnp.int32, (8, 128), 1)
    same = lax.broadcasted_iota(jnp.int32, (8, 8), 0) == lax.broadcasted_iota(jnp.int32, (8, 8), 1)
    table = jnp.zeros((8, 128), jnp.float32)
    for place, (source, k) in enumerate(((routes_ref, 0), (routes_ref, 1), (gates_ref, 0), (gates_ref, 1))):
        row = source[k : k + 1, :].astype(jnp.float32)
        column = jnp.sum(jnp.where(same, row, 0.0), axis=1, keepdims=True)
        table = jnp.where(lane == place, column, table)
    whole = hidden_ref[...].astype(jnp.float32)
    average = jnp.mean(whole, axis=-1, keepdims=True)
    centered = whole - average
    spread_of = jnp.mean(centered * centered, axis=-1, keepdims=True)
    normed = centered * lax.rsqrt(spread_of + 1e-05) * gain_ref[...]
    local[0] = normed.astype(jnp.bfloat16).astype(jnp.float32)
    local[1] = whole
    for box, half in ((outbox, theirs), (pack.at[core], mine)):
        box[:, 0:HALF] = local[0, :, half]
        box[:, HALF:features] = local[1, :, half]
        box[:, features:] = table
    pl.semaphore_wait(barrier, 32)
    swap = remote(outbox, pack.at[core], pack_send, pack_recv, where.sibling)
    swap.start()
    swap.wait()

    tokens = 16
    normed = pack[:, :, 0:HALF].reshape(tokens, HALF).astype(jnp.bfloat16)
    residual = pack[:, :, HALF:features].reshape(tokens, HALF)
    table = pack[:, :, features:].reshape(tokens, 128)
    chosen = one_hot(table, tokens)
    place = jnp.transpose(chosen[0] + chosen[1]).astype(jnp.bfloat16)
    slots = jnp.dot(place, stack(normed), preferred_element_type=jnp.float32).astype(jnp.bfloat16)
    outgoing[...] = slots.reshape(16, 16, 256)
    incoming[where.e] = outgoing[where.e]
    exchange(16, where.e, to_expert, lambda other: outgoing.at[other], incoming, go_send, go_recv)

    down = lax.broadcasted_iota(jnp.int32, (256, 256), 0)
    across = lax.broadcasted_iota(jnp.int32, (256, 256), 1)
    split = jnp.where(across == 4 * lax.rem(down, 64) + lax.div(down, 64), 1.0, 0.0).astype(jnp.bfloat16)
    join = jnp.where(down == 4 * lax.rem(across, 64) + lax.div(across, 64), 1.0, 0.0).astype(jnp.bfloat16)
    arrived = jnp.dot(split, incoming[...].reshape(256, 256), preferred_element_type=jnp.float32)
    for j in range(QUARTERS):
        rows[core, where.y, where.zl, :, j * 256 : (j + 1) * 256] = arrived[j * 64 : (j + 1) * 64].astype(jnp.bfloat16)

    wires, shared = spread_rows(where, rows, row_send, row_recv, rowp_send, rowp_recv)
    loads[0].wait()
    loads[1].wait()

    def first(half_of, i):
        some_rows = rows[half_of, pl.ds(i * 2, 2)].reshape(256, HALF)
        some_weights = weight_in[pl.ds(pl.multiple_of(half_of * HALF, HALF), HALF), :]
        return jnp.dot(some_rows, some_weights, preferred_element_type=jnp.float32)

    def first_own(i, _):
        begun[i] = first(core, i)
        return 0

    def first_other(i, _):
        found = begun[i] + first(1 - core, i)
        units[pl.ds(i * 2, 2)] = jnp.maximum(found, 0.0).astype(jnp.bfloat16).reshape(2, 128, -1)
        return 0

    lax.fori_loop(0, 2, first_own, 0)
    shared.pull()
    lax.fori_loop(0, 2, first_other, 0)

    def half(i, other):
        return remote(away.at[other], sent_half.at[other], half_send.at[i], half_recv.at[i], where.sibling)

    def second(i, _):
        other = lax.rem(where.y + 1 + i, 4)
        found = jnp.dot(units[other], weight_out[:, theirs], preferred_element_type=jnp.float32)
        away[other] = found.astype(jnp.bfloat16)
        half(i, other).start()
        return 0

    lax.fori_loop(0, 4, second, 0)

    def part(block, origin):
        return remote(summed.at[block], parts.at[origin], sum_send.at[block], sum_recv.at[origin], to_chip(block))

    def add(i, _):
        other = lax.rem(where.y + 1 + i, 4)
        near = jnp.dot(units[other], weight_out[:, mine], preferred_element_type=jnp.float32)
        half(i, other).wait_recv()
        total = (near + sent_half[other].astype(jnp.float32)).astype(jnp.bfloat16)
        summed[pl.ds(other * 2, 2)] = total.reshape(2, 64, HALF)
        for side in (0, 1):
            block = other * 2 + side

            @pl.when(block != m)
            def _():
                part(block, m).start()

        return 0

    lax.fori_loop(0, 4, add, 0)
    parts[m] = summed[m]

    def take_part(i, _):
        origin = lax.rem(m - i + 8, 8)
        remote(summed.at[origin], parts.at[origin], sum_send.at[origin], sum_recv.at[origin], to_chip(origin)).wait_recv()
        return 0

    lax.fori_loop(1, 8, take_part, 0)
    total = parts[0].astype(jnp.float32)
    for i in range(1, 8):
        total = total + parts[i].astype(jnp.float32)
    results = jnp.dot(join, stack(total.astype(jnp.bfloat16)), preferred_element_type=jnp.float32)
    returning[...] = results.astype(jnp.bfloat16).reshape(16, 16, 256)
    returned[where.e] = returning[where.e]
    exchange(16, where.e, to_expert, lambda other: returning.at[other], returned, back_send, back_recv)

    back = returned[...].reshape(256, 256)
    mixed = [residual[:, j * 256 : (j + 1) * 256] for j in range(QUARTERS)]
    for k in (0, 1):
        found = jnp.dot(chosen[k].astype(jnp.bfloat16), back, preferred_element_type=jnp.float32)
        gate = table[:, 2 + k : 3 + k]
        mixed = [old + gate * found[j * tokens : (j + 1) * tokens] for j, old in enumerate(mixed)]
    mixed = jnp.concatenate(mixed, axis=1)
    center = jnp.mean(mixed, axis=-1, keepdims=True)
    squares = jnp.sum((mixed - center) * (mixed - center), axis=-1, keepdims=True)
    lane = lax.broadcasted_iota(jnp.int32, (tokens, 128), 1)
    spread[core] = jnp.where(lane == 0, center, jnp.where(lane == 1, squares, 0.0))
    swap = remote(spread.at[core], spread.at[core], ln_send, ln_recv, where.sibling)
    swap.start()
    swap.wait()
    centers = [spread[i, :, 0:1] for i in (0, 1)]
    average = 0.5 * (centers[0] + centers[1])
    apart = centers[0] - centers[1]
    variance = (spread[0, :, 1:2] + spread[1, :, 1:2] + apart * apart * (0.5 * HALF)) / features
    late.wait()
    final = (mixed - average) * lax.rsqrt(variance + 1e-05) * final_gain_ref[:, mine]
    g[core, where.zl, where.y, where.x, where.zh] = final.astype(jnp.bfloat16)

    wires.drain()
    shared.wires.drain()

    def halves_left(i, _):
        half(i, lax.rem(where.y + 1 + i, 4)).wait_send()
        return 0

    lax.fori_loop(0, 4, halves_left, 0)

    def parts_left(i, _):
        part(lax.rem(m + i, 8), m).wait_send()
        return 0

    lax.fori_loop(1, 8, parts_left, 0)


def layer_kernel(
    hidden_hbm, routes_hbm, gates_hbm, gain_hbm, final_gain_hbm, targets_hbm, in_hbm, out_hbm, weight_hbm,
    kept, heads, norms_ref,
    g, weight, logits, wanted, stats, by_group, by_section, merged, solved,
    weight_sem, ring_send, ring_recv, pair_send, pair_recv,
    one_send, one_recv, two_send, two_recv, three_send, three_recv,
    weight_in, weight_out, weight_sems, hidden_ref, routes_ref, gates_ref, gain_ref, final_gain_ref, targets_ref,
    small_sems, *scratch,
):
    where = Place()
    barrier = pltpu.get_barrier_semaphore()
    pairs = (
        (hidden_hbm, hidden_ref), (routes_hbm, routes_ref), (gates_hbm, gates_ref), (gain_hbm, gain_ref),
        (final_gain_hbm, final_gain_ref), (targets_hbm, targets_ref),
    )
    small = [pltpu.make_async_copy(a, b, small_sems.at[i]) for i, (a, b) in enumerate(pairs)]
    for one in small:
        one.start()
    load = pltpu.make_async_copy(weight_hbm, weight, weight_sem)
    loads = [
        pltpu.make_async_copy(in_hbm.at[0], weight_in, weight_sems.at[0]),
        pltpu.make_async_copy(out_hbm.at[0], weight_out, weight_sems.at[1]),
    ]
    for one in loads:
        one.start()
    load.start()

    def greet(i, _):
        pl.semaphore_signal(
            barrier, inc=1, device_id=(lax.rem(where.s + i, 16), where.e), device_id_type=MESH
        )
        pl.semaphore_signal(
            barrier, inc=1, device_id=(where.s, lax.rem(where.e + i, 16)), device_id_type=MESH
        )
        return 0

    lax.fori_loop(1, 16, greet, 0)
    for step in (1, -1):
        pl.semaphore_signal(barrier, inc=1, device_id=where.beside("z", step), device_id_type=MESH)

    experts(
        where, barrier, small[:4], small[4], hidden_ref, routes_ref, gates_ref, gain_ref, final_gain_ref, weight_in, weight_out,
        loads, g, *scratch
    )
    load.wait()
    small[5].wait()

    def spread_targets():
        def body(group, _):
            row = targets_ref[pl.ds(group, 1), :].astype(jnp.float32)
            wanted[group] = jnp.transpose(jnp.broadcast_to(row, (128, 128))).astype(jnp.int32)
            return 0

        lax.fori_loop(0, 2 * PIECES, body, 0)

    gather(where, g, weight, logits, spread_targets, ring_send, ring_recv, pair_send, pair_recv)

    columns = weight.shape[1]
    offset = (where.s * 16 + where.e) * columns
    lane = lax.broadcasted_iota(jnp.int32, (128, 128), 1)

    def chunk(i, _):
        zl, y = lax.div(i, 4), lax.rem(i, 4)
        for core in (0, 1):
            group = i * 2 + core
            part = logits[zl, y, :, :, core * 8 : (core + 1) * 8]
            kept[group] = part
            part = part.reshape(128, columns)
            tiles = [part[:, i : i + 128] for i in range(0, columns, 128)]
            top = functools.reduce(jnp.maximum, tiles)
            total = sum(jnp.exp(tile - top) for tile in tiles)
            picked = sum(
                jnp.where(wanted[group] == lane + (offset + i * 128), tile, 0.0) for i, tile in enumerate(tiles)
            )
            top = jnp.transpose(top)
            highest = jnp.max(top, axis=0, keepdims=True)
            total = jnp.sum(jnp.transpose(total) * jnp.exp(top - highest), axis=0, keepdims=True)
            picked = jnp.sum(jnp.transpose(picked), axis=0, keepdims=True)
            stats[group] = rows8(highest, total, picked)
        return 0

    lax.fori_loop(0, PIECES, chunk, 0)

    to_expert = lambda other: (where.s, other)
    to_section = lambda other: (other, where.e)
    by_group[where.s] = stats[where.s]

    def round_logits():
        def body(group, _):
            heads[pl.ds(group * 128, 128), :] = kept[group].reshape(128, columns).astype(jnp.bfloat16)
            return 0

        lax.fori_loop(0, 2 * PIECES, body, 0)

    exchange(16, where.s, to_section, lambda other: stats.at[other], by_group, one_send, one_recv, round_logits)
    merged[...] = rows8(*merge(by_group[...]))
    by_section[where.e] = merged[...]
    exchange(16, where.e, to_expert, lambda other: merged, by_section, two_send, two_recv)
    top, total, picked = merge(by_section[...])
    log_norm = top + jnp.log(total)
    solved[...] = rows8(log_norm, log_norm - picked, jnp.zeros_like(picked))
    norms_ref[where.s] = solved[...]
    exchange(16, where.s, to_section, lambda other: solved, norms_ref, three_send, three_recv)


def layer(hidden, routes, gates, gain, final_gain, targets, weight_in, weight_out, weight):
    features, columns = weight.shape
    tokens = targets.size
    inner = weight_in.shape[2]
    dma = pltpu.SemaphoreType.DMA
    bf16, f32 = jnp.bfloat16, jnp.float32
    vmem = pl.BlockSpec(memory_space=pltpu.VMEM)
    operands = (hidden, routes, gates, gain, final_gain, targets, weight_in, weight_out, weight)
    return pl.pallas_call(
        layer_kernel,
        name="layer",
        out_shape=(
            pltpu.VMEM((16, 4, 4, 8, columns), f32),
            pltpu.VMEM((tokens, columns), bf16),
            pltpu.VMEM((16, 8, 128), f32),
        ),
        in_specs=[pl.BlockSpec(memory_space=pltpu.HBM)] * 9,
        out_specs=(vmem, vmem, vmem),
        scratch_shapes=[
            pltpu.VMEM((2, 2, 4, 4, 4, 16, HALF), bf16),
            pltpu.VMEM((features, columns), bf16),
            pltpu.VMEM((2, 4, 4, 4, 16, columns), f32),
            pltpu.VMEM((16, 128, 128), jnp.int32),
            pltpu.VMEM((16, 8, 128), f32),
            pltpu.VMEM((16, 8, 128), f32),
            pltpu.VMEM((16, 8, 128), f32),
            pltpu.VMEM((8, 128), f32),
            pltpu.VMEM((8, 128), f32),
            dma,
            dma((57,)), dma((57,)), dma((38,)), dma((38,)),
            dma((16,)), dma((16,)), dma((16,)), dma((16,)), dma((16,)), dma((16,)),
            pltpu.VMEM((features, inner), bf16),
            pltpu.VMEM((inner, features), bf16),
            dma((2,)),
            pltpu.VMEM(hidden.shape, bf16),
            pltpu.VMEM(routes.shape, jnp.int32),
            pltpu.VMEM(gates.shape, f32),
            pltpu.VMEM(gain.shape, f32),
            pltpu.VMEM(final_gain.shape, f32),
            pltpu.VMEM(targets.shape, jnp.int32),
            dma((6,)),
            pltpu.VMEM((2, 8, features), f32),
            pltpu.VMEM((8, features + 128), f32),
            pltpu.VMEM((2, 256, inner), f32),
            pltpu.VMEM((2, 8, features + 128), f32),
            pltpu.VMEM((16, 16, 256), bf16),
            pltpu.VMEM((16, 16, 256), bf16),
            pltpu.VMEM((2, 4, 2, 64, HALF), bf16),
            pltpu.VMEM((4, 128, inner), bf16),
            pltpu.VMEM((4, 128, HALF), bf16),
            pltpu.VMEM((4, 128, HALF), bf16),
            pltpu.VMEM((8, 64, HALF), bf16),
            pltpu.VMEM((8, 64, HALF), bf16),
            pltpu.VMEM((16, 16, 256), bf16),
            pltpu.VMEM((16, 16, 256), bf16),
            pltpu.VMEM((2, 16, 128), f32),
            dma, dma, dma((16,)), dma((16,)), dma((10,)), dma((10,)), dma((7,)), dma((7,)),
            dma((4,)), dma((4,)), dma((8,)), dma((8,)), dma((16,)), dma((16,)), dma, dma,
        ],
        compiler_params=pltpu.CompilerParams(
            collective_id=1, has_side_effects=True, vmem_limit_bytes=48 * 1024 * 1024
        ),
    )(*(pltpu.with_memory_space_constraint(one, pltpu.HBM) for one in operands))


def finish_kernel(logits_ref, heads_ref, norms_ref, lengths_ref, probs_hbm, head_hbm, loss_ref, probs, probs_sem, head_sem):
    position = lax.broadcasted_iota(jnp.int32, (1, TGT), 1)
    groups, columns = logits_ref.shape[0], logits_ref.shape[-1]
    rounded = pltpu.make_async_copy(heads_ref, head_hbm, head_sem)
    rounded.start()

    def copy(group):
        rows = pl.ds(group * TGT, TGT)
        return pltpu.make_async_copy(probs.at[rows], probs_hbm.at[rows], probs_sem.at[group])

    def each(group, _):
        rows = pl.ds(group * TGT, TGT)
        shift = jnp.transpose(jnp.broadcast_to(norms_ref[group, 0:1, :], (TGT, TGT)))
        for tile in range(columns // TGT):
            lanes = slice(tile * TGT, (tile + 1) * TGT)
            values = logits_ref[group, :, :, :, lanes].reshape(TGT, TGT)
            probs[rows, lanes] = (values - shift).astype(jnp.bfloat16)
        copy(group).start()
        loss_ref[pl.ds(group, 1), :] = jnp.where(position < lengths_ref[group], norms_ref[group, 1:2, :], 0.0)
        return 0

    def done(group, _):
        copy(group).wait()
        return 0

    lax.fori_loop(0, groups, each, 0)
    lax.fori_loop(0, groups, done, 0)
    rounded.wait()


def finish(logits, heads, norms, lengths):
    groups = logits.shape[0]
    vmem, hbm = pl.BlockSpec(memory_space=pltpu.VMEM), pl.BlockSpec(memory_space=pl.ANY)
    return pl.pallas_call(
        finish_kernel,
        name="finish",
        out_shape=(
            jax.ShapeDtypeStruct(heads.shape, jnp.bfloat16),
            jax.ShapeDtypeStruct(heads.shape, jnp.bfloat16),
            jax.ShapeDtypeStruct((groups, TGT), jnp.float32),
        ),
        in_specs=[vmem, vmem, vmem, pl.BlockSpec(memory_space=pltpu.SMEM)],
        out_specs=(hbm, hbm, vmem),
        scratch_shapes=[
            pltpu.VMEM(heads.shape, jnp.bfloat16),
            pltpu.SemaphoreType.DMA((groups,)),
            pltpu.SemaphoreType.DMA,
        ],
        compiler_params=pltpu.CompilerParams(vmem_limit_bytes=24 * 1024 * 1024),
    )(
        pltpu.with_memory_space_constraint(logits, pltpu.VMEM),
        pltpu.with_memory_space_constraint(heads, pltpu.VMEM),
        pltpu.with_memory_space_constraint(norms, pltpu.VMEM),
        lengths,
    )


def on_device(
    hidden, routes, gates, targets, target_lengths, moe_gain, fc_in, fc_out, final_gain, head_weight
):
    wanted = targets.reshape(-1, TGT)
    logits, heads, norms = layer(
        hidden, routes.T, gates.T, moe_gain[None], final_gain[None], wanted, fc_in, fc_out, head_weight
    )
    log_probs, head_logits, loss = finish(logits, heads, norms, target_lengths)
    return (log_probs, head_logits, loss.reshape(-1))


def solution(mesh):
    return jax.shard_map(
        on_device,
        mesh=mesh,
        in_specs=(
            P(("section", "expert"), None),
            P(("section", "expert"), None),
            P(("section", "expert"), None),
            P(),
            P(),
            P(),
            P("expert", None, "section"),
            P("expert", "section", None),
            P(),
            P(None, ("section", "expert")),
        ),
        out_specs=(P(None, ("section", "expert")), P(None, ("section", "expert")), P()),
        check_vma=False,
    )
```
